512 devices in a mesh: row: 16 (over z, y_lo), col: 32 (over y_hi, x, core).
Axes of the slice: x: 4, y: 8 (y_hi: 4, y_lo: 2; y = y_hi * 2 + y_lo), z: 8, core: 2. Of those that a mesh axis runs over, the one named last changes fastest.
Arguments:
- pair: bfloat16 [768, 768, 128], P('row', 'col'), may hold values from -100 to 100
- ln_gain: float32 [128], replicated, may hold values from 0.1 to 1.9
- w_query: bfloat16 [128, 128], replicated, may hold values from -0.5 to 0.5
- w_keyval: bfloat16 [128, 256], replicated, may hold values from -0.5 to 0.5
- w_gate: bfloat16 [128, 128], replicated, may hold values from -0.5 to 0.5
- w_bias: bfloat16 [128, 4], replicated, may hold values from -16 to 16
- w_out: bfloat16 [128, 128], replicated, may hold values from -0.5 to 0.5
Outputs:
- update: bfloat16 [128, 768, 128], P('row', 'col')
The draws below stay inside these ranges and needn't reach their ends.
All inputs are finite; a program needn't handle non-finite values.
Results may differ from the reference program's by a relative error of at most 0.0025.
The reference program's roundings to bfloat16 on the way (of `normed`, `query`, `keys` and `gated`) count: a program that leaves them out, or rounds other values in their place, can miss the bound.
Values may be sent and summed in bfloat16 or wider, within the bound.
No kernel may reach another device: no remote copies, remote signals or barrier semaphores. Data moves between devices by JAX's collectives and lax.ppermute only.
A program may use at most 64 MiB of HBM per device.

```python
import math
import jax
import jax.numpy as jnp
from jax import lax

C = 128
H = 4
HD = 32
QROWS = 8
N_RES = 768
ROW_BLK = 48
ROWS_Q = 128
N_ROW = 16


def draw_pair(key, part):
    key = jax.random.fold_in(key, 1)
    keys = jax.random.split(key, 3)
    cell_scale = jnp.exp(jax.random.uniform(keys[0], (N_RES, N_RES, 1), jnp.float32, 0.0, math.log(10.0)))
    chan_scale = jnp.exp(jax.random.uniform(keys[1], (C,), jnp.float32, math.log(0.5), math.log(2.0)))
    field = jnp.clip(jax.random.normal(keys[2], (N_RES, N_RES, C), jnp.float32), -4.0, 4.0) * chan_scale
    return (field * cell_scale).astype(jnp.bfloat16)


def draw_w_bias(key, part):
    key = jax.random.fold_in(key, 2)
    noise = jnp.clip(jax.random.normal(key, (C, H), jnp.float32), -4.0, 4.0) / math.sqrt(C)
    return noise.astype(jnp.bfloat16)


def normal_values(own_key, extent, scale, bound, kind=jnp.bfloat16):
    return jnp.clip(scale * jax.random.normal(own_key, extent, jnp.float32), -bound, bound).astype(kind)


def setup_inputs(seed: int = 0) -> dict:
    key_of = jax.random.split(jax.random.key(seed), 8)
    return {
        "pair": draw_pair(jax.random.fold_in(key_of[7], 71), 0),
        "ln_gain": jnp.clip(1.0 + 0.18 * jax.random.normal(key_of[1], (C,), jnp.float32), 0.1, 1.9),
        "w_query": normal_values(key_of[2], (C, H * HD), C ** -0.5, 0.5),
        "w_keyval": normal_values(key_of[3], (C, 2 * H * HD), C ** -0.5, 0.5),
        "w_gate": normal_values(key_of[4], (C, H * HD), C ** -0.5, 0.5),
        "w_bias": draw_w_bias(jax.random.fold_in(key_of[7], 71), 0),
        "w_out": normal_values(key_of[6], (H * HD, C), (H * HD) ** -0.5, 0.5),
    }


def layer_norm(block, gain):
    values = block.astype(jnp.float32)
    mean = lax.optimization_barrier(jnp.mean(values, axis=-1, keepdims=True))
    centred = values - mean
    variance = lax.optimization_barrier(jnp.mean(centred * centred, axis=-1, keepdims=True))
    return (centred * lax.rsqrt(variance + 1e-05) * gain).astype(jnp.bfloat16)

def reference(pair, ln_gain, w_query, w_keyval, w_gate, w_bias, w_out):
    blocks = pair.reshape(N_ROW, ROW_BLK, N_RES, C)

    def bias_block(block):
        normed = layer_norm(block, ln_gain)
        return jnp.dot(normed.reshape(-1, C), w_bias, preferred_element_type=jnp.float32).reshape(ROW_BLK, N_RES, H)
    bias = lax.map(bias_block, blocks).reshape(N_RES, N_RES, H)
    bias = jnp.transpose(bias, (2, 0, 1))
    query_rows = blocks[:, :QROWS].reshape(ROWS_Q, N_RES, C)
    scale = 1.0 / HD ** 0.5

    def one_row(row):
        normed = layer_norm(row, ln_gain)
        query = (jnp.dot(normed, w_query, preferred_element_type=jnp.float32) * scale).astype(jnp.bfloat16)
        keyval = jnp.dot(normed, w_keyval, preferred_element_type=jnp.float32).astype(jnp.bfloat16)
        gate = jax.nn.sigmoid(jnp.dot(normed, w_gate, preferred_element_type=jnp.float32))
        query = query.astype(jnp.float32).reshape(N_RES, H, HD)
        keys = keyval[:, :H * HD].astype(jnp.float32).reshape(N_RES, H, HD)
        values = keyval[:, H * HD:].astype(jnp.float32).reshape(N_RES, H, HD)
        score = jnp.einsum('jhd,khd->hjk', query, keys, precision=lax.Precision.HIGHEST) + bias
        top = lax.optimization_barrier(jnp.max(score, axis=-1, keepdims=True))
        weights = jnp.exp(score - top)
        total = lax.optimization_barrier(jnp.sum(weights, axis=-1))
        attended = jnp.einsum('hjk,khd->hjd', weights, values, precision=lax.Precision.HIGHEST) / total[..., None]
        attended = jnp.transpose(attended, (1, 0, 2)).reshape(N_RES, H * HD)
        gated = (gate * attended).astype(jnp.bfloat16)
        return jnp.dot(gated, w_out, preferred_element_type=jnp.float32).astype(jnp.bfloat16)
    return lax.map(one_row, query_rows)
```

```python
import jax
import jax.numpy as jnp
from jax import lax
from jax.experimental import pallas as pl
from jax.experimental.pallas import tpu as pltpu
from jax.sharding import PartitionSpec as P

QROWS = 8
KB = 24
HEADS = 4
LANES = 128
NROW = 16
NCOL = 32
F32 = jnp.float32
BF16 = jnp.bfloat16
VM = pltpu.VMEM


def whole(space=VM):
    return pl.BlockSpec(memory_space=space)


def norm_rows(block, gain):
    values = block.astype(F32)
    mean = jnp.mean(values, axis=-1, keepdims=True)
    centred = values - mean
    variance = jnp.mean(centred * centred, axis=-1, keepdims=True)
    return (centred * lax.rsqrt(variance + 1e-05) * gain).astype(BF16)


def query_norm_kernel(rows_ref, gain_ref, out_ref):
    out_ref[...] = norm_rows(rows_ref[...], gain_ref[...])


def bias_kernel(rows_ref, gain_ref, wb_ref, same_ref, other_ref):
    core = lax.rem(lax.axis_index("col"), 2)
    lane = lax.broadcasted_iota(jnp.int32, (LANES, LANES), 1)
    wb = wb_ref[...].astype(F32)
    spread = jnp.zeros((LANES, LANES), F32)
    for h in range(HEADS):
        inside = (lane >= h * KB) & (lane < (h + 1) * KB)
        spread = jnp.where(inside, wb[:, h : h + 1], spread)
    spread = spread.astype(BF16)
    lane = lax.broadcasted_iota(jnp.int32, (KB, LANES), 1)
    place = jnp.where(lane < HEADS * KB, lax.rem(lane, KB), -1)
    halves = []
    for half in range(2):
        first = half * KB * KB
        normed = norm_rows(rows_ref[first : first + KB * KB, :], gain_ref[...])
        wide = jnp.dot(normed, spread, preferred_element_type=F32)
        total = jnp.zeros((KB, LANES), F32)
        for j in range(KB):
            total = jnp.where(place == j, wide[j * KB : (j + 1) * KB, :], total)
        halves.append(total)
    same_ref[...] = jnp.where(core == 0, halves[0], halves[1])
    other_ref[...] = jnp.where(core == 0, halves[1], halves[0])


def attend_kernel(*refs):
    pieces = refs[0:8]
    biases = refs[8:16]
    nq_ref, wq_ref, wk_ref, wvt_ref, wg_ref, wo_ref = refs[16:22]
    out_ref = refs[22]
    bias_ref, x_ref, s_ref, q_ref, gate_ref, gated_ref = refs[23:29]
    row = lax.axis_index("row")
    col = lax.axis_index("col")
    core = lax.rem(col, 2)
    x = lax.rem(col // 2, 4)
    y_hi = col // 8
    z = row // 2
    y_lo = lax.rem(row, 2)
    for s in range(8):
        for t in range(2):
            source = lax.rem(z - s + 8, 8) * 2 + lax.rem(y_lo + t, 2)
            for e in range(2):
                block = source * 2 + lax.rem(core + e, 2)
                start = pl.multiple_of(block * KB, 8)
                bias_ref[pl.ds(start, KB), :] = biases[s][
                    (t * 2 + e) * KB : (t * 2 + e + 1) * KB, :
                ]
    nq = nq_ref[...]
    scale = 1.0 / 32**0.5
    q_ref[...] = jnp.dot(nq, wq_ref[...], preferred_element_type=F32) * scale
    gate_ref[...] = jax.nn.sigmoid(jnp.dot(nq, wg_ref[...], preferred_element_type=F32))
    lane = lax.broadcasted_iota(jnp.int32, (KB, LANES), 1)
    starts = []
    for p in range(8):
        for sy in range(4):
            block = (
                lax.rem(y_hi - sy + 4, 4) * 8
                + lax.rem(x - p % 4 + 4, 4) * 2
                + lax.rem(core + p // 4, 2)
            )
            starts.append(pl.multiple_of(block * KB, 8))

    def one_row(a, carry):
        qrows = pl.ds(pl.multiple_of(a * KB, 8), KB)
        q = q_ref[qrows, :].astype(BF16).astype(F32)
        masked = [jnp.where(lane // 32 == h, q, 0.0) for h in range(HEADS)]
        masked.append(jnp.zeros((LANES - HEADS * KB, LANES), F32))
        masked = jnp.concatenate(masked, axis=0).astype(BF16)
        for p in range(8):
            x_ref[p * 96 : (p + 1) * 96, :] = pieces[p][
                pl.ds(pl.multiple_of(a * 96, 32), 96), :
            ]
        rows = x_ref[...]
        keys = jnp.dot(rows, wk_ref[...], preferred_element_type=F32).astype(BF16)
        values_t = lax.dot_general(
            wvt_ref[...], rows, (((1,), (1,)), ((), ())), preferred_element_type=F32
        ).astype(BF16)
        score = lax.dot_general(
            keys, masked, (((1,), (1,)), ((), ())), preferred_element_type=F32
        )
        top = jnp.full((KB, LANES), -jnp.inf, F32)
        for i in range(32):
            part = score[i * KB : (i + 1) * KB, :] + bias_ref[pl.ds(starts[i], KB), :]
            s_ref[i * KB : (i + 1) * KB, :] = part
            top = jnp.maximum(top, part)
        top = jnp.max(top, axis=0, keepdims=True)
        weights = jnp.exp(s_ref[...] - top)
        total = jnp.sum(weights, axis=0, keepdims=True)
        high = weights.astype(BF16)
        low = (weights - high.astype(F32)).astype(BF16)
        attended = jnp.dot(values_t, high, preferred_element_type=F32) + jnp.dot(
            values_t, low, preferred_element_type=F32
        )
        attended = (attended / total).T
        mine = jnp.zeros((KB, LANES), F32)
        for h in range(HEADS):
            mine = jnp.where(lane // 32 == h, attended[h * KB : (h + 1) * KB, :], mine)
        gated_ref[qrows, :] = gate_ref[qrows, :] * mine
        return carry

    lax.fori_loop(0, QROWS, one_row, 0)
    out_ref[...] = jnp.dot(
        gated_ref[...].astype(BF16), wo_ref[...], preferred_element_type=F32
    ).astype(BF16)


def permute_col(value, target):
    return lax.ppermute(value, "col", [(c, target(c)) for c in range(NCOL)])


def permute_row(value, target):
    return lax.ppermute(value, "row", [(r, target(r)) for r in range(NROW)])


def permute_all(value, target):
    pairs = []
    for r in range(NROW):
        for c in range(NCOL):
            r2, c2 = target(r, c)
            pairs.append((r * NCOL + c, r2 * NCOL + c2))
    return lax.ppermute(value, ("row", "col"), pairs)


def shift_y(s):
    return lambda c: (c + 8 * s) % NCOL


def shift_x(s):
    return lambda c: c // 8 * 8 + (c % 8 + 2 * s) % 8


def shift_z(s):
    return lambda r: (r + 2 * s) % NROW


def body(pair, ln_gain, w_query, w_keyval, w_gate, w_bias, w_out):
    rows = pair.reshape(-1, LANES)
    gain = ln_gain.reshape(1, LANES)
    nrows = QROWS * KB
    nq = pl.pallas_call(
        query_norm_kernel,
        grid=(1,),
        in_specs=[
            pl.BlockSpec((nrows, LANES), lambda i: (0, 0)),
            pl.BlockSpec((1, LANES), lambda i: (0, 0)),
        ],
        out_specs=pl.BlockSpec((nrows, LANES), lambda i: (0, 0)),
        out_shape=jax.ShapeDtypeStruct((nrows, LANES), BF16),
        name="query_norm",
    )(rows, gain)
    ys = [nq] + [permute_col(nq, shift_y(s)) for s in range(1, 4)]
    same, other = pl.pallas_call(
        bias_kernel,
        in_specs=[whole()] * 3,
        out_specs=[whole()] * 2,
        out_shape=[jax.ShapeDtypeStruct((KB, LANES), F32)] * 2,
        name="bias_tile",
    )(rows, gain, w_bias)
    same = permute_all(same, lambda r, c: (c // 2, 2 * r + c % 2))
    other = permute_all(other, lambda r, c: (c // 2, 2 * r + 1 - c % 2))
    piece = jnp.concatenate([y.reshape(QROWS, KB, LANES) for y in ys], axis=1)
    piece = piece.reshape(-1, LANES)
    pieces = [piece] + [permute_col(piece, shift_x(s)) for s in range(1, 4)]
    pieces = pieces + [permute_col(p, lambda c: c + 1 - 2 * (c % 2)) for p in pieces]
    pair_bias = jnp.concatenate([same, other], axis=0)
    far = permute_row(pair_bias, lambda r: r + 1 - 2 * (r % 2))
    pair_bias = jnp.concatenate([pair_bias, far], axis=0)
    biases = [pair_bias] + [permute_row(pair_bias, shift_z(s)) for s in range(1, 8)]
    wk = w_keyval[:, :LANES]
    wvt = w_keyval[:, LANES:].T
    out = pl.pallas_call(
        attend_kernel,
        in_specs=[whole()] * 22,
        out_specs=whole(),
        out_shape=jax.ShapeDtypeStruct((nrows, LANES), BF16),
        scratch_shapes=[
            VM((768, LANES), F32),
            VM((768, LANES), BF16),
            VM((768, LANES), F32),
            VM((nrows, LANES), F32),
            VM((nrows, LANES), F32),
            VM((nrows, LANES), F32),
        ],
        compiler_params=pltpu.CompilerParams(vmem_limit_bytes=32 * 1024 * 1024),
        name="attend",
    )(*pieces, *biases, nq, w_query, wk, wvt, w_gate, w_out)
    return out.reshape(QROWS, KB, LANES)


def solution(mesh):
    placed = (P("row", "col", None), P(), P(), P(), P(), P(), P())
    return jax.shard_map(
        body, mesh=mesh, in_specs=placed, out_specs=P("row", "col", None), check_vma=False
    )
```

```python
import jax
import jax.numpy as jnp
from jax import lax
from jax.experimental import pallas as pl
from jax.experimental.pallas import tpu as pltpu
from jax.sharding import PartitionSpec as P

QROWS = 8
KB = 24
HEADS = 4
LANES = 128
NROW = 16
NCOL = 32
F32 = jnp.float32
BF16 = jnp.bfloat16
VM = pltpu.VMEM


def whole(space=VM):
    return pl.BlockSpec(memory_space=space)


def norm_rows(block, gain):
    values = block.astype(F32)
    mean = jnp.mean(values, axis=-1, keepdims=True)
    centred = values - mean
    variance = jnp.mean(centred * centred, axis=-1, keepdims=True)
    return (centred * lax.rsqrt(variance + 1e-05) * gain).astype(BF16)


def query_norm_kernel(rows_ref, gain_ref, out_ref):
    out_ref[...] = norm_rows(rows_ref[...], gain_ref[...])


def bias_kernel(rows_ref, gain_ref, wb_ref, out_ref):
    lane = lax.broadcasted_iota(jnp.int32, (LANES, LANES), 1)
    wb = wb_ref[...].astype(F32)
    spread = jnp.zeros((LANES, LANES), F32)
    for h in range(HEADS):
        inside = (lane >= h * KB) & (lane < (h + 1) * KB)
        spread = jnp.where(inside, wb[:, h : h + 1], spread)
    spread = spread.astype(BF16)
    lane = lax.broadcasted_iota(jnp.int32, (KB, LANES), 1)
    place = jnp.where(lane < HEADS * KB, lax.rem(lane, KB), -1)
    for half in range(2):
        first = half * KB * KB
        normed = norm_rows(rows_ref[first : first + KB * KB, :], gain_ref[...])
        wide = jnp.dot(normed, spread, preferred_element_type=F32)
        total = jnp.zeros((KB, LANES), F32)
        for j in range(KB):
            total = jnp.where(place == j, wide[j * KB : (j + 1) * KB, :], total)
        out_ref[half * KB : (half + 1) * KB, :] = total


def attend_kernel(
    mine_ref, theirs_ref, bias_ref, nq_ref, wq_ref, wk_ref, wvt_ref, wg_ref, wo_ref,
    out_ref, x_ref, s_ref, q_ref, gate_ref, gated_ref,
):
    core = lax.rem(lax.axis_index("col"), 2)
    nq = nq_ref[...]
    scale = 1.0 / 32**0.5
    q_ref[...] = jnp.dot(nq, wq_ref[...], preferred_element_type=F32) * scale
    gate_ref[...] = jax.nn.sigmoid(jnp.dot(nq, wg_ref[...], preferred_element_type=F32))
    lane = lax.broadcasted_iota(jnp.int32, (KB, LANES), 1)
    starts = []
    for p in range(8):
        for y in range(4):
            block = y * 8 + p % 4 * 2 + lax.rem(core + p // 4, 2)
            starts.append(pl.multiple_of(block * KB, 8))

    def one_row(a, carry):
        qrows = pl.ds(pl.multiple_of(a * KB, 8), KB)
        q = q_ref[qrows, :].astype(BF16).astype(F32)
        masked = [jnp.where(lane // 32 == h, q, 0.0) for h in range(HEADS)]
        masked.append(jnp.zeros((LANES - HEADS * KB, LANES), F32))
        masked = jnp.concatenate(masked, axis=0).astype(BF16)
        for p in range(8):
            source = mine_ref if p < 4 else theirs_ref
            x_ref[p * 96 : (p + 1) * 96, :] = source[
                p % 4, pl.ds(pl.multiple_of(a * 96, 32), 96), :
            ]
        rows = x_ref[...]
        keys = jnp.dot(rows, wk_ref[...], preferred_element_type=F32).astype(BF16)
        values_t = lax.dot_general(
            wvt_ref[...], rows, (((1,), (1,)), ((), ())), preferred_element_type=F32
        ).astype(BF16)
        score = lax.dot_general(
            keys, masked, (((1,), (1,)), ((), ())), preferred_element_type=F32
        )
        top = jnp.full((KB, LANES), -jnp.inf, F32)
        for i in range(32):
            part = score[i * KB : (i + 1) * KB, :] + bias_ref[pl.ds(starts[i], KB), :]
            s_ref[i * KB : (i + 1) * KB, :] = part
            top = jnp.maximum(top, part)
        top = jnp.max(top, axis=0, keepdims=True)
        weights = jnp.exp(s_ref[...] - top)
        total = jnp.sum(weights, axis=0, keepdims=True)
        high = weights.astype(BF16)
        low = (weights - high.astype(F32)).astype(BF16)
        attended = jnp.dot(values_t, high, preferred_element_type=F32) + jnp.dot(
            values_t, low, preferred_element_type=F32
        )
        attended = (attended / total).T
        mine = jnp.zeros((KB, LANES), F32)
        for h in range(HEADS):
            mine = jnp.where(lane // 32 == h, attended[h * KB : (h + 1) * KB, :], mine)
        gated_ref[qrows, :] = gate_ref[qrows, :] * mine
        return carry

    lax.fori_loop(0, QROWS, one_row, 0)
    out_ref[...] = jnp.dot(
        gated_ref[...].astype(BF16), wo_ref[...], preferred_element_type=F32
    ).astype(BF16)


def permute_col(value, target):
    return lax.ppermute(value, "col", [(c, target(c)) for c in range(NCOL)])


def permute_all(value, target):
    pairs = []
    for r in range(NROW):
        for c in range(NCOL):
            r2, c2 = target(r, c)
            pairs.append((r * NCOL + c, r2 * NCOL + c2))
    return lax.ppermute(value, ("row", "col"), pairs)


GROUPS_Y = [[y * 8 + i for y in range(4)] for i in range(8)]
GROUPS_X = [[y * 8 + x * 2 + e for x in range(4)] for y in range(4) for e in range(2)]
GROUPS_ROW_CORE = [
    [r * NCOL + 2 * q + e for r in range(NROW) for e in range(2)] for q in range(NCOL // 2)
]


def spread(value, axis, groups):
    copies = jnp.broadcast_to(value[None], (len(groups[0]),) + value.shape)
    return lax.all_to_all(copies, axis, 0, 0, axis_index_groups=groups)


def body(pair, ln_gain, w_query, w_keyval, w_gate, w_bias, w_out):
    rows = pair.reshape(-1, LANES)
    gain = ln_gain.reshape(1, LANES)
    nrows = QROWS * KB
    nq = pl.pallas_call(
        query_norm_kernel,
        grid=(1,),
        in_specs=[
            pl.BlockSpec((nrows, LANES), lambda i: (0, 0)),
            pl.BlockSpec((1, LANES), lambda i: (0, 0)),
        ],
        out_specs=pl.BlockSpec((nrows, LANES), lambda i: (0, 0)),
        out_shape=jax.ShapeDtypeStruct((nrows, LANES), BF16),
        name="query_norm",
    )(rows, gain)
    ys = spread(nq, "col", GROUPS_Y)
    tile = pl.pallas_call(
        bias_kernel,
        in_specs=[whole()] * 3,
        out_specs=whole(),
        out_shape=jax.ShapeDtypeStruct((2 * KB, LANES), F32),
        name="bias_tile",
    )(rows, gain, w_bias)
    tile = permute_all(tile, lambda r, c: (c // 2, 2 * r + c % 2))
    piece = jnp.transpose(ys.reshape(4, QROWS, KB, LANES), (1, 0, 2, 3))
    piece = piece.reshape(-1, LANES)
    mine = spread(piece, "col", GROUPS_X)
    theirs = permute_col(mine, lambda c: c + 1 - 2 * (c % 2))
    halves = jnp.broadcast_to(tile.reshape(1, 2, KB, LANES), (NROW, 2, KB, LANES))
    bias = lax.all_to_all(
        halves.reshape(2 * NROW, KB, LANES),
        ("row", "col"),
        0,
        0,
        axis_index_groups=GROUPS_ROW_CORE,
    )
    wk = w_keyval[:, :LANES]
    wvt = w_keyval[:, LANES:].T
    out = pl.pallas_call(
        attend_kernel,
        in_specs=[whole()] * 9,
        out_specs=whole(),
        out_shape=jax.ShapeDtypeStruct((nrows, LANES), BF16),
        scratch_shapes=[
            VM((768, LANES), BF16),
            VM((768, LANES), F32),
            VM((nrows, LANES), F32),
            VM((nrows, LANES), F32),
            VM((nrows, LANES), F32),
        ],
        compiler_params=pltpu.CompilerParams(vmem_limit_bytes=32 * 1024 * 1024),
        name="attend",
    )(mine, theirs, bias.reshape(-1, LANES), nq, w_query, wk, wvt, w_gate, w_out)
    return out.reshape(QROWS, KB, LANES)


def solution(mesh):
    placed = (P("row", "col", None), P(), P(), P(), P(), P(), P())
    return jax.shard_map(
        body, mesh=mesh, in_specs=placed, out_specs=P("row", "col", None), check_vma=False
    )
```

```python
import jax
import jax.numpy as jnp
from jax import lax
from jax.experimental import pallas as pl
from jax.experimental.pallas import tpu as pltpu
from jax.sharding import PartitionSpec as P

QROWS = 8
KB = 24
HEADS = 4
LANES = 128
NROW = 16
NCOL = 32
F32 = jnp.float32
BF16 = jnp.bfloat16
VM = pltpu.VMEM


def whole(space=VM):
    return pl.BlockSpec(memory_space=space)


def norm_rows(block, gain):
    values = block.astype(F32)
    mean = jnp.mean(values, axis=-1, keepdims=True)
    centred = values - mean
    variance = jnp.mean(centred * centred, axis=-1, keepdims=True)
    return (centred * lax.rsqrt(variance + 1e-05) * gain).astype(BF16)


CHUNKS = ((0, 192), (192, 576), (576, 1152))


def front_kernel(rows_ref, gain_ref, wb_ref, nq_ref, tile_ref, held_ref, sems):
    copies = []
    for i, (begin, end) in enumerate(CHUNKS):
        part = pl.ds(begin, end - begin)
        copy = pltpu.make_async_copy(rows_ref.at[part], held_ref.at[part], sems.at[i])
        copy.start()
        copies.append(copy)
    wb = wb_ref[...].astype(F32)
    spread_t = [jnp.broadcast_to(wb[h : h + 1, :], (KB, LANES)) for h in range(HEADS)]
    spread_t.append(jnp.zeros((LANES - HEADS * KB, LANES), F32))
    spread_t = jnp.concatenate(spread_t, axis=0).astype(BF16)
    lane = lax.broadcasted_iota(jnp.int32, (KB, LANES), 1)
    place = jnp.where(lane < HEADS * KB, lax.rem(lane, KB), -1)
    gain = gain_ref[...]
    total = jnp.zeros((KB, LANES), F32)
    for i, (begin, end) in enumerate(CHUNKS):
        copies[i].wait()
        normed = norm_rows(held_ref[begin:end, :], gain)
        if i == 0:
            for n in range(4):
                nq_ref[n] = normed
        wide = lax.dot_general(
            normed, spread_t, (((1,), (1,)), ((), ())), preferred_element_type=F32
        )
        for j in range(begin // KB, end // KB):
            row = j * KB - begin
            total = jnp.where(place == j % KB, wide[row : row + KB, :], total)
            if j % KB == KB - 1:
                tile_ref[j + 1 - KB : j + 1, :] = total


def attend_kernel(
    mine_ref, theirs_ref, bias_ref, nq_ref, wq_ref, wkv_ref, wg_ref, wo_ref,
    out_ref, x_ref, s_ref, q_ref, gate_ref, gated_ref,
):
    core = lax.rem(lax.axis_index("col"), 2)
    nq = nq_ref[0]
    wk = wkv_ref[:, :LANES]
    wvt = wkv_ref[:, LANES:].astype(F32).T.astype(BF16)
    scale = 1.0 / 32**0.5
    q_ref[...] = jnp.dot(nq, wq_ref[...], preferred_element_type=F32) * scale
    gate_ref[...] = jax.nn.sigmoid(jnp.dot(nq, wg_ref[...], preferred_element_type=F32))
    lane = lax.broadcasted_iota(jnp.int32, (KB, LANES), 1)
    starts = []
    for p in range(8):
        for y in range(4):
            block = y * 8 + p % 4 * 2 + lax.rem(core + p // 4, 2)
            starts.append(pl.multiple_of(block * KB, 8))

    def one_row(a, carry):
        qrows = pl.ds(pl.multiple_of(a * KB, 8), KB)
        q = q_ref[qrows, :].astype(BF16).astype(F32)
        masked = [jnp.where(lane // 32 == h, q, 0.0) for h in range(HEADS)]
        masked.append(jnp.zeros((LANES - HEADS * KB, LANES), F32))
        masked = jnp.concatenate(masked, axis=0).astype(BF16)
        for p in range(8):
            source = mine_ref if p < 4 else theirs_ref
            x_ref[p * 96 : (p + 1) * 96, :] = source[
                p % 4, pl.ds(pl.multiple_of(a * 96, 32), 96), :
            ]
        rows = x_ref[...]
        keys = jnp.dot(rows, wk, preferred_element_type=F32).astype(BF16)
        values_t = lax.dot_general(
            wvt, rows, (((1,), (1,)), ((), ())), preferred_element_type=F32
        ).astype(BF16)
        score = lax.dot_general(
            keys, masked, (((1,), (1,)), ((), ())), preferred_element_type=F32
        )
        top = jnp.full((KB, LANES), -jnp.inf, F32)
        for i in range(32):
            part = score[i * KB : (i + 1) * KB, :] + bias_ref[pl.ds(starts[i], KB), :]
            s_ref[i * KB : (i + 1) * KB, :] = part
            top = jnp.maximum(top, part)
        top = jnp.max(top, axis=0, keepdims=True)
        weights = jnp.exp(s_ref[...] - top)
        total = jnp.sum(weights, axis=0, keepdims=True)
        high = weights.astype(BF16)
        low = (weights - high.astype(F32)).astype(BF16)
        attended = jnp.dot(values_t, high, preferred_element_type=F32) + jnp.dot(
            values_t, low, preferred_element_type=F32
        )
        attended = (attended / total).T
        mine = jnp.zeros((KB, LANES), F32)
        for h in range(HEADS):
            mine = jnp.where(lane // 32 == h, attended[h * KB : (h + 1) * KB, :], mine)
        gated_ref[qrows, :] = gate_ref[qrows, :] * mine
        return carry

    lax.fori_loop(0, QROWS, one_row, 0)
    out_ref[...] = jnp.dot(
        gated_ref[...].astype(BF16), wo_ref[...], preferred_element_type=F32
    ).astype(BF16)


def permute_col(value, target):
    return lax.ppermute(value, "col", [(c, target(c)) for c in range(NCOL)])


def permute_all(value, target):
    pairs = []
    for r in range(NROW):
        for c in range(NCOL):
            r2, c2 = target(r, c)
            pairs.append((r * NCOL + c, r2 * NCOL + c2))
    return lax.ppermute(value, ("row", "col"), pairs)


GROUPS_Y = [[y * 8 + i for y in range(4)] for i in range(8)]
GROUPS_X = [[y * 8 + x * 2 + e for x in range(4)] for y in range(4) for e in range(2)]
GROUPS_ROW_CORE = [
    [r * NCOL + 2 * q + e for r in range(NROW) for e in range(2)] for q in range(NCOL // 2)
]


def spread(value, axis, groups):
    copies = jnp.broadcast_to(value[None], (len(groups[0]),) + value.shape)
    return lax.all_to_all(copies, axis, 0, 0, axis_index_groups=groups)


def body(pair, ln_gain, w_query, w_keyval, w_gate, w_bias, w_out):
    rows = pair.reshape(-1, LANES)
    gain = ln_gain.reshape(1, LANES)
    nrows = QROWS * KB
    nq, tile = pl.pallas_call(
        front_kernel,
        in_specs=[whole(pl.ANY), whole(), whole()],
        out_specs=[whole(), whole()],
        out_shape=[
            jax.ShapeDtypeStruct((4, nrows, LANES), BF16),
            jax.ShapeDtypeStruct((2 * KB, LANES), F32),
        ],
        scratch_shapes=[VM((rows.shape[0], LANES), BF16), pltpu.SemaphoreType.DMA((3,))],
        name="front",
    )(rows, gain, w_bias.T)
    tile = permute_all(tile, lambda r, c: (c // 2, 2 * r + c % 2))
    ys = lax.all_to_all(nq, "col", 0, 0, axis_index_groups=GROUPS_Y)
    piece = jnp.transpose(ys.reshape(4, QROWS, KB, LANES), (1, 0, 2, 3))
    piece = piece.reshape(-1, LANES)
    mine = spread(piece, "col", GROUPS_X)
    theirs = permute_col(mine, lambda c: c + 1 - 2 * (c % 2))
    halves = jnp.broadcast_to(tile.reshape(1, 2, KB, LANES), (NROW, 2, KB, LANES))
    bias = lax.all_to_all(
        halves.reshape(2 * NROW, KB, LANES),
        ("row", "col"),
        0,
        0,
        axis_index_groups=GROUPS_ROW_CORE,
    )
    out = pl.pallas_call(
        attend_kernel,
        in_specs=[whole()] * 8,
        out_specs=whole(),
        out_shape=jax.ShapeDtypeStruct((nrows, LANES), BF16),
        scratch_shapes=[
            VM((768, LANES), BF16),
            VM((768, LANES), F32),
            VM((nrows, LANES), F32),
            VM((nrows, LANES), F32),
            VM((nrows, LANES), F32),
        ],
        compiler_params=pltpu.CompilerParams(vmem_limit_bytes=32 * 1024 * 1024),
        name="attend",
    )(mine, theirs, bias.reshape(-1, LANES), nq, w_query, w_keyval, w_gate, w_out)
    return out.reshape(QROWS, KB, LANES)


def solution(mesh):
    placed = (P("row", "col", None), P(), P(), P(), P(), P(), P())
    return jax.shard_map(
        body, mesh=mesh, in_specs=placed, out_specs=P("row", "col", None), check_vma=False
    )
```

```python
import jax
import jax.numpy as jnp
from jax import lax
from jax.experimental import pallas as pl
from jax.experimental.pallas import tpu as pltpu
from jax.sharding import PartitionSpec as P

QROWS = 8
KB = 24
HEADS = 4
LANES = 128
NROW = 16
NCOL = 32
F32 = jnp.float32
BF16 = jnp.bfloat16
VM = pltpu.VMEM


def whole(space=VM):
    return pl.BlockSpec(memory_space=space)


def norm_rows(block, gain):
    values = block.astype(F32)
    mean = jnp.mean(values, axis=-1, keepdims=True)
    centred = values - mean
    variance = jnp.mean(centred * centred, axis=-1, keepdims=True)
    return (centred * lax.rsqrt(variance + 1e-05) * gain).astype(BF16)


CHUNKS = ((0, 192), (192, 576), (576, 1152))


def front_kernel(rows_ref, gain_ref, wb_ref, nq_ref, tile_ref, held_ref, sems):
    copies = []
    for i, (begin, end) in enumerate(CHUNKS):
        part = pl.ds(begin, end - begin)
        copy = pltpu.make_async_copy(rows_ref.at[part], held_ref.at[part], sems.at[i])
        copy.start()
        copies.append(copy)
    wb = wb_ref[...].astype(F32)
    spread_t = [jnp.broadcast_to(wb[h : h + 1, :], (KB, LANES)) for h in range(HEADS)]
    spread_t.append(jnp.zeros((LANES - HEADS * KB, LANES), F32))
    spread_t = jnp.concatenate(spread_t, axis=0).astype(BF16)
    lane = lax.broadcasted_iota(jnp.int32, (KB, LANES), 1)
    place = jnp.where(lane < HEADS * KB, lax.rem(lane, KB), -1)
    gain = gain_ref[...]
    total = jnp.zeros((KB, LANES), F32)
    for i, (begin, end) in enumerate(CHUNKS):
        copies[i].wait()
        normed = norm_rows(held_ref[begin:end, :], gain)
        if i == 0:
            for n in range(4):
                nq_ref[n] = normed
        wide = lax.dot_general(
            normed, spread_t, (((1,), (1,)), ((), ())), preferred_element_type=F32
        )
        for j in range(begin // KB, end // KB):
            row = j * KB - begin
            total = jnp.where(place == j % KB, wide[row : row + KB, :], total)
            if j % KB == KB - 1:
                tile_ref[j + 1 - KB : j + 1, :] = total


def relay_kernel(ys_ref, later_ref, out_ref):
    del later_ref
    for a in range(QROWS):
        parts = [ys_ref[y, a * KB : (a + 1) * KB, :].astype(F32) for y in range(4)]
        block = jnp.concatenate(parts, axis=0).astype(BF16)
        for n in range(4):
            out_ref[n, a * 96 : (a + 1) * 96, :] = block


def attend_kernel(
    mine_ref, theirs_ref, near_ref, far_ref, nq_ref, wq_ref, wkv_ref, wg_ref, wo_ref,
    out_ref, bias_ref, x_ref, s_ref, q_ref, gate_ref, gated_ref,
):
    core = lax.rem(lax.axis_index("col"), 2)
    y_lo = lax.rem(lax.axis_index("row"), 2)
    for z in range(8):
        for e in range(2):
            slot = z * 2 + e
            for source, t in ((near_ref, y_lo), (far_ref, 1 - y_lo)):
                start = pl.multiple_of((z * 4 + t * 2 + e) * KB, 8)
                bias_ref[pl.ds(start, KB), :] = source[slot]
    nq = nq_ref[0]
    wk = wkv_ref[:, :LANES]
    wvt = wkv_ref[:, LANES:].astype(F32).T.astype(BF16)
    scale = 1.0 / 32**0.5
    q_ref[...] = jnp.dot(nq, wq_ref[...], preferred_element_type=F32) * scale
    gate_ref[...] = jax.nn.sigmoid(jnp.dot(nq, wg_ref[...], preferred_element_type=F32))
    lane = lax.broadcasted_iota(jnp.int32, (KB, LANES), 1)
    starts = []
    for p in range(8):
        for y in range(4):
            block = y * 8 + p % 4 * 2 + lax.rem(core + p // 4, 2)
            starts.append(pl.multiple_of(block * KB, 8))

    def one_row(a, carry):
        qrows = pl.ds(pl.multiple_of(a * KB, 8), KB)
        q = q_ref[qrows, :].astype(BF16).astype(F32)
        masked = [jnp.where(lane // 32 == h, q, 0.0) for h in range(HEADS)]
        masked.append(jnp.zeros((LANES - HEADS * KB, LANES), F32))
        masked = jnp.concatenate(masked, axis=0).astype(BF16)
        for p in range(8):
            source = mine_ref if p < 4 else theirs_ref
            x_ref[p * 96 : (p + 1) * 96, :] = source[
                p % 4, pl.ds(pl.multiple_of(a * 96, 32), 96), :
            ]
        rows = x_ref[...]
        keys = jnp.dot(rows, wk, preferred_element_type=F32).astype(BF16)
        values_t = lax.dot_general(
            wvt, rows, (((1,), (1,)), ((), ())), preferred_element_type=F32
        ).astype(BF16)
        score = lax.dot_general(
            keys, masked, (((1,), (1,)), ((), ())), preferred_element_type=F32
        )
        top = jnp.full((KB, LANES), -jnp.inf, F32)
        for i in range(32):
            part = score[i * KB : (i + 1) * KB, :] + bias_ref[pl.ds(starts[i], KB), :]
            s_ref[i * KB : (i + 1) * KB, :] = part
            top = jnp.maximum(top, part)
        top = jnp.max(top, axis=0, keepdims=True)
        weights = jnp.exp(s_ref[...] - top)
        total = jnp.sum(weights, axis=0, keepdims=True)
        high = weights.astype(BF16)
        low = (weights - high.astype(F32)).astype(BF16)
        attended = jnp.dot(values_t, high, preferred_element_type=F32) + jnp.dot(
            values_t, low, preferred_element_type=F32
        )
        attended = (attended / total).T
        mine = jnp.zeros((KB, LANES), F32)
        for h in range(HEADS):
            mine = jnp.where(lane // 32 == h, attended[h * KB : (h + 1) * KB, :], mine)
        gated_ref[qrows, :] = gate_ref[qrows, :] * mine
        return carry

    lax.fori_loop(0, QROWS, one_row, 0)
    out_ref[...] = jnp.dot(
        gated_ref[...].astype(BF16), wo_ref[...], preferred_element_type=F32
    ).astype(BF16)


def permute_col(value, target):
    return lax.ppermute(value, "col", [(c, target(c)) for c in range(NCOL)])


def permute_all(value, target):
    pairs = []
    for r in range(NROW):
        for c in range(NCOL):
            r2, c2 = target(r, c)
            pairs.append((r * NCOL + c, r2 * NCOL + c2))
    return lax.ppermute(value, ("row", "col"), pairs)


GROUPS_Y = [[y * 8 + i for y in range(4)] for i in range(8)]
GROUPS_X = [[y * 8 + x * 2 + e for x in range(4)] for y in range(4) for e in range(2)]
GROUPS_Z_CORE = [
    [(z * 2 + t) * NCOL + 2 * q + e for z in range(8) for e in range(2)]
    for t in range(2)
    for q in range(NCOL // 2)
]


def body(pair, ln_gain, w_query, w_keyval, w_gate, w_bias, w_out):
    rows = pair.reshape(-1, LANES)
    gain = ln_gain.reshape(1, LANES)
    nrows = QROWS * KB
    nq, tile = pl.pallas_call(
        front_kernel,
        in_specs=[whole(pl.ANY), whole(), whole()],
        out_specs=[whole(), whole()],
        out_shape=[
            jax.ShapeDtypeStruct((4, nrows, LANES), BF16),
            jax.ShapeDtypeStruct((2 * KB, LANES), F32),
        ],
        scratch_shapes=[VM((rows.shape[0], LANES), BF16), pltpu.SemaphoreType.DMA((3,))],
        name="front",
    )(rows, gain, w_bias.T)
    tile = permute_all(tile, lambda r, c: (c // 2, 2 * r + c % 2))
    ys = lax.all_to_all(nq, "col", 0, 0, axis_index_groups=GROUPS_Y)
    halves = jnp.broadcast_to(tile.reshape(1, 2, KB, LANES), (8, 2, KB, LANES))
    near = lax.all_to_all(
        halves.reshape(16, KB, LANES), ("row", "col"), 0, 0, axis_index_groups=GROUPS_Z_CORE
    )
    far = lax.ppermute(near, "row", [(r, r + 1 - 2 * (r % 2)) for r in range(NROW)])
    piece = pl.pallas_call(
        relay_kernel,
        in_specs=[whole(), whole(pl.ANY)],
        out_specs=whole(),
        out_shape=jax.ShapeDtypeStruct((4, 4 * nrows, LANES), BF16),
        name="relay",
    )(ys, near)
    mine = lax.all_to_all(piece, "col", 0, 0, axis_index_groups=GROUPS_X)
    theirs = permute_col(mine, lambda c: c + 1 - 2 * (c % 2))
    out = pl.pallas_call(
        attend_kernel,
        in_specs=[whole()] * 9,
        out_specs=whole(),
        out_shape=jax.ShapeDtypeStruct((nrows, LANES), BF16),
        scratch_shapes=[
            VM((768, LANES), F32),
            VM((768, LANES), BF16),
            VM((768, LANES), F32),
            VM((nrows, LANES), F32),
            VM((nrows, LANES), F32),
            VM((nrows, LANES), F32),
        ],
        compiler_params=pltpu.CompilerParams(vmem_limit_bytes=32 * 1024 * 1024),
        name="attend",
    )(mine, theirs, near, far, nq, w_query, w_keyval, w_gate, w_out)
    return out.reshape(QROWS, KB, LANES)


def solution(mesh):
    placed = (P("row", "col", None), P(), P(), P(), P(), P(), P())
    return jax.shard_map(
        body, mesh=mesh, in_specs=placed, out_specs=P("row", "col", None), check_vma=False
    )
```

```python
import jax
import jax.numpy as jnp
from jax import lax
from jax.experimental import pallas as pl
from jax.experimental.pallas import tpu as pltpu
from jax.sharding import PartitionSpec as P

QROWS = 8
KB = 24
HEADS = 4
LANES = 128
NROW = 16
NCOL = 32
F32 = jnp.float32
BF16 = jnp.bfloat16
VM = pltpu.VMEM


def whole(space=VM):
    return pl.BlockSpec(memory_space=space)


PARTNERS = (0, 1, 3, 2)


def norm_rows(block, gain):
    values = block.astype(F32)
    mean = jnp.mean(values, axis=-1, keepdims=True)
    centred = values - mean
    variance = jnp.mean(centred * centred, axis=-1, keepdims=True)
    return (centred * lax.rsqrt(variance + 1e-05) * gain).astype(BF16)


CHUNKS = ((0, 192), (192, 576), (576, 1152))


def front_kernel(rows_ref, gain_ref, wb_ref, nq_ref, same_ref, other_ref, held_ref, sems):
    core = lax.rem(lax.axis_index("col"), 2)
    copies = []
    for i, (begin, end) in enumerate(CHUNKS):
        part = pl.ds(begin, end - begin)
        copy = pltpu.make_async_copy(rows_ref.at[part], held_ref.at[part], sems.at[i])
        copy.start()
        copies.append(copy)
    wb = wb_ref[...].astype(F32)
    spread_t = [jnp.broadcast_to(wb[h : h + 1, :], (KB, LANES)) for h in range(HEADS)]
    spread_t.append(jnp.zeros((LANES - HEADS * KB, LANES), F32))
    spread_t = jnp.concatenate(spread_t, axis=0).astype(BF16)
    lane = lax.broadcasted_iota(jnp.int32, (KB, LANES), 1)
    place = jnp.where(lane < HEADS * KB, lax.rem(lane, KB), -1)
    gain = gain_ref[...]
    halves = []
    total = jnp.zeros((KB, LANES), F32)
    for i, (begin, end) in enumerate(CHUNKS):
        copies[i].wait()
        normed = norm_rows(held_ref[begin:end, :], gain)
        if i == 0:
            nq_ref[...] = normed
        wide = lax.dot_general(
            normed, spread_t, (((1,), (1,)), ((), ())), preferred_element_type=F32
        )
        for j in range(begin // KB, end // KB):
            row = j * KB - begin
            total = jnp.where(place == j % KB, wide[row : row + KB, :], total)
            if j % KB == KB - 1:
                halves.append(total)
    same_ref[...] = jnp.where(core == 0, halves[0], halves[1])
    other_ref[...] = jnp.where(core == 0, halves[1], halves[0])


def across(z):
    return lax.rem(jnp.where(lax.rem(z, 2) == 1, z + 1, z + 7), 8)


def opposite(z):
    return jnp.where((z == 0) | (z == 3), 3 - z, jnp.where((z == 4) | (z == 7), 11 - z, 7 - z))


def attend_kernel(*refs):
    pieces = refs[0:4]
    theirs_a_ref, theirs_b_ref, near_ref, far_ref = refs[4:8]
    nq_ref, wq_ref, wkv_ref, wg_ref, wo_ref, out_ref = refs[8:14]
    bias_ref, x_ref, s_ref, q_ref, gate_ref, gated_ref = refs[14:20]
    row = lax.axis_index("row")
    col = lax.axis_index("col")
    core = lax.rem(col, 2)
    x = lax.rem(col // 2, 4)
    y_hi = col // 8
    z = row // 2
    y_lo = lax.rem(row, 2)
    held = []
    for base in (z, opposite(z)):
        for part in (base, across(base)):
            held += [part, lax.bitwise_xor(part, 1)]
    for slot in range(8):
        for e in range(2):
            block = held[slot] * 4 + lax.bitwise_xor(core, e)
            begin = (slot * 2 + e) * KB
            for source, t in ((near_ref, y_lo), (far_ref, 1 - y_lo)):
                start = pl.multiple_of((block + t * 2) * KB, 8)
                bias_ref[pl.ds(start, KB), :] = source[begin : begin + KB, :]
    nq = nq_ref[...]
    wk = wkv_ref[:, :LANES]
    wvt = wkv_ref[:, LANES:].astype(F32).T.astype(BF16)
    scale = 1.0 / 32**0.5
    q_ref[...] = jnp.dot(nq, wq_ref[...], preferred_element_type=F32) * scale
    gate_ref[...] = jax.nn.sigmoid(jnp.dot(nq, wg_ref[...], preferred_element_type=F32))
    lane = lax.broadcasted_iota(jnp.int32, (KB, LANES), 1)
    starts = []
    for p in range(8):
        for sy in range(4):
            block = (
                lax.bitwise_xor(y_hi, PARTNERS[sy]) * 8
                + lax.bitwise_xor(x, PARTNERS[p % 4]) * 2
                + lax.bitwise_xor(core, p // 4)
            )
            starts.append(pl.multiple_of(block * KB, 8))

    sources = list(pieces) + [theirs_a_ref.at[i] for i in range(3)] + [theirs_b_ref]

    def one_row(a, carry):
        qrows = pl.ds(pl.multiple_of(a * KB, 8), KB)
        q = q_ref[qrows, :].astype(BF16).astype(F32)
        masked = [jnp.where(lane // 32 == h, q, 0.0) for h in range(HEADS)]
        masked.append(jnp.zeros((LANES - HEADS * KB, LANES), F32))
        masked = jnp.concatenate(masked, axis=0).astype(BF16)
        for p in range(8):
            source = sources[p]
            x_ref[p * 96 : (p + 1) * 96, :] = source[pl.ds(pl.multiple_of(a * 96, 32), 96), :]
        rows = x_ref[...]
        keys = jnp.dot(rows, wk, preferred_element_type=F32).astype(BF16)
        values_t = lax.dot_general(
            wvt, rows, (((1,), (1,)), ((), ())), preferred_element_type=F32
        ).astype(BF16)
        score = lax.dot_general(
            keys, masked, (((1,), (1,)), ((), ())), preferred_element_type=F32
        )
        top = jnp.full((KB, LANES), -jnp.inf, F32)
        for i in range(32):
            part = score[i * KB : (i + 1) * KB, :] + bias_ref[pl.ds(starts[i], KB), :]
            s_ref[i * KB : (i + 1) * KB, :] = part
            top = jnp.maximum(top, part)
        top = jnp.max(top, axis=0, keepdims=True)
        weights = jnp.exp(s_ref[...] - top)
        total = jnp.sum(weights, axis=0, keepdims=True)
        high = weights.astype(BF16)
        low = (weights - high.astype(F32)).astype(BF16)
        attended = jnp.dot(values_t, high, preferred_element_type=F32) + jnp.dot(
            values_t, low, preferred_element_type=F32
        )
        attended = (attended / total).T
        mine = jnp.zeros((KB, LANES), F32)
        for h in range(HEADS):
            mine = jnp.where(lane // 32 == h, attended[h * KB : (h + 1) * KB, :], mine)
        gated_ref[qrows, :] = gate_ref[qrows, :] * mine
        return carry

    lax.fori_loop(0, QROWS, one_row, 0)
    out_ref[...] = jnp.dot(
        gated_ref[...].astype(BF16), wo_ref[...], preferred_element_type=F32
    ).astype(BF16)


def permute_col(value, target):
    return lax.ppermute(value, "col", [(c, target(c)) for c in range(NCOL)])


def permute_row(value, target):
    return lax.ppermute(value, "row", [(r, target(r)) for r in range(NROW)])


def permute_all(value, target):
    pairs = []
    for r in range(NROW):
        for c in range(NCOL):
            r2, c2 = target(r, c)
            pairs.append((r * NCOL + c, r2 * NCOL + c2))
    return lax.ppermute(value, ("row", "col"), pairs)


def near_y(mask):
    return lambda c: c ^ (mask * 8)


def near_x(mask):
    return lambda c: c ^ (mask * 2)


def near_z(partner):
    return lambda r: partner[r // 2] * 2 + r % 2


Z_STEPS = ((1, 0, 3, 2, 5, 4, 7, 6), (7, 2, 1, 4, 3, 6, 5, 0), (3, 6, 5, 0, 7, 2, 1, 4))


def gather_four(value, near):
    first = permute_col(value, near(1))
    second = permute_col(value, near(3))
    third = permute_col(first, near(3))
    return [value, first, second, third]


def body(pair, ln_gain, w_query, w_keyval, w_gate, w_bias, w_out):
    rows = pair.reshape(-1, LANES)
    gain = ln_gain.reshape(1, LANES)
    nrows = QROWS * KB
    nq, same, other = pl.pallas_call(
        front_kernel,
        in_specs=[whole(pl.ANY), whole(), whole()],
        out_specs=[whole()] * 3,
        out_shape=[
            jax.ShapeDtypeStruct((nrows, LANES), BF16),
            jax.ShapeDtypeStruct((KB, LANES), F32),
            jax.ShapeDtypeStruct((KB, LANES), F32),
        ],
        scratch_shapes=[VM((rows.shape[0], LANES), BF16), pltpu.SemaphoreType.DMA((3,))],
        name="front",
    )(rows, gain, w_bias.T)
    ys = gather_four(nq, near_y)
    same = permute_all(same, lambda r, c: (c // 2, 2 * r + c % 2))
    other = permute_all(other, lambda r, c: (c // 2, 2 * r + 1 - c % 2))
    near = jnp.concatenate([same, other], axis=0)
    for step in Z_STEPS:
        near = jnp.concatenate([near, permute_row(near, near_z(step))], axis=0)
    far = permute_row(near, lambda r: r ^ 1)
    piece = jnp.concatenate([y.reshape(QROWS, KB, LANES) for y in ys], axis=1)
    mine = gather_four(piece.reshape(-1, LANES), near_x)
    theirs_a = permute_col(jnp.stack(mine[:3]), lambda c: c ^ 1)
    theirs_b = permute_col(mine[3], lambda c: c ^ 1)
    out = pl.pallas_call(
        attend_kernel,
        in_specs=[whole()] * 13,
        out_specs=whole(),
        out_shape=jax.ShapeDtypeStruct((nrows, LANES), BF16),
        scratch_shapes=[
            VM((768, LANES), F32),
            VM((768, LANES), BF16),
            VM((768, LANES), F32),
            VM((nrows, LANES), F32),
            VM((nrows, LANES), F32),
            VM((nrows, LANES), F32),
        ],
        compiler_params=pltpu.CompilerParams(vmem_limit_bytes=32 * 1024 * 1024),
        name="attend",
    )(*mine, theirs_a, theirs_b, near, far, nq, w_query, w_keyval, w_gate, w_out)
    return out.reshape(QROWS, KB, LANES)


def solution(mesh):
    placed = (P("row", "col", None), P(), P(), P(), P(), P(), P())
    return jax.shard_map(
        body, mesh=mesh, in_specs=placed, out_specs=P("row", "col", None), check_vma=False
    )
```

```python
import jax
import jax.numpy as jnp
from jax import lax
from jax.experimental import pallas as pl
from jax.experimental.pallas import tpu as pltpu
from jax.sharding import PartitionSpec as P

QROWS = 8
KB = 24
HEADS = 4
LANES = 128
NROW = 16
NCOL = 32
F32 = jnp.float32
BF16 = jnp.bfloat16
VM = pltpu.VMEM


def whole(space=VM):
    return pl.BlockSpec(memory_space=space)


PARTNERS = (0, 1, 3, 2)


def norm_rows(block, gain):
    values = block.astype(F32)
    mean = jnp.mean(values, axis=-1, keepdims=True)
    centred = values - mean
    variance = jnp.mean(centred * centred, axis=-1, keepdims=True)
    return (centred * lax.rsqrt(variance + 1e-05) * gain).astype(BF16)


CHUNKS = ((0, 192), (192, 576), (576, 1152))


def front_kernel(rows_ref, gain_ref, wb_ref, nq_ref, tile_ref, held_ref, sems):
    copies = []
    for i, (begin, end) in enumerate(CHUNKS):
        part = pl.ds(begin, end - begin)
        copy = pltpu.make_async_copy(rows_ref.at[part], held_ref.at[part], sems.at[i])
        copy.start()
        copies.append(copy)
    wb = wb_ref[...].astype(F32)
    spread_t = [jnp.broadcast_to(wb[h : h + 1, :], (KB, LANES)) for h in range(HEADS)]
    spread_t.append(jnp.zeros((LANES - HEADS * KB, LANES), F32))
    spread_t = jnp.concatenate(spread_t, axis=0).astype(BF16)
    lane = lax.broadcasted_iota(jnp.int32, (KB, LANES), 1)
    place = jnp.where(lane < HEADS * KB, lax.rem(lane, KB), -1)
    gain = gain_ref[...]
    total = jnp.zeros((KB, LANES), F32)
    for i, (begin, end) in enumerate(CHUNKS):
        copies[i].wait()
        normed = norm_rows(held_ref[begin:end, :], gain)
        if i == 0:
            nq_ref[...] = normed
        wide = lax.dot_general(
            normed, spread_t, (((1,), (1,)), ((), ())), preferred_element_type=F32
        )
        for j in range(begin // KB, end // KB):
            row = j * KB - begin
            total = jnp.where(place == j % KB, wide[row : row + KB, :], total)
            if j % KB == KB - 1:
                tile_ref[j + 1 - KB : j + 1, :] = total


def attend_kernel(*refs):
    pieces = refs[0:4]
    theirs_a_ref, theirs_b_ref, bias_ref = refs[4:7]
    nq_ref, wq_ref, wkv_ref, wg_ref, wo_ref, out_ref = refs[7:13]
    x_ref, s_ref, q_ref, gate_ref, gated_ref = refs[13:18]
    col = lax.axis_index("col")
    core = lax.rem(col, 2)
    x = lax.rem(col // 2, 4)
    y_hi = col // 8
    nq = nq_ref[...]
    wk = wkv_ref[:, :LANES]
    wvt = wkv_ref[:, LANES:].astype(F32).T.astype(BF16)
    scale = 1.0 / 32**0.5
    q_ref[...] = jnp.dot(nq, wq_ref[...], preferred_element_type=F32) * scale
    gate_ref[...] = jax.nn.sigmoid(jnp.dot(nq, wg_ref[...], preferred_element_type=F32))
    lane = lax.broadcasted_iota(jnp.int32, (KB, LANES), 1)
    starts = []
    for p in range(8):
        for sy in range(4):
            block = (
                lax.bitwise_xor(y_hi, PARTNERS[sy]) * 8
                + lax.bitwise_xor(x, PARTNERS[p % 4]) * 2
                + lax.bitwise_xor(core, p // 4)
            )
            starts.append(pl.multiple_of(block * KB, 8))

    sources = list(pieces) + [theirs_a_ref.at[i] for i in range(3)] + [theirs_b_ref]

    def one_row(a, carry):
        qrows = pl.ds(pl.multiple_of(a * KB, 8), KB)
        q = q_ref[qrows, :].astype(BF16).astype(F32)
        masked = [jnp.where(lane // 32 == h, q, 0.0) for h in range(HEADS)]
        masked.append(jnp.zeros((LANES - HEADS * KB, LANES), F32))
        masked = jnp.concatenate(masked, axis=0).astype(BF16)
        for p in range(8):
            source = sources[p]
            x_ref[p * 96 : (p + 1) * 96, :] = source[pl.ds(pl.multiple_of(a * 96, 32), 96), :]
        rows = x_ref[...]
        keys = jnp.dot(rows, wk, preferred_element_type=F32).astype(BF16)
        values_t = lax.dot_general(
            wvt, rows, (((1,), (1,)), ((), ())), preferred_element_type=F32
        ).astype(BF16)
        score = lax.dot_general(
            keys, masked, (((1,), (1,)), ((), ())), preferred_element_type=F32
        )
        top = jnp.full((KB, LANES), -jnp.inf, F32)
        for i in range(32):
            part = score[i * KB : (i + 1) * KB, :] + bias_ref[pl.ds(starts[i], KB), :]
            s_ref[i * KB : (i + 1) * KB, :] = part
            top = jnp.maximum(top, part)
        top = jnp.max(top, axis=0, keepdims=True)
        weights = jnp.exp(s_ref[...] - top)
        total = jnp.sum(weights, axis=0, keepdims=True)
        high = weights.astype(BF16)
        low = (weights - high.astype(F32)).astype(BF16)
        attended = jnp.dot(values_t, high, preferred_element_type=F32) + jnp.dot(
            values_t, low, preferred_element_type=F32
        )
        attended = (attended / total).T
        mine = jnp.zeros((KB, LANES), F32)
        for h in range(HEADS):
            mine = jnp.where(lane // 32 == h, attended[h * KB : (h + 1) * KB, :], mine)
        gated_ref[qrows, :] = gate_ref[qrows, :] * mine
        return carry

    lax.fori_loop(0, QROWS, one_row, 0)
    out_ref[...] = jnp.dot(
        gated_ref[...].astype(BF16), wo_ref[...], preferred_element_type=F32
    ).astype(BF16)


def permute_col(value, target):
    return lax.ppermute(value, "col", [(c, target(c)) for c in range(NCOL)])


def permute_all(value, target):
    pairs = []
    for r in range(NROW):
        for c in range(NCOL):
            r2, c2 = target(r, c)
            pairs.append((r * NCOL + c, r2 * NCOL + c2))
    return lax.ppermute(value, ("row", "col"), pairs)


def near_y(mask):
    return lambda c: c ^ (mask * 8)


def near_x(mask):
    return lambda c: c ^ (mask * 2)


GROUPS_ROW_CORE = [
    [r * NCOL + 2 * q + e for r in range(NROW) for e in range(2)] for q in range(NCOL // 2)
]


def gather_four(value, near):
    first = permute_col(value, near(1))
    second = permute_col(value, near(3))
    third = permute_col(first, near(3))
    return [value, first, second, third]


def body(pair, ln_gain, w_query, w_keyval, w_gate, w_bias, w_out):
    rows = pair.reshape(-1, LANES)
    gain = ln_gain.reshape(1, LANES)
    nrows = QROWS * KB
    nq, tile = pl.pallas_call(
        front_kernel,
        in_specs=[whole(pl.ANY), whole(), whole()],
        out_specs=[whole()] * 2,
        out_shape=[
            jax.ShapeDtypeStruct((nrows, LANES), BF16),
            jax.ShapeDtypeStruct((2 * KB, LANES), F32),
        ],
        scratch_shapes=[VM((rows.shape[0], LANES), BF16), pltpu.SemaphoreType.DMA((3,))],
        name="front",
    )(rows, gain, w_bias.T)
    ys = gather_four(nq, near_y)
    tile = permute_all(tile, lambda r, c: (c // 2, 2 * r + c % 2))
    halves = jnp.broadcast_to(tile.reshape(1, 2, KB, LANES), (NROW, 2, KB, LANES))
    bias = lax.all_to_all(
        halves.reshape(2 * NROW, KB, LANES),
        ("row", "col"),
        0,
        0,
        axis_index_groups=GROUPS_ROW_CORE,
    )
    piece = jnp.concatenate([y.reshape(QROWS, KB, LANES) for y in ys], axis=1)
    mine = gather_four(piece.reshape(-1, LANES), near_x)
    theirs_a = permute_col(jnp.stack(mine[:3]), lambda c: c ^ 1)
    theirs_b = permute_col(mine[3], lambda c: c ^ 1)
    out = pl.pallas_call(
        attend_kernel,
        in_specs=[whole()] * 12,
        out_specs=whole(),
        out_shape=jax.ShapeDtypeStruct((nrows, LANES), BF16),
        scratch_shapes=[
            VM((768, LANES), BF16),
            VM((768, LANES), F32),
            VM((nrows, LANES), F32),
            VM((nrows, LANES), F32),
            VM((nrows, LANES), F32),
        ],
        compiler_params=pltpu.CompilerParams(vmem_limit_bytes=32 * 1024 * 1024),
        name="attend",
    )(*mine, theirs_a, theirs_b, bias.reshape(-1, LANES), nq, w_query, w_keyval, w_gate, w_out)
    return out.reshape(QROWS, KB, LANES)


def solution(mesh):
    placed = (P("row", "col", None), P(), P(), P(), P(), P(), P())
    return jax.shard_map(
        body, mesh=mesh, in_specs=placed, out_specs=P("row", "col", None), check_vma=False
    )
```

```python
import jax
import jax.numpy as jnp
from jax import lax
from jax.experimental import pallas as pl
from jax.experimental.pallas import tpu as pltpu
from jax.sharding import PartitionSpec as P

QROWS = 8
KB = 24
HEADS = 4
LANES = 128
NROW = 16
NCOL = 32
F32 = jnp.float32
BF16 = jnp.bfloat16
VM = pltpu.VMEM


def whole(space=VM):
    return pl.BlockSpec(memory_space=space)


PARTNERS = (0, 1, 3, 2)


def norm_rows(block, gain):
    values = block.astype(F32)
    mean = jnp.mean(values, axis=-1, keepdims=True)
    centred = values - mean
    variance = jnp.mean(centred * centred, axis=-1, keepdims=True)
    return (centred * lax.rsqrt(variance + 1e-05) * gain).astype(BF16)


CHUNKS = ((0, 192), (192, 576), (576, 1152))


def front_kernel(rows_ref, gain_ref, wb_ref, nq_ref, tile_ref, held_ref, sems):
    copies = []
    for i, (begin, end) in enumerate(CHUNKS):
        part = pl.ds(begin, end - begin)
        copy = pltpu.make_async_copy(rows_ref.at[part], held_ref.at[part], sems.at[i])
        copy.start()
        copies.append(copy)
    wb = wb_ref[...].astype(F32)
    spread_t = [jnp.broadcast_to(wb[h : h + 1, :], (KB, LANES)) for h in range(HEADS)]
    spread_t.append(jnp.zeros((LANES - HEADS * KB, LANES), F32))
    spread_t = jnp.concatenate(spread_t, axis=0).astype(BF16)
    lane = lax.broadcasted_iota(jnp.int32, (KB, LANES), 1)
    place = jnp.where(lane < HEADS * KB, lax.rem(lane, KB), -1)
    gain = gain_ref[...]
    total = jnp.zeros((KB, LANES), F32)
    for i, (begin, end) in enumerate(CHUNKS):
        copies[i].wait()
        normed = norm_rows(held_ref[begin:end, :], gain)
        if i == 0:
            for n in range(4):
                nq_ref[n] = normed
        wide = lax.dot_general(
            normed, spread_t, (((1,), (1,)), ((), ())), preferred_element_type=F32
        )
        for j in range(begin // KB, end // KB):
            row = j * KB - begin
            total = jnp.where(place == j % KB, wide[row : row + KB, :], total)
            if j % KB == KB - 1:
                tile_ref[j + 1 - KB : j + 1, :] = total


def relay_kernel(ys_ref, tile_ref, out_ref):
    del tile_ref
    for a in range(QROWS):
        parts = [ys_ref[y, a * KB : (a + 1) * KB, :].astype(F32) for y in range(4)]
        out_ref[a * 96 : (a + 1) * 96, :] = jnp.concatenate(parts, axis=0).astype(BF16)


def attend_kernel(*refs):
    pieces = refs[0:4]
    theirs_a_ref, theirs_b_ref, bias_ref = refs[4:7]
    nq_ref, wq_ref, wkv_ref, wg_ref, wo_ref, out_ref = refs[7:13]
    x_ref, s_ref, q_ref, gate_ref, gated_ref = refs[13:18]
    col = lax.axis_index("col")
    core = lax.rem(col, 2)
    x = lax.rem(col // 2, 4)
    nq = nq_ref[0]
    wk = wkv_ref[:, :LANES]
    wvt = wkv_ref[:, LANES:].astype(F32).T.astype(BF16)
    scale = 1.0 / 32**0.5
    q_ref[...] = jnp.dot(nq, wq_ref[...], preferred_element_type=F32) * scale
    gate_ref[...] = jax.nn.sigmoid(jnp.dot(nq, wg_ref[...], preferred_element_type=F32))
    lane = lax.broadcasted_iota(jnp.int32, (KB, LANES), 1)
    starts = []
    for p in range(8):
        for sy in range(4):
            block = (
                sy * 8
                + lax.bitwise_xor(x, PARTNERS[p % 4]) * 2
                + lax.bitwise_xor(core, p // 4)
            )
            starts.append(pl.multiple_of(block * KB, 8))

    sources = list(pieces) + [theirs_a_ref.at[i] for i in range(3)] + [theirs_b_ref]

    def one_row(a, carry):
        qrows = pl.ds(pl.multiple_of(a * KB, 8), KB)
        q = q_ref[qrows, :].astype(BF16).astype(F32)
        masked = [jnp.where(lane // 32 == h, q, 0.0) for h in range(HEADS)]
        masked.append(jnp.zeros((LANES - HEADS * KB, LANES), F32))
        masked = jnp.concatenate(masked, axis=0).astype(BF16)
        for p in range(8):
            source = sources[p]
            x_ref[p * 96 : (p + 1) * 96, :] = source[pl.ds(pl.multiple_of(a * 96, 32), 96), :]
        rows = x_ref[...]
        keys = jnp.dot(rows, wk, preferred_element_type=F32).astype(BF16)
        values_t = lax.dot_general(
            wvt, rows, (((1,), (1,)), ((), ())), preferred_element_type=F32
        ).astype(BF16)
        score = lax.dot_general(
            keys, masked, (((1,), (1,)), ((), ())), preferred_element_type=F32
        )
        top = jnp.full((KB, LANES), -jnp.inf, F32)
        for i in range(32):
            part = score[i * KB : (i + 1) * KB, :] + bias_ref[pl.ds(starts[i], KB), :]
            s_ref[i * KB : (i + 1) * KB, :] = part
            top = jnp.maximum(top, part)
        top = jnp.max(top, axis=0, keepdims=True)
        weights = jnp.exp(s_ref[...] - top)
        total = jnp.sum(weights, axis=0, keepdims=True)
        high = weights.astype(BF16)
        low = (weights - high.astype(F32)).astype(BF16)
        attended = jnp.dot(values_t, high, preferred_element_type=F32) + jnp.dot(
            values_t, low, preferred_element_type=F32
        )
        attended = (attended / total).T
        mine = jnp.zeros((KB, LANES), F32)
        for h in range(HEADS):
            mine = jnp.where(lane // 32 == h, attended[h * KB : (h + 1) * KB, :], mine)
        gated_ref[qrows, :] = gate_ref[qrows, :] * mine
        return carry

    lax.fori_loop(0, QROWS, one_row, 0)
    out_ref[...] = jnp.dot(
        gated_ref[...].astype(BF16), wo_ref[...], preferred_element_type=F32
    ).astype(BF16)


def permute_col(value, target):
    return lax.ppermute(value, "col", [(c, target(c)) for c in range(NCOL)])


def permute_all(value, target):
    pairs = []
    for r in range(NROW):
        for c in range(NCOL):
            r2, c2 = target(r, c)
            pairs.append((r * NCOL + c, r2 * NCOL + c2))
    return lax.ppermute(value, ("row", "col"), pairs)


GROUPS_Y = [[y * 8 + i for y in range(4)] for i in range(8)]


def near_x(mask):
    return lambda c: c ^ (mask * 2)


GROUPS_ROW_CORE = [
    [r * NCOL + 2 * q + e for r in range(NROW) for e in range(2)] for q in range(NCOL // 2)
]


def gather_x(value):
    first = permute_col(value, near_x(1))
    second = permute_col(value, near_x(3))
    third = permute_col(first, near_x(3))
    return [value, first, second, third]


def body(pair, ln_gain, w_query, w_keyval, w_gate, w_bias, w_out):
    rows = pair.reshape(-1, LANES)
    gain = ln_gain.reshape(1, LANES)
    nrows = QROWS * KB
    nq, tile = pl.pallas_call(
        front_kernel,
        in_specs=[whole(pl.ANY), whole(), whole()],
        out_specs=[whole()] * 2,
        out_shape=[
            jax.ShapeDtypeStruct((4, nrows, LANES), BF16),
            jax.ShapeDtypeStruct((2 * KB, LANES), F32),
        ],
        scratch_shapes=[VM((rows.shape[0], LANES), BF16), pltpu.SemaphoreType.DMA((3,))],
        name="front",
    )(rows, gain, w_bias.T)
    ys = lax.all_to_all(nq, "col", 0, 0, axis_index_groups=GROUPS_Y)
    tile = permute_all(tile, lambda r, c: (c // 2, 2 * r + c % 2))
    halves = jnp.broadcast_to(tile.reshape(1, 2, KB, LANES), (NROW, 2, KB, LANES))
    bias = lax.all_to_all(
        halves.reshape(2 * NROW, KB, LANES),
        ("row", "col"),
        0,
        0,
        axis_index_groups=GROUPS_ROW_CORE,
    )
    piece = pl.pallas_call(
        relay_kernel,
        in_specs=[whole(), whole(pl.ANY)],
        out_specs=whole(),
        out_shape=jax.ShapeDtypeStruct((4 * nrows, LANES), BF16),
        name="relay",
    )(ys, tile)
    mine = gather_x(piece)
    theirs_a = permute_col(jnp.stack(mine[:3]), lambda c: c ^ 1)
    theirs_b = permute_col(mine[3], lambda c: c ^ 1)
    out = pl.pallas_call(
        attend_kernel,
        in_specs=[whole()] * 12,
        out_specs=whole(),
        out_shape=jax.ShapeDtypeStruct((nrows, LANES), BF16),
        scratch_shapes=[
            VM((768, LANES), BF16),
            VM((768, LANES), F32),
            VM((nrows, LANES), F32),
            VM((nrows, LANES), F32),
            VM((nrows, LANES), F32),
        ],
        compiler_params=pltpu.CompilerParams(vmem_limit_bytes=32 * 1024 * 1024),
        name="attend",
    )(*mine, theirs_a, theirs_b, bias.reshape(-1, LANES), nq, w_query, w_keyval, w_gate, w_out)
    return out.reshape(QROWS, KB, LANES)


def solution(mesh):
    placed = (P("row", "col", None), P(), P(), P(), P(), P(), P())
    return jax.shard_map(
        body, mesh=mesh, in_specs=placed, out_specs=P("row", "col", None), check_vma=False
    )
```

```python
import jax
import jax.numpy as jnp
from jax import lax
from jax.experimental import pallas as pl
from jax.experimental.pallas import tpu as pltpu
from jax.sharding import PartitionSpec as P

QROWS = 8
KB = 24
HEADS = 4
LANES = 128
NROW = 16
NCOL = 32
F32 = jnp.float32
BF16 = jnp.bfloat16
VM = pltpu.VMEM


def whole():
    return pl.BlockSpec(memory_space=VM)


SEGMENTS = ((0, 0), (1, 0), (3, 0), (0, 1), (1, 1), (3, 1), (2, 0), (2, 1))


def norm_rows(block, gain):
    values = block.astype(F32)
    mean = jnp.mean(values, axis=-1, keepdims=True)
    centred = values - mean
    variance = jnp.mean(centred * centred, axis=-1, keepdims=True)
    return (centred * lax.rsqrt(variance + 1e-05) * gain).astype(BF16)


def front_kernel(rows_ref, gain_ref, wb_ref, nq_ref, tile_ref):
    wb = wb_ref[...].astype(F32)
    spread_t = [jnp.broadcast_to(wb[h : h + 1, :], (KB, LANES)) for h in range(HEADS)]
    spread_t.append(jnp.zeros((LANES - HEADS * KB, LANES), F32))
    spread_t = jnp.concatenate(spread_t, axis=0).astype(BF16)
    lane = lax.broadcasted_iota(jnp.int32, (KB, LANES), 1)
    place = jnp.where(lane < HEADS * KB, lax.rem(lane, KB), -1)
    gain = gain_ref[...]
    total = jnp.zeros((KB, LANES), F32)
    for begin in range(0, 2 * KB * KB, QROWS * KB):
        normed = norm_rows(rows_ref[begin : begin + QROWS * KB, :], gain)
        if begin == 0:
            for n in range(4):
                nq_ref[n] = normed
        wide = nt_dot(normed, spread_t)
        for n in range(QROWS):
            j = begin // KB + n
            total = jnp.where(place == j % KB, wide[n * KB : (n + 1) * KB, :], total)
            if j % KB == KB - 1:
                tile_ref[j + 1 - KB : j + 1, :] = total


def relay_kernel(ys_ref, tile_ref, out_ref, halves_ref):
    for half in range(2):
        part = tile_ref[half * KB : (half + 1) * KB, :]
        for r in range(NROW):
            halves_ref[2 * r + half] = part
    for a in range(QROWS):
        parts = [ys_ref[y, a * KB : (a + 1) * KB, :].astype(F32) for y in range(4)]
        out_ref[a * 96 : (a + 1) * 96, :] = jnp.concatenate(parts, axis=0).astype(BF16)


def nt_dot(left, right):
    return lax.dot_general(left, right, (((1,), (1,)), ((), ())), preferred_element_type=F32)


def twice(block):
    zero = jnp.zeros_like(block)
    top = jnp.concatenate([block, zero], axis=1)
    return jnp.concatenate([top, jnp.concatenate([zero, block], axis=1)], axis=0)


def prep_kernel(nq_ref, wq_ref, wkv_ref, wg_ref, qm_ref, gate_ref, wk_ref, wvt_ref):
    nq = nq_ref[0]
    query = jnp.dot(nq, wq_ref[...], preferred_element_type=F32) * (1.0 / 32**0.5)
    query = query.astype(BF16).astype(F32)
    gate_ref[...] = jax.nn.sigmoid(jnp.dot(nq, wg_ref[...], preferred_element_type=F32))
    wk_ref[...] = twice(wkv_ref[:, :LANES].astype(F32)).astype(BF16)
    wvt_ref[...] = twice(wkv_ref[:, LANES:].astype(F32).T).astype(BF16)
    lane = lax.broadcasted_iota(jnp.int32, (KB, LANES), 1)
    masked = []
    for a in range(QROWS):
        q = query[a * KB : (a + 1) * KB, :]
        parts = [jnp.where(lane // 32 == h, q, 0.0) for h in range(HEADS)]
        parts.append(jnp.zeros((LANES - HEADS * KB, LANES), F32))
        masked.append(jnp.concatenate(parts, axis=0))
    zero = jnp.zeros((LANES, LANES), F32)
    for i in range(QROWS // 2):
        top = jnp.concatenate([masked[2 * i], zero], axis=1)
        low = jnp.concatenate([zero, masked[2 * i + 1]], axis=1)
        qm_ref[i] = jnp.concatenate([top, low], axis=0).astype(BF16)


def score_pair(refs, i, qm_ref, wk_ref, wvt_ref):
    sides = []
    for a in (2 * i, 2 * i + 1):
        sides.append(jnp.concatenate([ref[a * 96 : (a + 1) * 96, :] for ref in refs], axis=0))
    rows = jnp.concatenate(sides, axis=1)
    keys = jnp.dot(rows, wk_ref[...], preferred_element_type=F32).astype(BF16)
    values_t = nt_dot(wvt_ref[...], rows).astype(BF16)
    return nt_dot(keys, qm_ref[i]), values_t


def early_theirs_kernel(three_ref, *refs):
    early_kernel(three_ref.at[0], three_ref.at[1], three_ref.at[2], *refs)


def early_kernel(a_ref, b_ref, c_ref, qm_ref, wk_ref, wvt_ref, s_ref, vt_ref):
    for i in range(QROWS // 2):
        score, values_t = score_pair((a_ref, b_ref, c_ref), i, qm_ref, wk_ref, wvt_ref)
        for n in range(2):
            s_ref[2 * i + n] = score[:, n * LANES : (n + 1) * LANES]
            vt_ref[2 * i + n] = values_t[n * LANES : (n + 1) * LANES, :]


def late_kernel(
    mine_ref, theirs_ref, bias_ref, s_mine_ref, vt_mine_ref, s_theirs_ref, vt_theirs_ref,
    qm_ref, gate_ref, wk_ref, wvt_ref, wo_ref, out_ref, order_ref, held_ref, gated_ref,
):
    col = lax.axis_index("col")
    core = lax.rem(col, 2)
    x = lax.rem(col // 2, 4)
    place = 0
    for mask, side in SEGMENTS:
        for y in range(4):
            block = y * 8 + lax.bitwise_xor(x, mask) * 2 + lax.bitwise_xor(core, side)
            start = pl.multiple_of(block * KB, 8)
            order_ref[place : place + KB, :] = bias_ref[pl.ds(start, KB), :]
            place += KB
    lane = lax.broadcasted_iota(jnp.int32, (KB, LANES), 1)
    for i in range(QROWS // 2):
        score, values_t = score_pair((mine_ref, theirs_ref), i, qm_ref, wk_ref, wvt_ref)
        for n in range(2):
            a = 2 * i + n
            parts = (
                s_mine_ref[a],
                s_theirs_ref[a],
                score[:, n * LANES : (n + 1) * LANES],
            )
            spans = ((0, 288), (288, 576), (576, 768))
            tops = []
            for part, (begin, end) in zip(parts, spans):
                full = part + order_ref[begin:end, :]
                held_ref[n, begin:end, :] = full
                tops.append(jnp.max(full, axis=0, keepdims=True))
            top = jnp.maximum(jnp.maximum(tops[0], tops[1]), tops[2])
            left = (vt_mine_ref[a], vt_theirs_ref[a], values_t[n * LANES : (n + 1) * LANES, :])
            total = jnp.zeros((1, LANES), F32)
            both = jnp.zeros((LANES, 2 * LANES), F32)
            for v, (begin, end) in zip(left, spans):
                weights = jnp.exp(held_ref[n, begin:end, :] - top)
                total = total + jnp.sum(weights, axis=0, keepdims=True)
                high = weights.astype(BF16)
                low = (weights - high.astype(F32)).astype(BF16)
                both = both + jnp.dot(
                    v, jnp.concatenate([high, low], axis=1), preferred_element_type=F32
                )
            attended = ((both[:, :LANES] + both[:, LANES:]) / total).T
            mine = jnp.zeros((KB, LANES), F32)
            for h in range(HEADS):
                mine = jnp.where(lane // 32 == h, attended[h * KB : (h + 1) * KB, :], mine)
            span = slice(a * KB, (a + 1) * KB)
            gated_ref[span, :] = gate_ref[span, :] * mine
    out_ref[...] = jnp.dot(
        gated_ref[...].astype(BF16), wo_ref[...], preferred_element_type=F32
    ).astype(BF16)


def call(kernel, name, inputs, outputs, scratch=(), micros=1.0):
    single = len(outputs) == 1
    return pl.pallas_call(
        kernel,
        in_specs=[whole()] * len(inputs),
        out_specs=whole() if single else [whole()] * len(outputs),
        out_shape=outputs[0] if single else list(outputs),
        scratch_shapes=list(scratch),
        compiler_params=pltpu.CompilerParams(vmem_limit_bytes=16 * 1024 * 1024),
        cost_estimate=pl.CostEstimate(
            flops=int(micros * 1e9), bytes_accessed=0, transcendentals=0
        ),
        name=name,
    )(*inputs)


def permute_col(value, target):
    return lax.ppermute(value, "col", [(c, target(c)) for c in range(NCOL)])


def permute_all(value, target):
    pairs = []
    for r in range(NROW):
        for c in range(NCOL):
            r2, c2 = target(r, c)
            pairs.append((r * NCOL + c, r2 * NCOL + c2))
    return lax.ppermute(value, ("row", "col"), pairs)


GROUPS_Y = [[y * 8 + i for y in range(4)] for i in range(8)]


def near_x(mask):
    return lambda c: c ^ (mask * 2)


GROUPS_ROW_CORE = [
    [r * NCOL + 2 * q + e for r in range(NROW) for e in range(2)] for q in range(NCOL // 2)
]


def gather_x(value):
    first = permute_col(value, near_x(1))
    second = permute_col(value, near_x(3))
    third = permute_col(first, near_x(3))
    return [value, first, second, third]


def body(pair, ln_gain, w_query, w_keyval, w_gate, w_bias, w_out):
    shape = jax.ShapeDtypeStruct
    rows = pair.reshape(-1, LANES)
    nrows = QROWS * KB
    nq, tile = call(
        front_kernel,
        "front",
        (rows, ln_gain.reshape(1, LANES), w_bias.T),
        (shape((4, nrows, LANES), BF16), shape((2 * KB, LANES), F32)),
        micros=2.0,
    )
    ys = lax.all_to_all(nq, "col", 0, 0, axis_index_groups=GROUPS_Y)
    tile = permute_all(tile, lambda r, c: (c // 2, 2 * r + c % 2))
    qm, gate, wk, wvt = call(
        prep_kernel,
        "prep",
        (nq, w_query, w_keyval, w_gate),
        (
            shape((QROWS // 2, 2 * LANES, 2 * LANES), BF16),
            shape((nrows, LANES), F32),
            shape((2 * LANES, 2 * LANES), BF16),
            shape((2 * LANES, 2 * LANES), BF16),
        ),
    )
    piece, halves = call(
        relay_kernel,
        "relay",
        (ys, tile),
        (shape((4 * nrows, LANES), BF16), shape((2 * NROW, KB, LANES), F32)),
    )
    bias = lax.all_to_all(halves, ("row", "col"), 0, 0, axis_index_groups=GROUPS_ROW_CORE)
    mine = gather_x(piece)
    theirs = permute_col(jnp.stack(mine[:3]), lambda c: c ^ 1)
    last = permute_col(mine[3], lambda c: c ^ 1)
    held = (shape((QROWS, 288, LANES), F32), shape((QROWS, LANES, 288), BF16))
    s_mine, vt_mine = call(
        early_kernel, "early_mine", (*mine[:3], qm, wk, wvt), held, micros=3.0
    )
    s_theirs, vt_theirs = call(
        early_theirs_kernel,
        "early_theirs",
        (theirs, qm, wk, wvt),
        held,
        micros=3.0,
    )
    out = call(
        late_kernel,
        "late",
        (
            mine[3], last, bias.reshape(-1, LANES), s_mine, vt_mine, s_theirs, vt_theirs,
            qm, gate, wk, wvt, w_out,
        ),
        (shape((nrows, LANES), BF16),),
        (VM((768, LANES), F32), VM((2, 768, LANES), F32), VM((nrows, LANES), F32)),
        micros=5.0,
    )
    return out.reshape(QROWS, KB, LANES)


def solution(mesh):
    placed = (P("row", "col", None), P(), P(), P(), P(), P(), P())
    return jax.shard_map(
        body, mesh=mesh, in_specs=placed, out_specs=P("row", "col", None), check_vma=False
    )
```

```python
import jax
import jax.numpy as jnp
from jax import lax
from jax.experimental import pallas as pl
from jax.experimental.pallas import tpu as pltpu
from jax.sharding import PartitionSpec as P

QROWS = 8
KB = 24
HEADS = 4
LANES = 128
NROW = 16
NCOL = 32
F32 = jnp.float32
BF16 = jnp.bfloat16
VM = pltpu.VMEM


def whole(space=VM):
    return pl.BlockSpec(memory_space=space)


MASKS = (0, 1, 3, 2)


def norm_rows(block, gain):
    values = block.astype(F32)
    mean = jnp.mean(values, axis=-1, keepdims=True)
    centred = values - mean
    variance = jnp.mean(centred * centred, axis=-1, keepdims=True)
    return (centred * lax.rsqrt(variance + 1e-05) * gain).astype(BF16)


CHUNKS = ((0, 192), (192, 576), (576, 1152))


def front_kernel(
    rows_ref, gain_ref, wb_ref, nq_ref, tile_ref, held_ref, gain_vm, wb_vm, nq_vm, sems, out_sems
):
    copies = []
    for i, (begin, end) in enumerate(CHUNKS):
        part = pl.ds(begin, end - begin)
        copies.append(pltpu.make_async_copy(rows_ref.at[part], held_ref.at[part], sems.at[i]))
    gain_copy = pltpu.make_async_copy(gain_ref, gain_vm, sems.at[3])
    wb_copy = pltpu.make_async_copy(wb_ref, wb_vm, sems.at[4])
    copies[0].start()
    gain_copy.start()
    wb_copy.start()
    copies[1].start()
    copies[2].start()
    lane = lax.broadcasted_iota(jnp.int32, (KB, LANES), 1)
    place = jnp.where(lane < HEADS * KB, lax.rem(lane, KB), -1)
    gain_copy.wait()
    gain = gain_vm[...]
    wb_copy.wait()
    wb = wb_vm[...].astype(F32)
    spread_t = [jnp.broadcast_to(wb[h : h + 1, :], (KB, LANES)) for h in range(HEADS)]
    spread_t.append(jnp.zeros((LANES - HEADS * KB, LANES), F32))
    spread_t = jnp.concatenate(spread_t, axis=0).astype(BF16)
    total = jnp.zeros((KB, LANES), F32)
    sends = []
    for i, (begin, end) in enumerate(CHUNKS):
        copies[i].wait()
        normed = norm_rows(held_ref[begin:end, :], gain)
        if i == 0:
            nq_vm[...] = normed
            for n in range(4):
                send = pltpu.make_async_copy(nq_vm, nq_ref.at[n], out_sems.at[n])
                send.start()
                sends.append(send)
        wide = nt_dot(normed, spread_t)
        for j in range(begin // KB, end // KB):
            row = j * KB - begin
            total = jnp.where(place == j % KB, wide[row : row + KB, :], total)
            if j % KB == KB - 1:
                tile_ref[j + 1 - KB : j + 1, :] = total
    for send in sends:
        send.wait()


def relay_kernel(ys_ref, tile_ref, out_ref, halves_ref):
    for half in range(2):
        part = tile_ref[half * KB : (half + 1) * KB, :]
        for r in range(NROW):
            halves_ref[2 * r + half] = part
    for a in range(QROWS):
        parts = [ys_ref[y, a * KB : (a + 1) * KB, :].astype(F32) for y in range(4)]
        out_ref[a * 96 : (a + 1) * 96, :] = jnp.concatenate(parts, axis=0).astype(BF16)


def nt_dot(left, right):
    return lax.dot_general(left, right, (((1,), (1,)), ((), ())), preferred_element_type=F32)


def twice(block):
    zero = jnp.zeros_like(block)
    top = jnp.concatenate([block, zero], axis=1)
    return jnp.concatenate([top, jnp.concatenate([zero, block], axis=1)], axis=0)


def attend_kernel(
    own_ref, first_ref, second_ref, third_ref, theirs_a_ref, theirs_b_ref, bias_ref,
    nq_ref, wq_ref, wkv_ref, wg_ref, wo_ref,
    out_ref, order_ref, held_ref, gate_ref, gated_ref,
):
    col = lax.axis_index("col")
    core = lax.rem(col, 2)
    x = lax.rem(col // 2, 4)
    sources = (
        own_ref, first_ref, second_ref, third_ref,
        theirs_a_ref.at[0], theirs_a_ref.at[1], theirs_b_ref.at[0], theirs_b_ref.at[1],
    )
    place = 0
    for side in range(2):
        for mask in MASKS:
            for y in range(4):
                block = y * 8 + lax.bitwise_xor(x, mask) * 2 + lax.bitwise_xor(core, side)
                start = pl.multiple_of(block * KB, 8)
                order_ref[place : place + KB, :] = bias_ref[pl.ds(start, KB), :]
                place += KB
    nq = nq_ref[0]
    query = jnp.dot(nq, wq_ref[...], preferred_element_type=F32) * (1.0 / 32**0.5)
    query = query.astype(BF16).astype(F32)
    gate_ref[...] = jax.nn.sigmoid(jnp.dot(nq, wg_ref[...], preferred_element_type=F32))
    wk = twice(wkv_ref[:, :LANES].astype(F32)).astype(BF16)
    wvt = twice(wkv_ref[:, LANES:].astype(F32).T).astype(BF16)
    lane = lax.broadcasted_iota(jnp.int32, (KB, LANES), 1)
    zero = jnp.zeros((LANES, LANES), F32)
    for i in range(QROWS // 2):
        sides = []
        masked = []
        for a in (2 * i, 2 * i + 1):
            sides.append(
                jnp.concatenate([ref[a * 96 : (a + 1) * 96, :] for ref in sources], axis=0)
            )
            q = query[a * KB : (a + 1) * KB, :]
            parts = [jnp.where(lane // 32 == h, q, 0.0) for h in range(HEADS)]
            parts.append(jnp.zeros((LANES - HEADS * KB, LANES), F32))
            masked.append(jnp.concatenate(parts, axis=0))
        queries = jnp.concatenate(
            [
                jnp.concatenate([masked[0], zero], axis=1),
                jnp.concatenate([zero, masked[1]], axis=1),
            ],
            axis=0,
        ).astype(BF16)
        rows = jnp.concatenate(sides, axis=1)
        keys = jnp.dot(rows, wk, preferred_element_type=F32).astype(BF16)
        values_t = nt_dot(wvt, rows).astype(BF16)
        score = nt_dot(keys, queries)
        for n in range(2):
            a = 2 * i + n
            full = score[:, n * LANES : (n + 1) * LANES] + order_ref[...]
            held_ref[a % 4] = full
            top = jnp.max(full, axis=0, keepdims=True)
            weights = jnp.exp(held_ref[a % 4] - top)
            total = jnp.sum(weights, axis=0, keepdims=True)
            high = weights.astype(BF16)
            low = (weights - high.astype(F32)).astype(BF16)
            both = jnp.dot(
                values_t[n * LANES : (n + 1) * LANES, :],
                jnp.concatenate([high, low], axis=1),
                preferred_element_type=F32,
            )
            attended = ((both[:, :LANES] + both[:, LANES:]) / total).T
            mine = jnp.zeros((KB, LANES), F32)
            for h in range(HEADS):
                mine = jnp.where(lane // 32 == h, attended[h * KB : (h + 1) * KB, :], mine)
            span = slice(a * KB, (a + 1) * KB)
            gated_ref[span, :] = gate_ref[span, :] * mine
    out_ref[...] = jnp.dot(
        gated_ref[...].astype(BF16), wo_ref[...], preferred_element_type=F32
    ).astype(BF16)


def permute_col(value, target):
    return lax.ppermute(value, "col", [(c, target(c)) for c in range(NCOL)])


def permute_all(value, target):
    pairs = []
    for r in range(NROW):
        for c in range(NCOL):
            r2, c2 = target(r, c)
            pairs.append((r * NCOL + c, r2 * NCOL + c2))
    return lax.ppermute(value, ("row", "col"), pairs)


GROUPS_Y = [[y * 8 + i for y in range(4)] for i in range(8)]


def near_x(mask):
    return lambda c: c ^ (mask * 2)


GROUPS_ROW_CORE = [
    [r * NCOL + 2 * q + e for r in range(NROW) for e in range(2)] for q in range(NCOL // 2)
]


def gather_x(value):
    first = permute_col(value, near_x(1))
    second = permute_col(value, near_x(3))
    third = permute_col(first, near_x(3))
    return [value, first, second, third]


def body(pair, ln_gain, w_query, w_keyval, w_gate, w_bias, w_out):
    shape = jax.ShapeDtypeStruct
    rows = pair.reshape(-1, LANES)
    nrows = QROWS * KB
    nq, tile = pl.pallas_call(
        front_kernel,
        in_specs=[whole(pl.ANY)] * 3,
        out_specs=[whole(pl.ANY), whole()],
        out_shape=[shape((4, nrows, LANES), BF16), shape((2 * KB, LANES), F32)],
        scratch_shapes=[
            VM(rows.shape, BF16),
            VM((1, LANES), F32),
            VM((HEADS, LANES), BF16),
            VM((nrows, LANES), BF16),
            pltpu.SemaphoreType.DMA((5,)),
            pltpu.SemaphoreType.DMA((4,)),
        ],
        name="front",
    )(rows, ln_gain.reshape(1, LANES), w_bias.T)
    ys = lax.all_to_all(nq, "col", 0, 0, axis_index_groups=GROUPS_Y)
    tile = permute_all(tile, lambda r, c: (c // 2, 2 * r + c % 2))
    piece, halves = pl.pallas_call(
        relay_kernel,
        in_specs=[whole()] * 2,
        out_specs=[whole()] * 2,
        out_shape=[shape((4 * nrows, LANES), BF16), shape((2 * NROW, KB, LANES), F32)],
        compiler_params=pltpu.CompilerParams(vmem_limit_bytes=16 * 1024 * 1024),
        name="relay",
    )(ys, tile)
    bias = lax.all_to_all(halves, ("row", "col"), 0, 0, axis_index_groups=GROUPS_ROW_CORE)
    mine = gather_x(piece)
    theirs = [permute_col(jnp.stack(mine[i : i + 2]), lambda c: c ^ 1) for i in (0, 2)]
    out = pl.pallas_call(
        attend_kernel,
        in_specs=[whole()] * 12,
        out_specs=whole(),
        out_shape=shape((nrows, LANES), BF16),
        scratch_shapes=[
            VM((768, LANES), F32),
            VM((4, 768, LANES), F32),
            VM((nrows, LANES), F32),
            VM((nrows, LANES), F32),
        ],
        compiler_params=pltpu.CompilerParams(vmem_limit_bytes=32 * 1024 * 1024),
        name="attend",
    )(*mine, *theirs, bias.reshape(-1, LANES), nq, w_query, w_keyval, w_gate, w_out)
    return out.reshape(QROWS, KB, LANES)


def solution(mesh):
    placed = (P("row", "col", None), P(), P(), P(), P(), P(), P())
    return jax.shard_map(
        body, mesh=mesh, in_specs=placed, out_specs=P("row", "col", None), check_vma=False
    )
```

```python
import jax
import jax.numpy as jnp
from jax import lax
from jax.experimental import pallas as pl
from jax.experimental.pallas import tpu as pltpu
from jax.sharding import PartitionSpec as P

QROWS = 8
KB = 24
HEADS = 4
LANES = 128
NROW = 16
N_RES = 768
NCOL = 32
F32 = jnp.float32
BF16 = jnp.bfloat16
VM = pltpu.VMEM


def whole(space=VM):
    return pl.BlockSpec(memory_space=space)


MASKS = (0, 1, 3, 2)


def norm_rows(block, gain):
    values = block.astype(F32)
    mean = jnp.mean(values, axis=-1, keepdims=True)
    centred = values - mean
    variance = jnp.mean(centred * centred, axis=-1, keepdims=True)
    return (centred * lax.rsqrt(variance + 1e-05) * gain).astype(BF16)


CHUNKS = ((0, 192), (192, 576), (576, 1152))


def front_kernel(
    rows_ref, gain_ref, wb_ref, nq_ref, tile_ref, held_ref, gain_vm, wb_vm, nq_vm, sems, out_sems
):
    copies = []
    for i, (begin, end) in enumerate(CHUNKS):
        part = pl.ds(begin, end - begin)
        copies.append(pltpu.make_async_copy(rows_ref.at[part], held_ref.at[part], sems.at[i]))
    gain_copy = pltpu.make_async_copy(gain_ref, gain_vm, sems.at[3])
    wb_copy = pltpu.make_async_copy(wb_ref, wb_vm, sems.at[4])
    copies[0].start()
    gain_copy.start()
    wb_copy.start()
    copies[1].start()
    copies[2].start()
    lane = lax.broadcasted_iota(jnp.int32, (KB, LANES), 1)
    place = jnp.where(lane < HEADS * KB, lax.rem(lane, KB), -1)
    gain_copy.wait()
    gain = gain_vm[...]
    wb_copy.wait()
    wb = wb_vm[...].astype(F32)
    spread_t = [jnp.broadcast_to(wb[h : h + 1, :], (KB, LANES)) for h in range(HEADS)]
    spread_t.append(jnp.zeros((LANES - HEADS * KB, LANES), F32))
    spread_t = jnp.concatenate(spread_t, axis=0).astype(BF16)
    total = jnp.zeros((KB, LANES), F32)
    sends = []
    for i, (begin, end) in enumerate(CHUNKS):
        copies[i].wait()
        normed = norm_rows(held_ref[begin:end, :], gain)
        if i == 0:
            nq_vm[...] = normed
            for n in range(4):
                send = pltpu.make_async_copy(nq_vm, nq_ref.at[n], out_sems.at[n])
                send.start()
                sends.append(send)
        wide = nt_dot(normed, spread_t)
        for j in range(begin // KB, end // KB):
            row = j * KB - begin
            total = jnp.where(place == j % KB, wide[row : row + KB, :], total)
            if j % KB == KB - 1:
                tile_ref[j + 1 - KB : j + 1, :] = total
    for send in sends:
        send.wait()


def copies_kernel(tile_ref, halves_ref):
    for half in range(2):
        part = tile_ref[half * KB : (half + 1) * KB, :]
        for r in range(NROW):
            halves_ref[2 * r + half] = part


def relay_kernel(ys_ref, out_ref):
    for a in range(QROWS):
        parts = [ys_ref[y, a * KB : (a + 1) * KB, :].astype(F32) for y in range(4)]
        out_ref[a * 96 : (a + 1) * 96, :] = jnp.concatenate(parts, axis=0).astype(BF16)


def join_kernel(second_ref, third_ref, bias_ref, pair_ref, order_ref):
    pair_ref[0] = second_ref[...]
    pair_ref[1] = third_ref[...]
    col = lax.axis_index("col")
    core = lax.rem(col, 2)
    x = lax.rem(col // 2, 4)
    place = 0
    for side in range(2):
        for mask in MASKS:
            for y in range(4):
                block = y * 8 + lax.bitwise_xor(x, mask) * 2 + lax.bitwise_xor(core, side)
                start = pl.multiple_of(block * KB, 8)
                order_ref[place : place + KB, :] = bias_ref[pl.ds(start, KB), :]
                place += KB


def nt_dot(left, right):
    return lax.dot_general(left, right, (((1,), (1,)), ((), ())), preferred_element_type=F32)


def twice(block):
    zero = jnp.zeros_like(block)
    top = jnp.concatenate([block, zero], axis=1)
    return jnp.concatenate([top, jnp.concatenate([zero, block], axis=1)], axis=0)


def attend_kernel(
    own_ref, first_ref, second_ref, third_ref, theirs_a_ref, theirs_b_ref, order_ref,
    nq_ref, wq_ref, wkv_ref, wg_ref, wo_ref,
    out_ref, held_ref, gate_ref, gated_ref,
):
    sources = (
        own_ref, first_ref, second_ref, third_ref,
        theirs_a_ref.at[0], theirs_a_ref.at[1], theirs_b_ref.at[0], theirs_b_ref.at[1],
    )
    nq = nq_ref[0]
    query = jnp.dot(nq, wq_ref[...], preferred_element_type=F32) * (1.0 / 32**0.5)
    query = query.astype(BF16).astype(F32)
    gate_ref[...] = jax.nn.sigmoid(jnp.dot(nq, wg_ref[...], preferred_element_type=F32))
    wk = twice(wkv_ref[:, :LANES].astype(F32)).astype(BF16)
    wvt = twice(wkv_ref[:, LANES:].astype(F32).T).astype(BF16)
    lane = lax.broadcasted_iota(jnp.int32, (KB, LANES), 1)
    zero = jnp.zeros((LANES, LANES), F32)
    for i in range(QROWS // 2):
        sides = []
        masked = []
        for a in (2 * i, 2 * i + 1):
            sides.append(
                jnp.concatenate([ref[a * 96 : (a + 1) * 96, :] for ref in sources], axis=0)
            )
            q = query[a * KB : (a + 1) * KB, :]
            parts = [jnp.where(lane // 32 == h, q, 0.0) for h in range(HEADS)]
            parts.append(jnp.zeros((LANES - HEADS * KB, LANES), F32))
            masked.append(jnp.concatenate(parts, axis=0))
        queries = jnp.concatenate(
            [
                jnp.concatenate([masked[0], zero], axis=1),
                jnp.concatenate([zero, masked[1]], axis=1),
            ],
            axis=0,
        ).astype(BF16)
        rows = jnp.concatenate(sides, axis=1)
        keys = jnp.dot(rows, wk, preferred_element_type=F32).astype(BF16)
        values_t = nt_dot(wvt, rows).astype(BF16)
        score = nt_dot(keys, queries)
        for n in range(2):
            a = 2 * i + n
            full = score[:, n * LANES : (n + 1) * LANES] + order_ref[...]
            held_ref[a % 4] = full
            top = jnp.max(full, axis=0, keepdims=True)
            weights = jnp.exp(held_ref[a % 4] - top)
            total = jnp.sum(weights, axis=0, keepdims=True)
            high = weights.astype(BF16)
            low = (weights - high.astype(F32)).astype(BF16)
            both = jnp.dot(
                values_t[n * LANES : (n + 1) * LANES, :],
                jnp.concatenate([high, low], axis=1),
                preferred_element_type=F32,
            )
            attended = ((both[:, :LANES] + both[:, LANES:]) / total).T
            mine = jnp.zeros((KB, LANES), F32)
            for h in range(HEADS):
                mine = jnp.where(lane // 32 == h, attended[h * KB : (h + 1) * KB, :], mine)
            span = slice(a * KB, (a + 1) * KB)
            gated_ref[span, :] = gate_ref[span, :] * mine
    out_ref[...] = jnp.dot(
        gated_ref[...].astype(BF16), wo_ref[...], preferred_element_type=F32
    ).astype(BF16)


def permute_col(value, target):
    return lax.ppermute(value, "col", [(c, target(c)) for c in range(NCOL)])


def permute_all(value, target):
    pairs = []
    for r in range(NROW):
        for c in range(NCOL):
            r2, c2 = target(r, c)
            pairs.append((r * NCOL + c, r2 * NCOL + c2))
    return lax.ppermute(value, ("row", "col"), pairs)


GROUPS_Y = [[y * 8 + i for y in range(4)] for i in range(8)]


def near_x(mask):
    return lambda c: c ^ (mask * 2)


GROUPS_ROW_CORE = [
    [r * NCOL + 2 * q + e for r in range(NROW) for e in range(2)] for q in range(NCOL // 2)
]


def gather_x(value):
    first = permute_col(value, near_x(1))
    second = permute_col(value, near_x(3))
    third = permute_col(first, near_x(3))
    return [value, first, second, third]


def body(pair, ln_gain, w_query, w_keyval, w_gate, w_bias, w_out):
    shape = jax.ShapeDtypeStruct
    rows = pair.reshape(-1, LANES)
    nrows = QROWS * KB
    nq, tile = pl.pallas_call(
        front_kernel,
        in_specs=[whole(pl.ANY)] * 3,
        out_specs=[whole(pl.ANY), whole()],
        out_shape=[shape((4, nrows, LANES), BF16), shape((2 * KB, LANES), F32)],
        scratch_shapes=[
            VM(rows.shape, BF16),
            VM((1, LANES), F32),
            VM((HEADS, LANES), BF16),
            VM((nrows, LANES), BF16),
            pltpu.SemaphoreType.DMA((5,)),
            pltpu.SemaphoreType.DMA((4,)),
        ],
        name="front",
    )(rows, ln_gain.reshape(1, LANES), w_bias.T)
    ys = lax.all_to_all(nq, "col", 0, 0, axis_index_groups=GROUPS_Y)
    tile = permute_all(tile, lambda r, c: (c // 2, 2 * r + c % 2))
    small = pltpu.CompilerParams(vmem_limit_bytes=16 * 1024 * 1024)
    halves = pl.pallas_call(
        copies_kernel,
        in_specs=[whole()],
        out_specs=whole(),
        out_shape=shape((2 * NROW, KB, LANES), F32),
        compiler_params=small,
        name="copies",
    )(tile)
    bias = lax.all_to_all(halves, ("row", "col"), 0, 0, axis_index_groups=GROUPS_ROW_CORE)
    piece = pl.pallas_call(
        relay_kernel,
        in_specs=[whole()],
        out_specs=whole(),
        out_shape=shape((4 * nrows, LANES), BF16),
        compiler_params=small,
        name="relay",
    )(ys)
    mine = gather_x(piece)
    joined, order = pl.pallas_call(
        join_kernel,
        in_specs=[whole()] * 3,
        out_specs=[whole()] * 2,
        out_shape=[shape((2, 4 * nrows, LANES), BF16), shape((N_RES, LANES), F32)],
        compiler_params=small,
        name="join",
    )(mine[2], mine[3], bias.reshape(-1, LANES))
    theirs = [permute_col(both, lambda c: c ^ 1) for both in (jnp.stack(mine[:2]), joined)]
    out = pl.pallas_call(
        attend_kernel,
        in_specs=[whole()] * 12,
        out_specs=whole(),
        out_shape=shape((nrows, LANES), BF16),
        scratch_shapes=[
            VM((4, 768, LANES), F32),
            VM((nrows, LANES), F32),
            VM((nrows, LANES), F32),
        ],
        compiler_params=pltpu.CompilerParams(vmem_limit_bytes=32 * 1024 * 1024),
        name="attend",
    )(*mine, *theirs, order, nq, w_query, w_keyval, w_gate, w_out)
    return out.reshape(QROWS, KB, LANES)


def solution(mesh):
    placed = (P("row", "col", None), P(), P(), P(), P(), P(), P())
    return jax.shard_map(
        body, mesh=mesh, in_specs=placed, out_specs=P("row", "col", None), check_vma=False
    )
```

```python
import jax
import jax.numpy as jnp
from jax import lax
from jax.experimental import pallas as pl
from jax.experimental.pallas import tpu as pltpu
from jax.sharding import PartitionSpec as P

QROWS = 8
KB = 24
HEADS = 4
LANES = 128
NROW = 16
N_RES = 768
NCOL = 32
F32 = jnp.float32
BF16 = jnp.bfloat16
VM = pltpu.VMEM


def whole(space=VM):
    return pl.BlockSpec(memory_space=space)


MASKS = (0, 1, 3, 2)


def norm_rows(block, gain):
    values = block.astype(F32)
    mean = jnp.mean(values, axis=-1, keepdims=True)
    centred = values - mean
    variance = jnp.mean(centred * centred, axis=-1, keepdims=True)
    return (centred * lax.rsqrt(variance + 1e-05) * gain).astype(BF16)


def query_kernel(rows_ref, gain_ref, nq_ref, held_ref, gain_vm, nq_vm, sems, out_sems):
    part = pl.ds(0, QROWS * KB)
    rows_copy = pltpu.make_async_copy(rows_ref.at[part], held_ref, sems.at[0])
    gain_copy = pltpu.make_async_copy(gain_ref, gain_vm, sems.at[1])
    rows_copy.start()
    gain_copy.start()
    gain_copy.wait()
    rows_copy.wait()
    nq_vm[...] = norm_rows(held_ref[...], gain_vm[...])
    sends = []
    for n in range(4):
        send = pltpu.make_async_copy(nq_vm, nq_ref.at[n], out_sems.at[n])
        send.start()
        sends.append(send)
    for send in sends:
        send.wait()


CHUNKS = ((0, 384), (384, 768), (768, 1152))


def bias_kernel(rows_ref, gain_ref, wb_ref, tile_ref, held_ref, gain_vm, wb_vm, sems):
    copies = []
    for i, (begin, end) in enumerate(CHUNKS):
        part = pl.ds(begin, end - begin)
        copies.append(pltpu.make_async_copy(rows_ref.at[part], held_ref.at[part], sems.at[i]))
    gain_copy = pltpu.make_async_copy(gain_ref, gain_vm, sems.at[3])
    wb_copy = pltpu.make_async_copy(wb_ref, wb_vm, sems.at[4])
    for copy in (copies[0], gain_copy, wb_copy, copies[1], copies[2]):
        copy.start()
    lane = lax.broadcasted_iota(jnp.int32, (KB, LANES), 1)
    place = jnp.where(lane < HEADS * KB, lax.rem(lane, KB), -1)
    gain_copy.wait()
    gain = gain_vm[...]
    wb_copy.wait()
    wb = wb_vm[...].astype(F32)
    spread_t = [jnp.broadcast_to(wb[h : h + 1, :], (KB, LANES)) for h in range(HEADS)]
    spread_t.append(jnp.zeros((LANES - HEADS * KB, LANES), F32))
    spread_t = jnp.concatenate(spread_t, axis=0).astype(BF16)
    total = jnp.zeros((KB, LANES), F32)
    for i, (begin, end) in enumerate(CHUNKS):
        copies[i].wait()
        wide = nt_dot(norm_rows(held_ref[begin:end, :], gain), spread_t)
        for j in range(begin // KB, end // KB):
            row = j * KB - begin
            total = jnp.where(place == j % KB, wide[row : row + KB, :], total)
            if j % KB == KB - 1:
                tile_ref[j + 1 - KB : j + 1, :] = total


def copies_kernel(tile_ref, halves_ref):
    for half in range(2):
        part = tile_ref[half * KB : (half + 1) * KB, :]
        for r in range(NROW):
            halves_ref[2 * r + half] = part


def relay_kernel(ys_ref, out_ref):
    for a in range(QROWS):
        parts = [ys_ref[y, a * KB : (a + 1) * KB, :].astype(F32) for y in range(4)]
        out_ref[a * 96 : (a + 1) * 96, :] = jnp.concatenate(parts, axis=0).astype(BF16)


def holder(r, y, x):
    z = lax.rem(r // 2 + 2 * (x - lax.rem(r, 4)) + y // 2 + 8, 8)
    return z * 2 + lax.rem(y + r, 2)


def join_kernel(second_ref, third_ref, bias_ref, pair_ref, order_ref):
    pair_ref[0] = second_ref[...]
    pair_ref[1] = third_ref[...]
    col = lax.axis_index("col")
    core = lax.rem(col, 2)
    x = lax.rem(col // 2, 4)
    held_row = col // 2
    place = 0
    for side in range(2):
        for mask in MASKS:
            for y in range(4):
                spot = holder(held_row, y, lax.bitwise_xor(x, mask)) * 2
                start = pl.multiple_of((spot + lax.bitwise_xor(core, side)) * KB, 8)
                order_ref[place : place + KB, :] = bias_ref[pl.ds(start, KB), :]
                place += KB


def nt_dot(left, right):
    return lax.dot_general(left, right, (((1,), (1,)), ((), ())), preferred_element_type=F32)


def twice(block):
    zero = jnp.zeros_like(block)
    top = jnp.concatenate([block, zero], axis=1)
    return jnp.concatenate([top, jnp.concatenate([zero, block], axis=1)], axis=0)


def attend_kernel(
    own_ref, first_ref, second_ref, third_ref, theirs_a_ref, theirs_b_ref, order_ref,
    nq_ref, wq_ref, wkv_ref, wg_ref, wo_ref,
    out_ref, held_ref, gate_ref, gated_ref,
):
    sources = (
        own_ref, first_ref, second_ref, third_ref,
        theirs_a_ref.at[0], theirs_a_ref.at[1], theirs_b_ref.at[0], theirs_b_ref.at[1],
    )
    nq = nq_ref[0]
    query = jnp.dot(nq, wq_ref[...], preferred_element_type=F32) * (1.0 / 32**0.5)
    query = query.astype(BF16).astype(F32)
    gate_ref[...] = jax.nn.sigmoid(jnp.dot(nq, wg_ref[...], preferred_element_type=F32))
    wk = twice(wkv_ref[:, :LANES].astype(F32)).astype(BF16)
    wvt = twice(wkv_ref[:, LANES:].astype(F32).T).astype(BF16)
    lane = lax.broadcasted_iota(jnp.int32, (KB, LANES), 1)
    zero = jnp.zeros((LANES, LANES), F32)
    for i in range(QROWS // 2):
        sides = []
        masked = []
        for a in (2 * i, 2 * i + 1):
            sides.append(
                jnp.concatenate([ref[a * 96 : (a + 1) * 96, :] for ref in sources], axis=0)
            )
            q = query[a * KB : (a + 1) * KB, :]
            parts = [jnp.where(lane // 32 == h, q, 0.0) for h in range(HEADS)]
            parts.append(jnp.zeros((LANES - HEADS * KB, LANES), F32))
            masked.append(jnp.concatenate(parts, axis=0))
        queries = jnp.concatenate(
            [
                jnp.concatenate([masked[0], zero], axis=1),
                jnp.concatenate([zero, masked[1]], axis=1),
            ],
            axis=0,
        ).astype(BF16)
        rows = jnp.concatenate(sides, axis=1)
        keys = jnp.dot(rows, wk, preferred_element_type=F32).astype(BF16)
        values_t = nt_dot(wvt, rows).astype(BF16)
        score = nt_dot(keys, queries)
        for n in range(2):
            a = 2 * i + n
            full = score[:, n * LANES : (n + 1) * LANES] + order_ref[...]
            held_ref[a % 4] = full
            top = jnp.max(full, axis=0, keepdims=True)
            weights = jnp.exp(held_ref[a % 4] - top)
            total = jnp.sum(weights, axis=0, keepdims=True)
            high = weights.astype(BF16)
            low = (weights - high.astype(F32)).astype(BF16)
            both = jnp.dot(
                values_t[n * LANES : (n + 1) * LANES, :],
                jnp.concatenate([high, low], axis=1),
                preferred_element_type=F32,
            )
            attended = ((both[:, :LANES] + both[:, LANES:]) / total).T
            mine = jnp.zeros((KB, LANES), F32)
            for h in range(HEADS):
                mine = jnp.where(lane // 32 == h, attended[h * KB : (h + 1) * KB, :], mine)
            span = slice(a * KB, (a + 1) * KB)
            gated_ref[span, :] = gate_ref[span, :] * mine
    out_ref[...] = jnp.dot(
        gated_ref[...].astype(BF16), wo_ref[...], preferred_element_type=F32
    ).astype(BF16)


def permute_col(value, target):
    return lax.ppermute(value, "col", [(c, target(c)) for c in range(NCOL)])


def permute_all(value, target):
    pairs = []
    for r in range(NROW):
        for c in range(NCOL):
            r2, c2 = target(r, c)
            pairs.append((r * NCOL + c, r2 * NCOL + c2))
    return lax.ppermute(value, ("row", "col"), pairs)


GROUPS_Y = [[y * 8 + i for y in range(4)] for i in range(8)]


def holder_of(r, c):
    y, x = c // 8, c // 2 % 4
    z = (r // 2 + 2 * (x - r % 4) + y // 2) % 8
    return z * 2 + (y + r) % 2, 2 * r + c % 2


def near_x(mask):
    return lambda c: c ^ (mask * 2)


GROUPS_ROW_CORE = [
    [r * NCOL + 2 * q + e for r in range(NROW) for e in range(2)] for q in range(NCOL // 2)
]


def gather_x(value):
    first = permute_col(value, near_x(1))
    second = permute_col(value, near_x(3))
    third = permute_col(first, near_x(3))
    return [value, first, second, third]


def body(pair, ln_gain, w_query, w_keyval, w_gate, w_bias, w_out):
    shape = jax.ShapeDtypeStruct
    rows = pair.reshape(-1, LANES)
    nrows = QROWS * KB
    gain = ln_gain.reshape(1, LANES)
    nq = pl.pallas_call(
        query_kernel,
        in_specs=[whole(pl.ANY)] * 2,
        out_specs=whole(pl.ANY),
        out_shape=shape((4, nrows, LANES), BF16),
        scratch_shapes=[
            VM((nrows, LANES), BF16),
            VM((1, LANES), F32),
            VM((nrows, LANES), BF16),
            pltpu.SemaphoreType.DMA((2,)),
            pltpu.SemaphoreType.DMA((4,)),
        ],
        name="query_norm",
    )(rows, gain)
    ys = lax.all_to_all(nq, "col", 0, 0, axis_index_groups=GROUPS_Y)
    tile = pl.pallas_call(
        bias_kernel,
        in_specs=[whole(pl.ANY)] * 3,
        out_specs=whole(),
        out_shape=shape((2 * KB, LANES), F32),
        scratch_shapes=[
            VM(rows.shape, BF16),
            VM((1, LANES), F32),
            VM((HEADS, LANES), BF16),
            pltpu.SemaphoreType.DMA((5,)),
        ],
        name="bias_tile",
    )(rows, gain, w_bias.T)
    tile = permute_all(tile, holder_of)
    small = pltpu.CompilerParams(vmem_limit_bytes=16 * 1024 * 1024)
    halves = pl.pallas_call(
        copies_kernel,
        in_specs=[whole()],
        out_specs=whole(),
        out_shape=shape((2 * NROW, KB, LANES), F32),
        compiler_params=small,
        name="copies",
    )(tile)
    bias = lax.all_to_all(halves, ("row", "col"), 0, 0, axis_index_groups=GROUPS_ROW_CORE)
    piece = pl.pallas_call(
        relay_kernel,
        in_specs=[whole()],
        out_specs=whole(),
        out_shape=shape((4 * nrows, LANES), BF16),
        compiler_params=small,
        name="relay",
    )(ys)
    mine = gather_x(piece)
    joined, order = pl.pallas_call(
        join_kernel,
        in_specs=[whole()] * 3,
        out_specs=[whole()] * 2,
        out_shape=[shape((2, 4 * nrows, LANES), BF16), shape((N_RES, LANES), F32)],
        compiler_params=small,
        name="join",
    )(mine[2], mine[3], bias.reshape(-1, LANES))
    theirs = [permute_col(both, lambda c: c ^ 1) for both in (jnp.stack(mine[:2]), joined)]
    out = pl.pallas_call(
        attend_kernel,
        in_specs=[whole()] * 12,
        out_specs=whole(),
        out_shape=shape((nrows, LANES), BF16),
        scratch_shapes=[
            VM((4, 768, LANES), F32),
            VM((nrows, LANES), F32),
            VM((nrows, LANES), F32),
        ],
        compiler_params=pltpu.CompilerParams(vmem_limit_bytes=32 * 1024 * 1024),
        name="attend",
    )(*mine, *theirs, order, nq, w_query, w_keyval, w_gate, w_out)
    return out.reshape(QROWS, KB, LANES)


def solution(mesh):
    placed = (P("row", "col", None), P(), P(), P(), P(), P(), P())
    return jax.shard_map(
        body, mesh=mesh, in_specs=placed, out_specs=P("row", "col", None), check_vma=False
    )
```

```python
import jax
import jax.numpy as jnp
from jax import lax
from jax.experimental import pallas as pl
from jax.experimental.pallas import tpu as pltpu
from jax.sharding import PartitionSpec as P

QROWS = 8
KB = 24
HEADS = 4
LANES = 128
NROW = 16
N_RES = 768
NCOL = 32
F32 = jnp.float32
BF16 = jnp.bfloat16
VM = pltpu.VMEM


def whole(space=VM):
    return pl.BlockSpec(memory_space=space)


MASKS = (0, 1, 3, 2)


def norm_rows(block, gain):
    values = block.astype(F32)
    mean = jnp.mean(values, axis=-1, keepdims=True)
    centred = values - mean
    variance = jnp.mean(centred * centred, axis=-1, keepdims=True)
    return (centred * lax.rsqrt(variance + 1e-05) * gain).astype(BF16)


CHUNKS = ((0, 192), (192, 576), (576, 1152))


def front_kernel(
    rows_ref, gain_ref, wb_ref, nq_ref, tile_ref, held_ref, gain_vm, wb_vm, nq_vm, sems, out_sems
):
    copies = []
    for i, (begin, end) in enumerate(CHUNKS):
        part = pl.ds(begin, end - begin)
        copies.append(pltpu.make_async_copy(rows_ref.at[part], held_ref.at[part], sems.at[i]))
    gain_copy = pltpu.make_async_copy(gain_ref, gain_vm, sems.at[3])
    wb_copy = pltpu.make_async_copy(wb_ref, wb_vm, sems.at[4])
    copies[0].start()
    gain_copy.start()
    wb_copy.start()
    copies[1].start()
    copies[2].start()
    lane = lax.broadcasted_iota(jnp.int32, (KB, LANES), 1)
    place = jnp.where(lane < HEADS * KB, lax.rem(lane, KB), -1)
    gain_copy.wait()
    gain = gain_vm[...]
    wb_copy.wait()
    wb = wb_vm[...].astype(F32)
    spread_t = [jnp.broadcast_to(wb[h : h + 1, :], (KB, LANES)) for h in range(HEADS)]
    spread_t.append(jnp.zeros((LANES - HEADS * KB, LANES), F32))
    spread_t = jnp.concatenate(spread_t, axis=0).astype(BF16)
    total = jnp.zeros((KB, LANES), F32)
    sends = []
    for i, (begin, end) in enumerate(CHUNKS):
        copies[i].wait()
        normed = norm_rows(held_ref[begin:end, :], gain)
        if i == 0:
            nq_vm[...] = normed
            for n in range(4):
                send = pltpu.make_async_copy(nq_vm, nq_ref.at[n], out_sems.at[n])
                send.start()
                sends.append(send)
        wide = nt_dot(normed, spread_t)
        for j in range(begin // KB, end // KB):
            row = j * KB - begin
            total = jnp.where(place == j % KB, wide[row : row + KB, :], total)
            if j % KB == KB - 1:
                tile_ref[j + 1 - KB : j + 1, :] = total
    for send in sends:
        send.wait()


def copies_kernel(tile_ref, halves_ref):
    for half in range(2):
        part = tile_ref[half * KB : (half + 1) * KB, :]
        for r in range(NROW):
            halves_ref[2 * r + half] = part


def relay_kernel(ys_ref, out_ref):
    for a in range(QROWS):
        parts = [ys_ref[y, a * KB : (a + 1) * KB, :].astype(F32) for y in range(4)]
        out_ref[a * 96 : (a + 1) * 96, :] = jnp.concatenate(parts, axis=0).astype(BF16)


def hold_kernel(first_ref, bias_ref, again_ref, order_ref):
    again_ref[...] = first_ref[...]
    col = lax.axis_index("col")
    core = lax.rem(col, 2)
    x = lax.rem(col // 2, 4)
    place = 0
    for side in range(2):
        for mask in MASKS:
            for y in range(4):
                block = y * 8 + lax.bitwise_xor(x, mask) * 2 + lax.bitwise_xor(core, side)
                start = pl.multiple_of(block * KB, 8)
                order_ref[place : place + KB, :] = bias_ref[pl.ds(start, KB), :]
                place += KB


def nt_dot(left, right):
    return lax.dot_general(left, right, (((1,), (1,)), ((), ())), preferred_element_type=F32)


def twice(block):
    zero = jnp.zeros_like(block)
    top = jnp.concatenate([block, zero], axis=1)
    return jnp.concatenate([top, jnp.concatenate([zero, block], axis=1)], axis=0)


def attend_kernel(
    own_ref, first_ref, second_ref, third_ref, theirs_a_ref, theirs_b_ref, order_ref,
    nq_ref, wq_ref, wkv_ref, wg_ref, wo_ref,
    out_ref, held_ref, gate_ref, gated_ref,
):
    sources = (
        own_ref, first_ref, second_ref, third_ref,
        theirs_a_ref.at[0], theirs_a_ref.at[1], theirs_b_ref.at[0], theirs_b_ref.at[1],
    )
    nq = nq_ref[0]
    query = jnp.dot(nq, wq_ref[...], preferred_element_type=F32) * (1.0 / 32**0.5)
    query = query.astype(BF16).astype(F32)
    gate_ref[...] = jax.nn.sigmoid(jnp.dot(nq, wg_ref[...], preferred_element_type=F32))
    wk = twice(wkv_ref[:, :LANES].astype(F32)).astype(BF16)
    wvt = twice(wkv_ref[:, LANES:].astype(F32).T).astype(BF16)
    lane = lax.broadcasted_iota(jnp.int32, (KB, LANES), 1)
    zero = jnp.zeros((LANES, LANES), F32)
    for i in range(QROWS // 2):
        sides = []
        masked = []
        for a in (2 * i, 2 * i + 1):
            sides.append(
                jnp.concatenate([ref[a * 96 : (a + 1) * 96, :] for ref in sources], axis=0)
            )
            q = query[a * KB : (a + 1) * KB, :]
            parts = [jnp.where(lane // 32 == h, q, 0.0) for h in range(HEADS)]
            parts.append(jnp.zeros((LANES - HEADS * KB, LANES), F32))
            masked.append(jnp.concatenate(parts, axis=0))
        queries = jnp.concatenate(
            [
                jnp.concatenate([masked[0], zero], axis=1),
                jnp.concatenate([zero, masked[1]], axis=1),
            ],
            axis=0,
        ).astype(BF16)
        rows = jnp.concatenate(sides, axis=1)
        keys = jnp.dot(rows, wk, preferred_element_type=F32).astype(BF16)
        values_t = nt_dot(wvt, rows).astype(BF16)
        score = nt_dot(keys, queries)
        for n in range(2):
            a = 2 * i + n
            full = score[:, n * LANES : (n + 1) * LANES] + order_ref[...]
            held_ref[a % 4] = full
            top = jnp.max(full, axis=0, keepdims=True)
            weights = jnp.exp(held_ref[a % 4] - top)
            total = jnp.sum(weights, axis=0, keepdims=True)
            high = weights.astype(BF16)
            low = (weights - high.astype(F32)).astype(BF16)
            both = jnp.dot(
                values_t[n * LANES : (n + 1) * LANES, :],
                jnp.concatenate([high, low], axis=1),
                preferred_element_type=F32,
            )
            attended = ((both[:, :LANES] + both[:, LANES:]) / total).T
            mine = jnp.zeros((KB, LANES), F32)
            for h in range(HEADS):
                mine = jnp.where(lane // 32 == h, attended[h * KB : (h + 1) * KB, :], mine)
            span = slice(a * KB, (a + 1) * KB)
            gated_ref[span, :] = gate_ref[span, :] * mine
    out_ref[...] = jnp.dot(
        gated_ref[...].astype(BF16), wo_ref[...], preferred_element_type=F32
    ).astype(BF16)


def permute_col(value, target):
    return lax.ppermute(value, "col", [(c, target(c)) for c in range(NCOL)])


def permute_all(value, target):
    pairs = []
    for r in range(NROW):
        for c in range(NCOL):
            r2, c2 = target(r, c)
            pairs.append((r * NCOL + c, r2 * NCOL + c2))
    return lax.ppermute(value, ("row", "col"), pairs)


GROUPS_Y = [[y * 8 + i for y in range(4)] for i in range(8)]


def near_x(mask):
    return lambda c: c ^ (mask * 2)


GROUPS_ROW_CORE = [
    [r * NCOL + 2 * q + e for r in range(NROW) for e in range(2)] for q in range(NCOL // 2)
]


def body(pair, ln_gain, w_query, w_keyval, w_gate, w_bias, w_out):
    shape = jax.ShapeDtypeStruct
    rows = pair.reshape(-1, LANES)
    nrows = QROWS * KB
    nq, tile = pl.pallas_call(
        front_kernel,
        in_specs=[whole(pl.ANY)] * 3,
        out_specs=[whole(pl.ANY), whole()],
        out_shape=[shape((4, nrows, LANES), BF16), shape((2 * KB, LANES), F32)],
        scratch_shapes=[
            VM(rows.shape, BF16),
            VM((1, LANES), F32),
            VM((HEADS, LANES), BF16),
            VM((nrows, LANES), BF16),
            pltpu.SemaphoreType.DMA((5,)),
            pltpu.SemaphoreType.DMA((4,)),
        ],
        name="front",
    )(rows, ln_gain.reshape(1, LANES), w_bias.T)
    ys = lax.all_to_all(nq, "col", 0, 0, axis_index_groups=GROUPS_Y)
    tile = permute_all(tile, lambda r, c: (c // 2, 2 * r + c % 2))
    small = pltpu.CompilerParams(vmem_limit_bytes=16 * 1024 * 1024)
    halves = pl.pallas_call(
        copies_kernel,
        in_specs=[whole()],
        out_specs=whole(),
        out_shape=shape((2 * NROW, KB, LANES), F32),
        compiler_params=small,
        cost_estimate=pl.CostEstimate(flops=20 * 10**9, bytes_accessed=0, transcendentals=0),
        name="copies",
    )(tile)
    bias = lax.all_to_all(halves, ("row", "col"), 0, 0, axis_index_groups=GROUPS_ROW_CORE)
    piece = pl.pallas_call(
        relay_kernel,
        in_specs=[whole()],
        out_specs=whole(),
        out_shape=shape((4 * nrows, LANES), BF16),
        compiler_params=small,
        name="relay",
    )(ys)
    first = permute_col(piece, near_x(1))
    second = permute_col(piece, near_x(3))
    again, order = pl.pallas_call(
        hold_kernel,
        in_specs=[whole()] * 2,
        out_specs=[whole()] * 2,
        out_shape=[shape((4 * nrows, LANES), BF16), shape((N_RES, LANES), F32)],
        compiler_params=small,
        name="hold",
    )(first, bias.reshape(-1, LANES))
    third = permute_col(again, near_x(3))
    mine = [piece, first, second, third]
    theirs = [permute_col(jnp.stack(mine[i : i + 2]), lambda c: c ^ 1) for i in (0, 2)]
    out = pl.pallas_call(
        attend_kernel,
        in_specs=[whole()] * 12,
        out_specs=whole(),
        out_shape=shape((nrows, LANES), BF16),
        scratch_shapes=[
            VM((4, 768, LANES), F32),
            VM((nrows, LANES), F32),
            VM((nrows, LANES), F32),
        ],
        compiler_params=pltpu.CompilerParams(vmem_limit_bytes=32 * 1024 * 1024),
        name="attend",
    )(*mine, *theirs, order, nq, w_query, w_keyval, w_gate, w_out)
    return out.reshape(QROWS, KB, LANES)


def solution(mesh):
    placed = (P("row", "col", None), P(), P(), P(), P(), P(), P())
    return jax.shard_map(
        body, mesh=mesh, in_specs=placed, out_specs=P("row", "col", None), check_vma=False
    )
```

```python
import jax
import jax.numpy as jnp
from jax import lax
from jax.experimental import pallas as pl
from jax.experimental.pallas import tpu as pltpu
from jax.sharding import PartitionSpec as P

QROWS = 8
KB = 24
HEADS = 4
LANES = 128
NROW = 16
N_RES = 768
NCOL = 32
F32 = jnp.float32
BF16 = jnp.bfloat16
VM = pltpu.VMEM


def whole(space=VM):
    return pl.BlockSpec(memory_space=space)


MASKS = (0, 1, 3, 2)


def norm_rows(block, gain):
    values = block.astype(F32)
    mean = jnp.mean(values, axis=-1, keepdims=True)
    centred = values - mean
    variance = jnp.mean(centred * centred, axis=-1, keepdims=True)
    return (centred * lax.rsqrt(variance + 1e-05) * gain).astype(BF16)


CHUNKS = ((0, 192), (192, 576), (576, 1152))


def front_kernel(
    rows_ref, gain_ref, wb_ref, nq_ref, tile_ref, held_ref, gain_vm, wb_vm, sems
):
    copies = []
    for i, (begin, end) in enumerate(CHUNKS):
        part = pl.ds(begin, end - begin)
        copies.append(pltpu.make_async_copy(rows_ref.at[part], held_ref.at[part], sems.at[i]))
    gain_copy = pltpu.make_async_copy(gain_ref, gain_vm, sems.at[3])
    wb_copy = pltpu.make_async_copy(wb_ref, wb_vm, sems.at[4])
    copies[0].start()
    gain_copy.start()
    wb_copy.start()
    copies[1].start()
    copies[2].start()
    lane = lax.broadcasted_iota(jnp.int32, (KB, LANES), 1)
    place = jnp.where(lane < HEADS * KB, lax.rem(lane, KB), -1)
    gain_copy.wait()
    gain = gain_vm[...]
    wb_copy.wait()
    wb = wb_vm[...].astype(F32)
    spread_t = [jnp.broadcast_to(wb[h : h + 1, :], (KB, LANES)) for h in range(HEADS)]
    spread_t.append(jnp.zeros((LANES - HEADS * KB, LANES), F32))
    spread_t = jnp.concatenate(spread_t, axis=0).astype(BF16)
    total = jnp.zeros((KB, LANES), F32)
    for i, (begin, end) in enumerate(CHUNKS):
        copies[i].wait()
        normed = norm_rows(held_ref[begin:end, :], gain)
        if i == 0:
            nq_ref[...] = normed
        wide = nt_dot(normed, spread_t)
        for j in range(begin // KB, end // KB):
            row = j * KB - begin
            total = jnp.where(place == j % KB, wide[row : row + KB, :], total)
            if j % KB == KB - 1:
                tile_ref[j + 1 - KB : j + 1, :] = total


def copies_kernel(tile_ref, halves_ref):
    for half in range(2):
        part = tile_ref[half * KB : (half + 1) * KB, :]
        for r in range(NROW):
            halves_ref[2 * r + half] = part


def relay_kernel(own_ref, first_ref, second_ref, third_ref, out_ref):
    for a in range(QROWS):
        span = slice(a * KB, (a + 1) * KB)
        refs = (own_ref, first_ref, second_ref, third_ref)
        parts = [ref[span, :].astype(F32) for ref in refs]
        out_ref[a * 96 : (a + 1) * 96, :] = jnp.concatenate(parts, axis=0).astype(BF16)


def hold_kernel(first_ref, bias_ref, again_ref, order_ref):
    again_ref[...] = first_ref[...]
    col = lax.axis_index("col")
    core = lax.rem(col, 2)
    x = lax.rem(col // 2, 4)
    y_hi = col // 8
    place = 0
    for side in range(2):
        for mask in MASKS:
            for y_mask in MASKS:
                y = lax.bitwise_xor(y_hi, y_mask)
                block = y * 8 + lax.bitwise_xor(x, mask) * 2 + lax.bitwise_xor(core, side)
                start = pl.multiple_of(block * KB, 8)
                order_ref[place : place + KB, :] = bias_ref[pl.ds(start, KB), :]
                place += KB


def nt_dot(left, right):
    return lax.dot_general(left, right, (((1,), (1,)), ((), ())), preferred_element_type=F32)


def twice(block):
    zero = jnp.zeros_like(block)
    top = jnp.concatenate([block, zero], axis=1)
    return jnp.concatenate([top, jnp.concatenate([zero, block], axis=1)], axis=0)


def attend_kernel(
    own_ref, first_ref, second_ref, third_ref, theirs_a_ref, theirs_b_ref, order_ref,
    nq_ref, wq_ref, wkv_ref, wg_ref, wo_ref,
    out_ref, held_ref, gate_ref, gated_ref,
):
    sources = (
        own_ref, first_ref, second_ref, third_ref,
        theirs_a_ref.at[0], theirs_a_ref.at[1], theirs_b_ref.at[0], theirs_b_ref.at[1],
    )
    nq = nq_ref[...]
    query = jnp.dot(nq, wq_ref[...], preferred_element_type=F32) * (1.0 / 32**0.5)
    query = query.astype(BF16).astype(F32)
    gate_ref[...] = jax.nn.sigmoid(jnp.dot(nq, wg_ref[...], preferred_element_type=F32))
    wk = twice(wkv_ref[:, :LANES].astype(F32)).astype(BF16)
    wvt = twice(wkv_ref[:, LANES:].astype(F32).T).astype(BF16)
    lane = lax.broadcasted_iota(jnp.int32, (KB, LANES), 1)
    zero = jnp.zeros((LANES, LANES), F32)
    for i in range(QROWS // 2):
        sides = []
        masked = []
        for a in (2 * i, 2 * i + 1):
            sides.append(
                jnp.concatenate([ref[a * 96 : (a + 1) * 96, :] for ref in sources], axis=0)
            )
            q = query[a * KB : (a + 1) * KB, :]
            parts = [jnp.where(lane // 32 == h, q, 0.0) for h in range(HEADS)]
            parts.append(jnp.zeros((LANES - HEADS * KB, LANES), F32))
            masked.append(jnp.concatenate(parts, axis=0))
        queries = jnp.concatenate(
            [
                jnp.concatenate([masked[0], zero], axis=1),
                jnp.concatenate([zero, masked[1]], axis=1),
            ],
            axis=0,
        ).astype(BF16)
        rows = jnp.concatenate(sides, axis=1)
        keys = jnp.dot(rows, wk, preferred_element_type=F32).astype(BF16)
        values_t = nt_dot(wvt, rows).astype(BF16)
        score = nt_dot(keys, queries)
        for n in range(2):
            a = 2 * i + n
            full = score[:, n * LANES : (n + 1) * LANES] + order_ref[...]
            held_ref[a % 4] = full
            top = jnp.max(full, axis=0, keepdims=True)
            weights = jnp.exp(held_ref[a % 4] - top)
            total = jnp.sum(weights, axis=0, keepdims=True)
            high = weights.astype(BF16)
            low = (weights - high.astype(F32)).astype(BF16)
            both = jnp.dot(
                values_t[n * LANES : (n + 1) * LANES, :],
                jnp.concatenate([high, low], axis=1),
                preferred_element_type=F32,
            )
            attended = ((both[:, :LANES] + both[:, LANES:]) / total).T
            mine = jnp.zeros((KB, LANES), F32)
            for h in range(HEADS):
                mine = jnp.where(lane // 32 == h, attended[h * KB : (h + 1) * KB, :], mine)
            span = slice(a * KB, (a + 1) * KB)
            gated_ref[span, :] = gate_ref[span, :] * mine
    out_ref[...] = jnp.dot(
        gated_ref[...].astype(BF16), wo_ref[...], preferred_element_type=F32
    ).astype(BF16)


def permute_col(value, target):
    return lax.ppermute(value, "col", [(c, target(c)) for c in range(NCOL)])


def permute_all(value, target):
    pairs = []
    for r in range(NROW):
        for c in range(NCOL):
            r2, c2 = target(r, c)
            pairs.append((r * NCOL + c, r2 * NCOL + c2))
    return lax.ppermute(value, ("row", "col"), pairs)


def near_y(mask):
    return lambda c: c ^ (mask * 8)


def near_x(mask):
    return lambda c: c ^ (mask * 2)


GROUPS_ROW_CORE = [
    [r * NCOL + 2 * q + e for r in range(NROW) for e in range(2)] for q in range(NCOL // 2)
]


def body(pair, ln_gain, w_query, w_keyval, w_gate, w_bias, w_out):
    shape = jax.ShapeDtypeStruct
    rows = pair.reshape(-1, LANES)
    nrows = QROWS * KB
    nq, tile = pl.pallas_call(
        front_kernel,
        in_specs=[whole(pl.ANY)] * 3,
        out_specs=[whole(), whole()],
        out_shape=[shape((nrows, LANES), BF16), shape((2 * KB, LANES), F32)],
        scratch_shapes=[
            VM(rows.shape, BF16),
            VM((1, LANES), F32),
            VM((HEADS, LANES), BF16),
            pltpu.SemaphoreType.DMA((5,)),
        ],
        name="front",
    )(rows, ln_gain.reshape(1, LANES), w_bias.T)
    ys = [nq] + [permute_col(nq, near_y(mask)) for mask in MASKS[1:]]
    tile = permute_all(tile, lambda r, c: (c // 2, 2 * r + c % 2))
    small = pltpu.CompilerParams(vmem_limit_bytes=16 * 1024 * 1024)
    halves = pl.pallas_call(
        copies_kernel,
        in_specs=[whole()],
        out_specs=whole(),
        out_shape=shape((2 * NROW, KB, LANES), F32),
        compiler_params=small,
        cost_estimate=pl.CostEstimate(flops=20 * 10**9, bytes_accessed=0, transcendentals=0),
        name="copies",
    )(tile)
    bias = lax.all_to_all(halves, ("row", "col"), 0, 0, axis_index_groups=GROUPS_ROW_CORE)
    piece = pl.pallas_call(
        relay_kernel,
        in_specs=[whole()] * 4,
        out_specs=whole(),
        out_shape=shape((4 * nrows, LANES), BF16),
        compiler_params=small,
        name="relay",
    )(*ys)
    first = permute_col(piece, near_x(1))
    second = permute_col(piece, near_x(3))
    again, order = pl.pallas_call(
        hold_kernel,
        in_specs=[whole()] * 2,
        out_specs=[whole()] * 2,
        out_shape=[shape((4 * nrows, LANES), BF16), shape((N_RES, LANES), F32)],
        compiler_params=small,
        name="hold",
    )(first, bias.reshape(-1, LANES))
    third = permute_col(again, near_x(3))
    mine = [piece, first, second, third]
    theirs = [permute_col(jnp.stack(mine[i : i + 2]), lambda c: c ^ 1) for i in (0, 2)]
    out = pl.pallas_call(
        attend_kernel,
        in_specs=[whole()] * 12,
        out_specs=whole(),
        out_shape=shape((nrows, LANES), BF16),
        scratch_shapes=[
            VM((4, 768, LANES), F32),
            VM((nrows, LANES), F32),
            VM((nrows, LANES), F32),
        ],
        compiler_params=pltpu.CompilerParams(vmem_limit_bytes=32 * 1024 * 1024),
        name="attend",
    )(*mine, *theirs, order, nq, w_query, w_keyval, w_gate, w_out)
    return out.reshape(QROWS, KB, LANES)


def solution(mesh):
    placed = (P("row", "col", None), P(), P(), P(), P(), P(), P())
    return jax.shard_map(
        body, mesh=mesh, in_specs=placed, out_specs=P("row", "col", None), check_vma=False
    )
```

```python
import jax
import jax.numpy as jnp
from jax import lax
from jax.experimental import pallas as pl
from jax.experimental.pallas import tpu as pltpu
from jax.sharding import PartitionSpec as P

QROWS = 8
KB = 24
HEADS = 4
LANES = 128
NROW = 16
N_RES = 768
NCOL = 32
F32 = jnp.float32
BF16 = jnp.bfloat16
VM = pltpu.VMEM


def whole(space=VM):
    return pl.BlockSpec(memory_space=space)


MASKS = (0, 1, 3, 2)


def norm_rows(block, gain):
    values = block.astype(F32)
    mean = jnp.mean(values, axis=-1, keepdims=True)
    centred = values - mean
    variance = jnp.mean(centred * centred, axis=-1, keepdims=True)
    return (centred * lax.rsqrt(variance + 1e-05) * gain).astype(BF16)


CHUNKS = ((0, 192), (192, 576), (576, 1152))


def front_kernel(
    rows_ref, gain_ref, wb_ref, nq_ref, tile_ref, held_ref, gain_vm, wb_vm, sems
):
    copies = []
    for i, (begin, end) in enumerate(CHUNKS):
        part = pl.ds(begin, end - begin)
        copies.append(pltpu.make_async_copy(rows_ref.at[part], held_ref.at[part], sems.at[i]))
    gain_copy = pltpu.make_async_copy(gain_ref, gain_vm, sems.at[3])
    wb_copy = pltpu.make_async_copy(wb_ref, wb_vm, sems.at[4])
    copies[0].start()
    gain_copy.start()
    wb_copy.start()
    copies[1].start()
    copies[2].start()
    lane = lax.broadcasted_iota(jnp.int32, (KB, LANES), 1)
    place = jnp.where(lane < HEADS * KB, lax.rem(lane, KB), -1)
    gain_copy.wait()
    gain = gain_vm[...]
    wb_copy.wait()
    wb = wb_vm[...].astype(F32)
    spread_t = [jnp.broadcast_to(wb[h : h + 1, :], (KB, LANES)) for h in range(HEADS)]
    spread_t.append(jnp.zeros((LANES - HEADS * KB, LANES), F32))
    spread_t = jnp.concatenate(spread_t, axis=0).astype(BF16)
    total = jnp.zeros((KB, LANES), F32)
    for i, (begin, end) in enumerate(CHUNKS):
        copies[i].wait()
        normed = norm_rows(held_ref[begin:end, :], gain)
        if i == 0:
            nq_ref[...] = normed
        wide = nt_dot(normed, spread_t)
        for j in range(begin // KB, end // KB):
            row = j * KB - begin
            total = jnp.where(place == j % KB, wide[row : row + KB, :], total)
            if j % KB == KB - 1:
                tile_ref[j + 1 - KB : j + 1, :] = total


def copies_kernel(tile_ref, halves_ref):
    for half in range(2):
        part = tile_ref[half * KB : (half + 1) * KB, :]
        for r in range(NROW):
            halves_ref[2 * r + half] = part


def relay_kernel(own_ref, first_ref, second_ref, third_ref, out_ref):
    for a in range(QROWS):
        span = slice(a * KB, (a + 1) * KB)
        refs = (own_ref, first_ref, second_ref, third_ref)
        parts = [ref[span, :].astype(F32) for ref in refs]
        out_ref[a * 96 : (a + 1) * 96, :] = jnp.concatenate(parts, axis=0).astype(BF16)


def join_kernel(second_ref, third_ref, bias_ref, pair_ref, order_ref):
    pair_ref[0] = second_ref[...]
    pair_ref[1] = third_ref[...]
    col = lax.axis_index("col")
    core = lax.rem(col, 2)
    x = lax.rem(col // 2, 4)
    y_hi = col // 8
    place = 0
    for side in range(2):
        for mask in MASKS:
            for y_mask in MASKS:
                y = lax.bitwise_xor(y_hi, y_mask)
                block = y * 8 + lax.bitwise_xor(x, mask) * 2 + lax.bitwise_xor(core, side)
                start = pl.multiple_of(block * KB, 8)
                order_ref[place : place + KB, :] = bias_ref[pl.ds(start, KB), :]
                place += KB


def nt_dot(left, right):
    return lax.dot_general(left, right, (((1,), (1,)), ((), ())), preferred_element_type=F32)


def twice(block):
    zero = jnp.zeros_like(block)
    top = jnp.concatenate([block, zero], axis=1)
    return jnp.concatenate([top, jnp.concatenate([zero, block], axis=1)], axis=0)


def attend_kernel(
    own_ref, first_ref, second_ref, third_ref, theirs_a_ref, theirs_b_ref, order_ref,
    nq_ref, wq_ref, wkv_ref, wg_ref, wo_ref,
    out_ref, held_ref, gate_ref, gated_ref,
):
    sources = (
        own_ref, first_ref, second_ref, third_ref,
        theirs_a_ref.at[0], theirs_a_ref.at[1], theirs_b_ref.at[0], theirs_b_ref.at[1],
    )
    nq = nq_ref[...]
    query = jnp.dot(nq, wq_ref[...], preferred_element_type=F32) * (1.0 / 32**0.5)
    query = query.astype(BF16).astype(F32)
    gate_ref[...] = jax.nn.sigmoid(jnp.dot(nq, wg_ref[...], preferred_element_type=F32))
    wk = twice(wkv_ref[:, :LANES].astype(F32)).astype(BF16)
    wvt = twice(wkv_ref[:, LANES:].astype(F32).T).astype(BF16)
    lane = lax.broadcasted_iota(jnp.int32, (KB, LANES), 1)
    zero = jnp.zeros((LANES, LANES), F32)
    for i in range(QROWS // 2):
        sides = []
        masked = []
        for a in (2 * i, 2 * i + 1):
            sides.append(
                jnp.concatenate([ref[a * 96 : (a + 1) * 96, :] for ref in sources], axis=0)
            )
            q = query[a * KB : (a + 1) * KB, :]
            parts = [jnp.where(lane // 32 == h, q, 0.0) for h in range(HEADS)]
            parts.append(jnp.zeros((LANES - HEADS * KB, LANES), F32))
            masked.append(jnp.concatenate(parts, axis=0))
        queries = jnp.concatenate(
            [
                jnp.concatenate([masked[0], zero], axis=1),
                jnp.concatenate([zero, masked[1]], axis=1),
            ],
            axis=0,
        ).astype(BF16)
        rows = jnp.concatenate(sides, axis=1)
        keys = jnp.dot(rows, wk, preferred_element_type=F32).astype(BF16)
        values_t = nt_dot(wvt, rows).astype(BF16)
        score = nt_dot(keys, queries)
        for n in range(2):
            a = 2 * i + n
            full = score[:, n * LANES : (n + 1) * LANES] + order_ref[...]
            held_ref[a % 4] = full
            top = jnp.max(full, axis=0, keepdims=True)
            weights = jnp.exp(held_ref[a % 4] - top)
            total = jnp.sum(weights, axis=0, keepdims=True)
            high = weights.astype(BF16)
            low = (weights - high.astype(F32)).astype(BF16)
            both = jnp.dot(
                values_t[n * LANES : (n + 1) * LANES, :],
                jnp.concatenate([high, low], axis=1),
                preferred_element_type=F32,
            )
            attended = ((both[:, :LANES] + both[:, LANES:]) / total).T
            mine = jnp.zeros((KB, LANES), F32)
            for h in range(HEADS):
                mine = jnp.where(lane // 32 == h, attended[h * KB : (h + 1) * KB, :], mine)
            span = slice(a * KB, (a + 1) * KB)
            gated_ref[span, :] = gate_ref[span, :] * mine
    out_ref[...] = jnp.dot(
        gated_ref[...].astype(BF16), wo_ref[...], preferred_element_type=F32
    ).astype(BF16)


def permute_col(value, target):
    return lax.ppermute(value, "col", [(c, target(c)) for c in range(NCOL)])


def permute_all(value, target):
    pairs = []
    for r in range(NROW):
        for c in range(NCOL):
            r2, c2 = target(r, c)
            pairs.append((r * NCOL + c, r2 * NCOL + c2))
    return lax.ppermute(value, ("row", "col"), pairs)


def near_y(mask):
    return lambda c: c ^ (mask * 8)


def near_x(mask):
    return lambda c: c ^ (mask * 2)


GROUPS_ROW_CORE = [
    [r * NCOL + 2 * q + e for r in range(NROW) for e in range(2)] for q in range(NCOL // 2)
]


def body(pair, ln_gain, w_query, w_keyval, w_gate, w_bias, w_out):
    shape = jax.ShapeDtypeStruct
    rows = pair.reshape(-1, LANES)
    nrows = QROWS * KB
    nq, tile = pl.pallas_call(
        front_kernel,
        in_specs=[whole(pl.ANY)] * 3,
        out_specs=[whole(), whole()],
        out_shape=[shape((nrows, LANES), BF16), shape((2 * KB, LANES), F32)],
        scratch_shapes=[
            VM(rows.shape, BF16),
            VM((1, LANES), F32),
            VM((HEADS, LANES), BF16),
            pltpu.SemaphoreType.DMA((5,)),
        ],
        name="front",
    )(rows, ln_gain.reshape(1, LANES), w_bias.T)
    ys = [nq] + [permute_col(nq, near_y(mask)) for mask in MASKS[1:]]
    tile = permute_all(tile, lambda r, c: (c // 2, 2 * r + c % 2))
    small = pltpu.CompilerParams(vmem_limit_bytes=16 * 1024 * 1024)
    halves = pl.pallas_call(
        copies_kernel,
        in_specs=[whole()],
        out_specs=whole(),
        out_shape=shape((2 * NROW, KB, LANES), F32),
        compiler_params=small,
        cost_estimate=pl.CostEstimate(flops=20 * 10**9, bytes_accessed=0, transcendentals=0),
        name="copies",
    )(tile)
    bias = lax.all_to_all(halves, ("row", "col"), 0, 0, axis_index_groups=GROUPS_ROW_CORE)
    piece = pl.pallas_call(
        relay_kernel,
        in_specs=[whole()] * 4,
        out_specs=whole(),
        out_shape=shape((4 * nrows, LANES), BF16),
        compiler_params=small,
        cost_estimate=pl.CostEstimate(flops=30 * 10**9, bytes_accessed=0, transcendentals=0),
        name="relay",
    )(*ys)
    first = permute_col(piece, near_x(1))
    second = permute_col(piece, near_x(3))
    third = permute_col(first, near_x(3))
    mine = [piece, first, second, third]
    joined, order = pl.pallas_call(
        join_kernel,
        in_specs=[whole()] * 3,
        out_specs=[whole()] * 2,
        out_shape=[shape((2, 4 * nrows, LANES), BF16), shape((N_RES, LANES), F32)],
        compiler_params=small,
        name="join",
    )(second, third, bias.reshape(-1, LANES))
    theirs = [permute_col(both, lambda c: c ^ 1) for both in (jnp.stack(mine[:2]), joined)]
    out = pl.pallas_call(
        attend_kernel,
        in_specs=[whole()] * 12,
        out_specs=whole(),
        out_shape=shape((nrows, LANES), BF16),
        scratch_shapes=[
            VM((4, 768, LANES), F32),
            VM((nrows, LANES), F32),
            VM((nrows, LANES), F32),
        ],
        compiler_params=pltpu.CompilerParams(vmem_limit_bytes=32 * 1024 * 1024),
        name="attend",
    )(*mine, *theirs, order, nq, w_query, w_keyval, w_gate, w_out)
    return out.reshape(QROWS, KB, LANES)


def solution(mesh):
    placed = (P("row", "col", None), P(), P(), P(), P(), P(), P())
    return jax.shard_map(
        body, mesh=mesh, in_specs=placed, out_specs=P("row", "col", None), check_vma=False
    )
```

```python
import jax
import jax.numpy as jnp
from jax import lax
from jax.experimental import pallas as pl
from jax.experimental.pallas import tpu as pltpu
from jax.sharding import PartitionSpec as P

QROWS = 8
KB = 24
HEADS = 4
LANES = 128
NROW = 16
N_RES = 768
NCOL = 32
F32 = jnp.float32
BF16 = jnp.bfloat16
VM = pltpu.VMEM


def whole(space=VM):
    return pl.BlockSpec(memory_space=space)


MASKS = (0, 1, 3, 2)


def norm_rows(block, gain):
    values = block.astype(F32)
    mean = jnp.mean(values, axis=-1, keepdims=True)
    centred = values - mean
    variance = jnp.mean(centred * centred, axis=-1, keepdims=True)
    return (centred * lax.rsqrt(variance + 1e-05) * gain).astype(BF16)


CHUNKS = ((0, 192), (192, 576), (576, 1152))


def front_kernel(
    rows_ref, gain_ref, wb_ref, nq_ref, tile_ref, held_ref, gain_vm, wb_vm, sems
):
    copies = []
    for i, (begin, end) in enumerate(CHUNKS):
        part = pl.ds(begin, end - begin)
        copies.append(pltpu.make_async_copy(rows_ref.at[part], held_ref.at[part], sems.at[i]))
    gain_copy = pltpu.make_async_copy(gain_ref, gain_vm, sems.at[3])
    wb_copy = pltpu.make_async_copy(wb_ref, wb_vm, sems.at[4])
    copies[0].start()
    gain_copy.start()
    wb_copy.start()
    copies[1].start()
    copies[2].start()
    lane = lax.broadcasted_iota(jnp.int32, (KB, LANES), 1)
    place = jnp.where(lane < HEADS * KB, lax.rem(lane, KB), -1)
    gain_copy.wait()
    gain = gain_vm[...]
    wb_copy.wait()
    wb = wb_vm[...].astype(F32)
    spread_t = [jnp.broadcast_to(wb[h : h + 1, :], (KB, LANES)) for h in range(HEADS)]
    spread_t.append(jnp.zeros((LANES - HEADS * KB, LANES), F32))
    spread_t = jnp.concatenate(spread_t, axis=0).astype(BF16)
    total = jnp.zeros((KB, LANES), F32)
    for i, (begin, end) in enumerate(CHUNKS):
        copies[i].wait()
        normed = norm_rows(held_ref[begin:end, :], gain)
        if i == 0:
            nq_ref[...] = normed
        wide = nt_dot(normed, spread_t)
        for j in range(begin // KB, end // KB):
            row = j * KB - begin
            total = jnp.where(place == j % KB, wide[row : row + KB, :], total)
            if j % KB == KB - 1:
                tile_ref[j + 1 - KB : j + 1, :] = total


def copies_kernel(tile_ref, out_ref, sems):
    sends = []
    for r in range(NROW):
        send = pltpu.make_async_copy(tile_ref, out_ref.at[r], sems.at[r])
        send.start()
        sends.append(send)
    for send in sends:
        send.wait()


def relay_kernel(own_ref, first_ref, second_ref, third_ref, out_ref):
    for a in range(QROWS):
        span = slice(a * KB, (a + 1) * KB)
        refs = (own_ref, first_ref, second_ref, third_ref)
        parts = [ref[span, :].astype(F32) for ref in refs]
        out_ref[a * 96 : (a + 1) * 96, :] = jnp.concatenate(parts, axis=0).astype(BF16)


HALF_K = NROW * KB


def join_kernel(third_ref, bias_ref, payload_ref, order_ref):
    rows = third_ref.shape[0]
    payload_ref[0:rows, :] = third_ref[...]
    col = lax.axis_index("col")
    core = lax.rem(col, 2)
    x = lax.rem(col // 2, 4)
    y_hi = col // 8
    place = 0
    rest = []
    for mask in MASKS:
        for y_mask in MASKS:
            slot = lax.bitwise_xor(y_hi, y_mask) * 4 + lax.bitwise_xor(x, mask)
            mine = pl.multiple_of((slot * 2 + core) * KB, 8)
            theirs = pl.multiple_of((slot * 2 + 1 - core) * KB, 8)
            order_ref[place : place + KB, :] = bias_ref[pl.ds(mine, KB), :]
            rest.append(bias_ref[pl.ds(theirs, KB), :])
            place += KB
    rest = jnp.concatenate(rest, axis=0)
    for term in range(3):
        part = rest.astype(BF16)
        rest = rest - part.astype(F32)
        begin = rows + term * HALF_K
        payload_ref[begin : begin + HALF_K, :] = part


def nt_dot(left, right):
    return lax.dot_general(left, right, (((1,), (1,)), ((), ())), preferred_element_type=F32)


def twice(block):
    zero = jnp.zeros_like(block)
    top = jnp.concatenate([block, zero], axis=1)
    return jnp.concatenate([top, jnp.concatenate([zero, block], axis=1)], axis=0)


def attend_kernel(
    own_ref, first_ref, second_ref, third_ref, theirs_a_ref, theirs_b_ref, order_ref,
    nq_ref, wq_ref, wkv_ref, wg_ref, wo_ref,
    out_ref, bias_ref, held_ref, gate_ref, gated_ref,
):
    sources = (
        own_ref, first_ref, second_ref, third_ref,
        theirs_a_ref.at[0], theirs_a_ref.at[1], theirs_a_ref.at[2], theirs_b_ref,
    )
    bias_ref[0:HALF_K, :] = order_ref[...]
    terms = []
    for term in range(3):
        begin = third_ref.shape[0] + term * HALF_K
        terms.append(theirs_b_ref[begin : begin + HALF_K, :].astype(F32))
    bias_ref[HALF_K:, :] = (terms[0] + terms[1]) + terms[2]
    nq = nq_ref[...]
    query = jnp.dot(nq, wq_ref[...], preferred_element_type=F32) * (1.0 / 32**0.5)
    query = query.astype(BF16).astype(F32)
    gate_ref[...] = jax.nn.sigmoid(jnp.dot(nq, wg_ref[...], preferred_element_type=F32))
    wk = twice(wkv_ref[:, :LANES].astype(F32)).astype(BF16)
    wvt = twice(wkv_ref[:, LANES:].astype(F32).T).astype(BF16)
    lane = lax.broadcasted_iota(jnp.int32, (KB, LANES), 1)
    zero = jnp.zeros((LANES, LANES), F32)
    for i in range(QROWS // 2):
        sides = []
        masked = []
        for a in (2 * i, 2 * i + 1):
            sides.append(
                jnp.concatenate([ref[a * 96 : (a + 1) * 96, :] for ref in sources], axis=0)
            )
            q = query[a * KB : (a + 1) * KB, :]
            parts = [jnp.where(lane // 32 == h, q, 0.0) for h in range(HEADS)]
            parts.append(jnp.zeros((LANES - HEADS * KB, LANES), F32))
            masked.append(jnp.concatenate(parts, axis=0))
        queries = jnp.concatenate(
            [
                jnp.concatenate([masked[0], zero], axis=1),
                jnp.concatenate([zero, masked[1]], axis=1),
            ],
            axis=0,
        ).astype(BF16)
        rows = jnp.concatenate(sides, axis=1)
        keys = jnp.dot(rows, wk, preferred_element_type=F32).astype(BF16)
        values_t = nt_dot(wvt, rows).astype(BF16)
        score = nt_dot(keys, queries)
        for n in range(2):
            a = 2 * i + n
            full = score[:, n * LANES : (n + 1) * LANES] + bias_ref[...]
            held_ref[a % 4] = full
            top = jnp.max(full, axis=0, keepdims=True)
            weights = jnp.exp(held_ref[a % 4] - top)
            total = jnp.sum(weights, axis=0, keepdims=True)
            high = weights.astype(BF16)
            low = (weights - high.astype(F32)).astype(BF16)
            both = jnp.dot(
                values_t[n * LANES : (n + 1) * LANES, :],
                jnp.concatenate([high, low], axis=1),
                preferred_element_type=F32,
            )
            attended = ((both[:, :LANES] + both[:, LANES:]) / total).T
            mine = jnp.zeros((KB, LANES), F32)
            for h in range(HEADS):
                mine = jnp.where(lane // 32 == h, attended[h * KB : (h + 1) * KB, :], mine)
            span = slice(a * KB, (a + 1) * KB)
            gated_ref[span, :] = gate_ref[span, :] * mine
    out_ref[...] = jnp.dot(
        gated_ref[...].astype(BF16), wo_ref[...], preferred_element_type=F32
    ).astype(BF16)


def permute_col(value, target):
    return lax.ppermute(value, "col", [(c, target(c)) for c in range(NCOL)])


def permute_all(value, target):
    pairs = []
    for r in range(NROW):
        for c in range(NCOL):
            r2, c2 = target(r, c)
            pairs.append((r * NCOL + c, r2 * NCOL + c2))
    return lax.ppermute(value, ("row", "col"), pairs)


def near_y(mask):
    return lambda c: c ^ (mask * 8)


def near_x(mask):
    return lambda c: c ^ (mask * 2)


def body(pair, ln_gain, w_query, w_keyval, w_gate, w_bias, w_out):
    shape = jax.ShapeDtypeStruct
    rows = pair.reshape(-1, LANES)
    nrows = QROWS * KB
    nq, tile = pl.pallas_call(
        front_kernel,
        in_specs=[whole(pl.ANY)] * 3,
        out_specs=[whole(), whole()],
        out_shape=[shape((nrows, LANES), BF16), shape((2 * KB, LANES), F32)],
        scratch_shapes=[
            VM(rows.shape, BF16),
            VM((1, LANES), F32),
            VM((HEADS, LANES), BF16),
            pltpu.SemaphoreType.DMA((5,)),
        ],
        name="front",
    )(rows, ln_gain.reshape(1, LANES), w_bias.T)
    ys = [nq] + [permute_col(nq, near_y(mask)) for mask in MASKS[1:]]
    tile = permute_all(tile, lambda r, c: (c // 2, 2 * r + c % 2))
    small = pltpu.CompilerParams(vmem_limit_bytes=16 * 1024 * 1024)
    tiles = pl.pallas_call(
        copies_kernel,
        in_specs=[whole()],
        out_specs=whole(pl.ANY),
        out_shape=shape((NROW, 2 * KB, LANES), F32),
        scratch_shapes=[pltpu.SemaphoreType.DMA((NROW,))],
        compiler_params=small,
        cost_estimate=pl.CostEstimate(flops=20 * 10**9, bytes_accessed=0, transcendentals=0),
        name="copies",
    )(tile)
    bias = lax.all_to_all(tiles, "row", 0, 0)
    piece = pl.pallas_call(
        relay_kernel,
        in_specs=[whole()] * 4,
        out_specs=whole(),
        out_shape=shape((4 * nrows, LANES), BF16),
        compiler_params=small,
        cost_estimate=pl.CostEstimate(flops=30 * 10**9, bytes_accessed=0, transcendentals=0),
        name="relay",
    )(*ys)
    first = permute_col(piece, near_x(1))
    second = permute_col(piece, near_x(3))
    third = permute_col(first, near_x(3))
    mine = [piece, first, second, third]
    last, order = pl.pallas_call(
        join_kernel,
        in_specs=[whole()] * 2,
        out_specs=[whole()] * 2,
        out_shape=[
            shape((4 * nrows + 3 * HALF_K, LANES), BF16),
            shape((HALF_K, LANES), F32),
        ],
        compiler_params=small,
        name="join",
    )(third, bias.reshape(-1, LANES))
    theirs = [permute_col(value, lambda c: c ^ 1) for value in (jnp.stack(mine[:3]), last)]
    out = pl.pallas_call(
        attend_kernel,
        in_specs=[whole()] * 12,
        out_specs=whole(),
        out_shape=shape((nrows, LANES), BF16),
        scratch_shapes=[
            VM((N_RES, LANES), F32),
            VM((4, 768, LANES), F32),
            VM((nrows, LANES), F32),
            VM((nrows, LANES), F32),
        ],
        compiler_params=pltpu.CompilerParams(vmem_limit_bytes=32 * 1024 * 1024),
        name="attend",
    )(*mine, *theirs, order, nq, w_query, w_keyval, w_gate, w_out)
    return out.reshape(QROWS, KB, LANES)


def solution(mesh):
    placed = (P("row", "col", None), P(), P(), P(), P(), P(), P())
    return jax.shard_map(
        body, mesh=mesh, in_specs=placed, out_specs=P("row", "col", None), check_vma=False
    )
```

```python
import jax
import jax.numpy as jnp
from jax import lax
from jax.experimental import pallas as pl
from jax.experimental.pallas import tpu as pltpu
from jax.sharding import PartitionSpec as P

QROWS = 8
KB = 24
HEADS = 4
LANES = 128
NROW = 16
N_RES = 768
NCOL = 32
F32 = jnp.float32
BF16 = jnp.bfloat16
VM = pltpu.VMEM


def whole(space=VM):
    return pl.BlockSpec(memory_space=space)


MASKS = (0, 1, 3, 2)


def norm_rows(block, gain):
    values = block.astype(F32)
    mean = jnp.mean(values, axis=-1, keepdims=True)
    centred = values - mean
    variance = jnp.mean(centred * centred, axis=-1, keepdims=True)
    return (centred * lax.rsqrt(variance + 1e-05) * gain).astype(BF16)


CHUNKS = ((0, 192), (192, 576), (576, 1152))


def front_kernel(
    rows_ref, gain_ref, wb_ref, nq_ref, tile_ref, held_ref, gain_vm, wb_vm, sems
):
    copies = []
    for i, (begin, end) in enumerate(CHUNKS):
        part = pl.ds(begin, end - begin)
        copies.append(pltpu.make_async_copy(rows_ref.at[part], held_ref.at[part], sems.at[i]))
    gain_copy = pltpu.make_async_copy(gain_ref, gain_vm, sems.at[3])
    wb_copy = pltpu.make_async_copy(wb_ref, wb_vm, sems.at[4])
    copies[0].start()
    gain_copy.start()
    wb_copy.start()
    copies[1].start()
    copies[2].start()
    lane = lax.broadcasted_iota(jnp.int32, (KB, LANES), 1)
    place = jnp.where(lane < HEADS * KB, lax.rem(lane, KB), -1)
    gain_copy.wait()
    gain = gain_vm[...]
    wb_copy.wait()
    wb = wb_vm[...].astype(F32)
    spread_t = [jnp.broadcast_to(wb[h : h + 1, :], (KB, LANES)) for h in range(HEADS)]
    spread_t.append(jnp.zeros((LANES - HEADS * KB, LANES), F32))
    spread_t = jnp.concatenate(spread_t, axis=0).astype(BF16)
    total = jnp.zeros((KB, LANES), F32)
    for i, (begin, end) in enumerate(CHUNKS):
        copies[i].wait()
        normed = norm_rows(held_ref[begin:end, :], gain)
        if i == 0:
            nq_ref[...] = normed
        wide = nt_dot(normed, spread_t)
        for j in range(begin // KB, end // KB):
            row = j * KB - begin
            total = jnp.where(place == j % KB, wide[row : row + KB, :], total)
            if j % KB == KB - 1:
                tile_ref[j + 1 - KB : j + 1, :] = total


def copies_kernel(tile_ref, out_ref, sems):
    sends = []
    for r in range(NROW):
        send = pltpu.make_async_copy(tile_ref, out_ref.at[r], sems.at[r])
        send.start()
        sends.append(send)
    for send in sends:
        send.wait()


def relay_kernel(own_ref, first_ref, second_ref, third_ref, out_ref):
    for a in range(QROWS):
        span = slice(a * KB, (a + 1) * KB)
        refs = (own_ref, first_ref, second_ref, third_ref)
        parts = [ref[span, :].astype(F32) for ref in refs]
        out_ref[a * 96 : (a + 1) * 96, :] = jnp.concatenate(parts, axis=0).astype(BF16)


HALF_K = NROW * KB
GROUP = HEADS * KB


def join_kernel(third_ref, bias_ref, payload_ref, order_ref):
    rows = third_ref.shape[0]
    payload_ref[0:rows, :] = third_ref[...]
    col = lax.axis_index("col")
    core = lax.rem(col, 2)
    x = lax.rem(col // 2, 4)
    y_hi = col // 8
    place = 0
    rest = []
    for mask in MASKS:
        for y_mask in MASKS:
            slot = lax.bitwise_xor(y_hi, y_mask) * 4 + lax.bitwise_xor(x, mask)
            mine = pl.multiple_of((slot * 2 + core) * KB, 8)
            theirs = pl.multiple_of((slot * 2 + 1 - core) * KB, 8)
            order_ref[place : place + KB, :] = bias_ref[pl.ds(mine, KB), :]
            rest.append(bias_ref[pl.ds(theirs, KB), :])
            place += KB
    rest = jnp.concatenate(rest, axis=0)
    for term in range(3):
        part = rest.astype(BF16)
        rest = rest - part.astype(F32)
        begin = rows + term * HALF_K
        payload_ref[begin : begin + HALF_K, :] = part


def nt_dot(left, right):
    return lax.dot_general(left, right, (((1,), (1,)), ((), ())), preferred_element_type=F32)


def twice(block):
    zero = jnp.zeros_like(block)
    top = jnp.concatenate([block, zero], axis=1)
    return jnp.concatenate([top, jnp.concatenate([zero, block], axis=1)], axis=0)


def attend_kernel(
    own_ref, first_ref, second_ref, third_ref, theirs_a_ref, theirs_b_ref, order_ref,
    nq_ref, wq_ref, wkv_ref, wg_ref, wo_ref,
    out_ref, bias_ref, held_ref, gate_ref, gated_ref,
):
    sources = (
        own_ref, first_ref, second_ref, third_ref,
        theirs_a_ref.at[0], theirs_a_ref.at[1], theirs_a_ref.at[2], theirs_b_ref,
    )
    terms = []
    for term in range(3):
        begin = third_ref.shape[0] + term * HALF_K
        terms.append(theirs_b_ref[begin : begin + HALF_K, :].astype(F32))
    theirs = (terms[0] + terms[1]) + terms[2]
    for part in range(HALF_K // LANES):
        span = slice(part * LANES, (part + 1) * LANES)
        bias_ref[:, span] = order_ref[span, :].T[:GROUP, :]
        bias_ref[:, HALF_K + part * LANES : HALF_K + (part + 1) * LANES] = theirs[span, :].T[
            :GROUP, :
        ]
    nq = nq_ref[...]
    query = jnp.dot(nq, wq_ref[...], preferred_element_type=F32) * (1.0 / 32**0.5)
    query = query.astype(BF16).astype(F32)
    gate_ref[...] = jax.nn.sigmoid(jnp.dot(nq, wg_ref[...], preferred_element_type=F32))
    wk = twice(wkv_ref[:, :LANES].astype(F32)).astype(BF16)
    wv = twice(wkv_ref[:, LANES:].astype(F32)).astype(BF16)
    lane = lax.broadcasted_iota(jnp.int32, (KB, LANES), 1)
    zero = jnp.zeros((GROUP, LANES), F32)
    for i in range(QROWS // 2):
        sides = []
        masked = []
        for a in (2 * i, 2 * i + 1):
            sides.append(
                jnp.concatenate([ref[a * 96 : (a + 1) * 96, :] for ref in sources], axis=0)
            )
            q = query[a * KB : (a + 1) * KB, :]
            parts = [jnp.where(lane // 32 == h, q, 0.0) for h in range(HEADS)]
            masked.append(jnp.concatenate(parts, axis=0))
        queries = jnp.concatenate(
            [
                jnp.concatenate([masked[0], zero], axis=1),
                jnp.concatenate([zero, masked[1]], axis=1),
            ],
            axis=0,
        ).astype(BF16)
        rows = jnp.concatenate(sides, axis=1)
        keys = jnp.dot(rows, wk, preferred_element_type=F32).astype(BF16)
        values = jnp.dot(rows, wv, preferred_element_type=F32).astype(BF16)
        score = nt_dot(queries, keys)
        for n in range(2):
            a = 2 * i + n
            full = score[n * GROUP : (n + 1) * GROUP, :] + bias_ref[...]
            held_ref[a % 4] = full
            top = jnp.max(full, axis=1, keepdims=True)
            weights = jnp.exp(held_ref[a % 4] - top)
            total = jnp.sum(weights, axis=1, keepdims=True)
            high = weights.astype(BF16)
            low = (weights - high.astype(F32)).astype(BF16)
            both = jnp.dot(
                jnp.concatenate([high, low], axis=0),
                values[:, n * LANES : (n + 1) * LANES],
                preferred_element_type=F32,
            )
            attended = (both[:GROUP, :] + both[GROUP:, :]) / total
            mine = jnp.zeros((KB, LANES), F32)
            for h in range(HEADS):
                mine = jnp.where(lane // 32 == h, attended[h * KB : (h + 1) * KB, :], mine)
            span = slice(a * KB, (a + 1) * KB)
            gated_ref[span, :] = gate_ref[span, :] * mine
    out_ref[...] = jnp.dot(
        gated_ref[...].astype(BF16), wo_ref[...], preferred_element_type=F32
    ).astype(BF16)


def permute_col(value, target):
    return lax.ppermute(value, "col", [(c, target(c)) for c in range(NCOL)])


def permute_all(value, target):
    pairs = []
    for r in range(NROW):
        for c in range(NCOL):
            r2, c2 = target(r, c)
            pairs.append((r * NCOL + c, r2 * NCOL + c2))
    return lax.ppermute(value, ("row", "col"), pairs)


def near_y(mask):
    return lambda c: c ^ (mask * 8)


def near_x(mask):
    return lambda c: c ^ (mask * 2)


def body(pair, ln_gain, w_query, w_keyval, w_gate, w_bias, w_out):
    shape = jax.ShapeDtypeStruct
    rows = pair.reshape(-1, LANES)
    nrows = QROWS * KB
    nq, tile = pl.pallas_call(
        front_kernel,
        in_specs=[whole(pl.ANY)] * 3,
        out_specs=[whole(), whole()],
        out_shape=[shape((nrows, LANES), BF16), shape((2 * KB, LANES), F32)],
        scratch_shapes=[
            VM(rows.shape, BF16),
            VM((1, LANES), F32),
            VM((HEADS, LANES), BF16),
            pltpu.SemaphoreType.DMA((5,)),
        ],
        name="front",
    )(rows, ln_gain.reshape(1, LANES), w_bias.T)
    ys = [nq] + [permute_col(nq, near_y(mask)) for mask in MASKS[1:]]
    tile = permute_all(tile, lambda r, c: (c // 2, 2 * r + c % 2))
    small = pltpu.CompilerParams(vmem_limit_bytes=16 * 1024 * 1024)
    tiles = pl.pallas_call(
        copies_kernel,
        in_specs=[whole()],
        out_specs=whole(pl.ANY),
        out_shape=shape((NROW, 2 * KB, LANES), F32),
        scratch_shapes=[pltpu.SemaphoreType.DMA((NROW,))],
        compiler_params=small,
        cost_estimate=pl.CostEstimate(flops=20 * 10**9, bytes_accessed=0, transcendentals=0),
        name="copies",
    )(tile)
    bias = lax.all_to_all(tiles, "row", 0, 0)
    piece = pl.pallas_call(
        relay_kernel,
        in_specs=[whole()] * 4,
        out_specs=whole(),
        out_shape=shape((4 * nrows, LANES), BF16),
        compiler_params=small,
        cost_estimate=pl.CostEstimate(flops=30 * 10**9, bytes_accessed=0, transcendentals=0),
        name="relay",
    )(*ys)
    first = permute_col(piece, near_x(1))
    second = permute_col(piece, near_x(3))
    third = permute_col(first, near_x(3))
    mine = [piece, first, second, third]
    last, order = pl.pallas_call(
        join_kernel,
        in_specs=[whole()] * 2,
        out_specs=[whole()] * 2,
        out_shape=[
            shape((4 * nrows + 3 * HALF_K, LANES), BF16),
            shape((HALF_K, LANES), F32),
        ],
        compiler_params=small,
        name="join",
    )(third, bias.reshape(-1, LANES))
    theirs = [permute_col(value, lambda c: c ^ 1) for value in (jnp.stack(mine[:3]), last)]
    out = pl.pallas_call(
        attend_kernel,
        in_specs=[whole()] * 12,
        out_specs=whole(),
        out_shape=shape((nrows, LANES), BF16),
        scratch_shapes=[
            VM((GROUP, N_RES), F32),
            VM((4, GROUP, N_RES), F32),
            VM((nrows, LANES), F32),
            VM((nrows, LANES), F32),
        ],
        compiler_params=pltpu.CompilerParams(vmem_limit_bytes=32 * 1024 * 1024),
        name="attend",
    )(*mine, *theirs, order, nq, w_query, w_keyval, w_gate, w_out)
    return out.reshape(QROWS, KB, LANES)


def solution(mesh):
    placed = (P("row", "col", None), P(), P(), P(), P(), P(), P())
    return jax.shard_map(
        body, mesh=mesh, in_specs=placed, out_specs=P("row", "col", None), check_vma=False
    )
```

```python
import jax
import jax.numpy as jnp
from jax import lax
from jax.experimental import pallas as pl
from jax.experimental.pallas import tpu as pltpu
from jax.sharding import PartitionSpec as P

QROWS = 8
KB = 24
HEADS = 4
LANES = 128
NROW = 16
N_RES = 768
NCOL = 32
F32 = jnp.float32
BF16 = jnp.bfloat16
VM = pltpu.VMEM


def whole(space=VM):
    return pl.BlockSpec(memory_space=space)


MASKS = (0, 1, 3, 2)


def norm_rows(block, gain):
    values = block.astype(F32)
    mean = jnp.mean(values, axis=-1, keepdims=True)
    centred = values - mean
    variance = jnp.mean(centred * centred, axis=-1, keepdims=True)
    return (centred * lax.rsqrt(variance + 1e-05) * gain).astype(BF16)


CHUNKS = ((0, 192), (192, 576), (576, 1152))


def front_kernel(
    rows_ref, gain_ref, wb_ref, nq_ref, tile_ref, held_ref, gain_vm, wb_vm, sems
):
    copies = []
    for i, (begin, end) in enumerate(CHUNKS):
        part = pl.ds(begin, end - begin)
        copies.append(pltpu.make_async_copy(rows_ref.at[part], held_ref.at[part], sems.at[i]))
    gain_copy = pltpu.make_async_copy(gain_ref, gain_vm, sems.at[3])
    wb_copy = pltpu.make_async_copy(wb_ref, wb_vm, sems.at[4])
    copies[0].start()
    gain_copy.start()
    wb_copy.start()
    copies[1].start()
    copies[2].start()
    lane = lax.broadcasted_iota(jnp.int32, (KB, LANES), 1)
    place = jnp.where(lane < HEADS * KB, lax.rem(lane, KB), -1)
    gain_copy.wait()
    gain = gain_vm[...]
    wb_copy.wait()
    wb = wb_vm[...].astype(F32)
    spread_t = [jnp.broadcast_to(wb[h : h + 1, :], (KB, LANES)) for h in range(HEADS)]
    spread_t.append(jnp.zeros((LANES - HEADS * KB, LANES), F32))
    spread_t = jnp.concatenate(spread_t, axis=0).astype(BF16)
    total = jnp.zeros((KB, LANES), F32)
    for i, (begin, end) in enumerate(CHUNKS):
        copies[i].wait()
        normed = norm_rows(held_ref[begin:end, :], gain)
        if i == 0:
            nq_ref[...] = normed
        wide = nt_dot(normed, spread_t)
        for j in range(begin // KB, end // KB):
            row = j * KB - begin
            total = jnp.where(place == j % KB, wide[row : row + KB, :], total)
            if j % KB == KB - 1:
                tile_ref[j + 1 - KB : j + 1, :] = total


def copies_kernel(tile_ref, out_ref, sems):
    sends = []
    for r in range(NROW):
        send = pltpu.make_async_copy(tile_ref, out_ref.at[r], sems.at[r])
        send.start()
        sends.append(send)
    for send in sends:
        send.wait()


def relay_kernel(own_ref, near_ref, far_ref, out_ref):
    for a in range(QROWS):
        span = slice(a * KB, (a + 1) * KB)
        refs = (own_ref, near_ref, far_ref.at[0], far_ref.at[1])
        parts = [ref[span, :].astype(F32) for ref in refs]
        out_ref[a * 96 : (a + 1) * 96, :] = jnp.concatenate(parts, axis=0).astype(BF16)


HALF_K = NROW * KB
GROUP = HEADS * KB


def join_kernel(third_ref, bias_ref, payload_ref, order_ref):
    rows = third_ref.shape[0]
    payload_ref[0:rows, :] = third_ref[...]
    col = lax.axis_index("col")
    core = lax.rem(col, 2)
    x = lax.rem(col // 2, 4)
    y_hi = col // 8
    place = 0
    rest = []
    for mask in MASKS:
        for y_mask in MASKS:
            slot = lax.bitwise_xor(y_hi, y_mask) * 4 + lax.bitwise_xor(x, mask)
            mine = pl.multiple_of((slot * 2 + core) * KB, 8)
            theirs = pl.multiple_of((slot * 2 + 1 - core) * KB, 8)
            order_ref[place : place + KB, :] = bias_ref[pl.ds(mine, KB), :]
            rest.append(bias_ref[pl.ds(theirs, KB), :])
            place += KB
    rest = jnp.concatenate(rest, axis=0)
    for term in range(3):
        part = rest.astype(BF16)
        rest = rest - part.astype(F32)
        begin = rows + term * HALF_K
        payload_ref[begin : begin + HALF_K, :] = part


def nt_dot(left, right):
    return lax.dot_general(left, right, (((1,), (1,)), ((), ())), preferred_element_type=F32)


def twice(block):
    zero = jnp.zeros_like(block)
    top = jnp.concatenate([block, zero], axis=1)
    return jnp.concatenate([top, jnp.concatenate([zero, block], axis=1)], axis=0)


def attend_kernel(
    own_ref, first_ref, second_ref, third_ref, theirs_a_ref, theirs_b_ref, order_ref,
    nq_ref, wq_ref, wkv_ref, wg_ref, wo_ref,
    out_ref, bias_ref, held_ref, gate_ref, gated_ref,
):
    sources = (
        own_ref, first_ref, second_ref, third_ref,
        theirs_a_ref.at[0], theirs_a_ref.at[1], theirs_a_ref.at[2], theirs_b_ref,
    )
    terms = []
    for term in range(3):
        begin = third_ref.shape[0] + term * HALF_K
        terms.append(theirs_b_ref[begin : begin + HALF_K, :].astype(F32))
    theirs = (terms[0] + terms[1]) + terms[2]
    for part in range(HALF_K // LANES):
        span = slice(part * LANES, (part + 1) * LANES)
        bias_ref[:, span] = order_ref[span, :].T[:GROUP, :]
        bias_ref[:, HALF_K + part * LANES : HALF_K + (part + 1) * LANES] = theirs[span, :].T[
            :GROUP, :
        ]
    nq = nq_ref[...]
    query = jnp.dot(nq, wq_ref[...], preferred_element_type=F32) * (1.0 / 32**0.5)
    query = query.astype(BF16).astype(F32)
    gate_ref[...] = jax.nn.sigmoid(jnp.dot(nq, wg_ref[...], preferred_element_type=F32))
    wk = twice(wkv_ref[:, :LANES].astype(F32)).astype(BF16)
    wv = twice(wkv_ref[:, LANES:].astype(F32)).astype(BF16)
    lane = lax.broadcasted_iota(jnp.int32, (KB, LANES), 1)
    zero = jnp.zeros((GROUP, LANES), F32)
    for i in range(QROWS // 2):
        sides = []
        masked = []
        for a in (2 * i, 2 * i + 1):
            sides.append(
                jnp.concatenate([ref[a * 96 : (a + 1) * 96, :] for ref in sources], axis=0)
            )
            q = query[a * KB : (a + 1) * KB, :]
            parts = [jnp.where(lane // 32 == h, q, 0.0) for h in range(HEADS)]
            masked.append(jnp.concatenate(parts, axis=0))
        queries = jnp.concatenate(
            [
                jnp.concatenate([masked[0], zero], axis=1),
                jnp.concatenate([zero, masked[1]], axis=1),
            ],
            axis=0,
        ).astype(BF16)
        rows = jnp.concatenate(sides, axis=1)
        keys = jnp.dot(rows, wk, preferred_element_type=F32).astype(BF16)
        values = jnp.dot(rows, wv, preferred_element_type=F32).astype(BF16)
        score = nt_dot(queries, keys)
        for n in range(2):
            a = 2 * i + n
            full = score[n * GROUP : (n + 1) * GROUP, :] + bias_ref[...]
            held_ref[a % 4] = full
            top = jnp.max(full, axis=1, keepdims=True)
            weights = jnp.exp(held_ref[a % 4] - top)
            total = jnp.sum(weights, axis=1, keepdims=True)
            high = weights.astype(BF16)
            low = (weights - high.astype(F32)).astype(BF16)
            both = jnp.dot(
                jnp.concatenate([high, low], axis=0),
                values[:, n * LANES : (n + 1) * LANES],
                preferred_element_type=F32,
            )
            attended = (both[:GROUP, :] + both[GROUP:, :]) / total
            mine = jnp.zeros((KB, LANES), F32)
            for h in range(HEADS):
                mine = jnp.where(lane // 32 == h, attended[h * KB : (h + 1) * KB, :], mine)
            span = slice(a * KB, (a + 1) * KB)
            gated_ref[span, :] = gate_ref[span, :] * mine
    out_ref[...] = jnp.dot(
        gated_ref[...].astype(BF16), wo_ref[...], preferred_element_type=F32
    ).astype(BF16)


def permute_col(value, target):
    return lax.ppermute(value, "col", [(c, target(c)) for c in range(NCOL)])


def permute_all(value, target):
    pairs = []
    for r in range(NROW):
        for c in range(NCOL):
            r2, c2 = target(r, c)
            pairs.append((r * NCOL + c, r2 * NCOL + c2))
    return lax.ppermute(value, ("row", "col"), pairs)


def near_y(mask):
    return lambda c: c ^ (mask * 8)


def near_x(mask):
    return lambda c: c ^ (mask * 2)


def body(pair, ln_gain, w_query, w_keyval, w_gate, w_bias, w_out):
    shape = jax.ShapeDtypeStruct
    rows = pair.reshape(-1, LANES)
    nrows = QROWS * KB
    nq, tile = pl.pallas_call(
        front_kernel,
        in_specs=[whole(pl.ANY)] * 3,
        out_specs=[whole(), whole()],
        out_shape=[shape((nrows, LANES), BF16), shape((2 * KB, LANES), F32)],
        scratch_shapes=[
            VM(rows.shape, BF16),
            VM((1, LANES), F32),
            VM((HEADS, LANES), BF16),
            pltpu.SemaphoreType.DMA((5,)),
        ],
        name="front",
    )(rows, ln_gain.reshape(1, LANES), w_bias.T)
    near = permute_col(nq, near_y(1))
    far = permute_col(jnp.stack([nq, near]), near_y(3))
    tile = permute_all(tile, lambda r, c: (c // 2, 2 * r + c % 2))
    small = pltpu.CompilerParams(vmem_limit_bytes=16 * 1024 * 1024)
    tiles = pl.pallas_call(
        copies_kernel,
        in_specs=[whole()],
        out_specs=whole(pl.ANY),
        out_shape=shape((NROW, 2 * KB, LANES), F32),
        scratch_shapes=[pltpu.SemaphoreType.DMA((NROW,))],
        compiler_params=small,
        cost_estimate=pl.CostEstimate(flops=20 * 10**9, bytes_accessed=0, transcendentals=0),
        name="copies",
    )(tile)
    bias = lax.all_to_all(tiles, "row", 0, 0)
    piece = pl.pallas_call(
        relay_kernel,
        in_specs=[whole()] * 3,
        out_specs=whole(),
        out_shape=shape((4 * nrows, LANES), BF16),
        compiler_params=small,
        cost_estimate=pl.CostEstimate(flops=30 * 10**9, bytes_accessed=0, transcendentals=0),
        name="relay",
    )(nq, near, far)
    first = permute_col(piece, near_x(1))
    second = permute_col(piece, near_x(3))
    third = permute_col(first, near_x(3))
    mine = [piece, first, second, third]
    last, order = pl.pallas_call(
        join_kernel,
        in_specs=[whole()] * 2,
        out_specs=[whole()] * 2,
        out_shape=[
            shape((4 * nrows + 3 * HALF_K, LANES), BF16),
            shape((HALF_K, LANES), F32),
        ],
        compiler_params=small,
        name="join",
    )(third, bias.reshape(-1, LANES))
    theirs = [permute_col(value, lambda c: c ^ 1) for value in (jnp.stack(mine[:3]), last)]
    out = pl.pallas_call(
        attend_kernel,
        in_specs=[whole()] * 12,
        out_specs=whole(),
        out_shape=shape((nrows, LANES), BF16),
        scratch_shapes=[
            VM((GROUP, N_RES), F32),
            VM((4, GROUP, N_RES), F32),
            VM((nrows, LANES), F32),
            VM((nrows, LANES), F32),
        ],
        compiler_params=pltpu.CompilerParams(vmem_limit_bytes=32 * 1024 * 1024),
        name="attend",
    )(*mine, *theirs, order, nq, w_query, w_keyval, w_gate, w_out)
    return out.reshape(QROWS, KB, LANES)


def solution(mesh):
    placed = (P("row", "col", None), P(), P(), P(), P(), P(), P())
    return jax.shard_map(
        body, mesh=mesh, in_specs=placed, out_specs=P("row", "col", None), check_vma=False
    )
```

```python
import jax
import jax.numpy as jnp
from jax import lax
from jax.experimental import pallas as pl
from jax.experimental.pallas import tpu as pltpu
from jax.sharding import PartitionSpec as P

QROWS = 8
KB = 24
HEADS = 4
LANES = 128
NROW = 16
N_RES = 768
NCOL = 32
F32 = jnp.float32
BF16 = jnp.bfloat16
VM = pltpu.VMEM


def whole(space=VM):
    return pl.BlockSpec(memory_space=space)


MASKS = (0, 1, 3, 2)


def norm_rows(block, gain):
    values = block.astype(F32)
    mean = jnp.mean(values, axis=-1, keepdims=True)
    centred = values - mean
    variance = jnp.mean(centred * centred, axis=-1, keepdims=True)
    return (centred * lax.rsqrt(variance + 1e-05) * gain).astype(BF16)


CHUNKS = ((0, 192), (192, 576), (576, 1152))


def front_kernel(
    rows_ref, gain_ref, wb_ref, nq_ref, tile_ref, held_ref, gain_vm, wb_vm, sems
):
    copies = []
    for i, (begin, end) in enumerate(CHUNKS):
        part = pl.ds(begin, end - begin)
        copies.append(pltpu.make_async_copy(rows_ref.at[part], held_ref.at[part], sems.at[i]))
    gain_copy = pltpu.make_async_copy(gain_ref, gain_vm, sems.at[3])
    wb_copy = pltpu.make_async_copy(wb_ref, wb_vm, sems.at[4])
    copies[0].start()
    gain_copy.start()
    wb_copy.start()
    copies[1].start()
    copies[2].start()
    lane = lax.broadcasted_iota(jnp.int32, (KB, LANES), 1)
    place = jnp.where(lane < HEADS * KB, lax.rem(lane, KB), -1)
    gain_copy.wait()
    gain = gain_vm[...]
    wb_copy.wait()
    wb = wb_vm[...].astype(F32)
    spread_t = [jnp.broadcast_to(wb[h : h + 1, :], (KB, LANES)) for h in range(HEADS)]
    spread_t.append(jnp.zeros((LANES - HEADS * KB, LANES), F32))
    spread_t = jnp.concatenate(spread_t, axis=0).astype(BF16)
    total = jnp.zeros((KB, LANES), F32)
    for i, (begin, end) in enumerate(CHUNKS):
        copies[i].wait()
        normed = norm_rows(held_ref[begin:end, :], gain)
        if i == 0:
            nq_ref[...] = normed
        wide = nt_dot(normed, spread_t)
        for j in range(begin // KB, end // KB):
            row = j * KB - begin
            total = jnp.where(place == j % KB, wide[row : row + KB, :], total)
            if j % KB == KB - 1:
                tile_ref[j + 1 - KB : j + 1, :] = total


def copies_kernel(tile_ref, out_ref, sems):
    sends = []
    for r in range(NROW):
        send = pltpu.make_async_copy(tile_ref, out_ref.at[r], sems.at[r])
        send.start()
        sends.append(send)
    for send in sends:
        send.wait()


def relay_kernel(own_ref, first_ref, second_ref, third_ref, out_ref):
    for a in range(QROWS):
        span = slice(a * KB, (a + 1) * KB)
        refs = (own_ref, first_ref, second_ref, third_ref)
        parts = [ref[span, :].astype(F32) for ref in refs]
        out_ref[a * 96 : (a + 1) * 96, :] = jnp.concatenate(parts, axis=0).astype(BF16)


HALF_K = NROW * KB
GROUP = HEADS * KB


def join_kernel(third_ref, bias_ref, payload_ref, order_ref):
    rows = third_ref.shape[0]
    payload_ref[0:rows, :] = third_ref[...]
    col = lax.axis_index("col")
    core = lax.rem(col, 2)
    x = lax.rem(col // 2, 4)
    y_hi = col // 8
    place = 0
    rest = []
    for mask in (0, 1 + 2 * core, 3 - 2 * core, 2):
        for y_mask in MASKS:
            slot = lax.bitwise_xor(y_hi, y_mask) * 4 + lax.bitwise_xor(x, mask)
            mine = pl.multiple_of((slot * 2 + core) * KB, 8)
            theirs = pl.multiple_of((slot * 2 + 1 - core) * KB, 8)
            order_ref[place : place + KB, :] = bias_ref[pl.ds(mine, KB), :]
            rest.append(bias_ref[pl.ds(theirs, KB), :])
            place += KB
    rest = jnp.concatenate(rest, axis=0)
    for term in range(3):
        part = rest.astype(BF16)
        rest = rest - part.astype(F32)
        begin = rows + term * HALF_K
        payload_ref[begin : begin + HALF_K, :] = part


def nt_dot(left, right):
    return lax.dot_general(left, right, (((1,), (1,)), ((), ())), preferred_element_type=F32)


def twice(block):
    zero = jnp.zeros_like(block)
    top = jnp.concatenate([block, zero], axis=1)
    return jnp.concatenate([top, jnp.concatenate([zero, block], axis=1)], axis=0)


def attend_kernel(
    own_ref, first_ref, second_ref, third_ref, theirs_a_ref, theirs_b_ref, order_ref,
    nq_ref, wq_ref, wkv_ref, wg_ref, wo_ref,
    out_ref, bias_ref, held_ref, gate_ref, gated_ref,
):
    sources = (
        own_ref, first_ref, second_ref, third_ref,
        theirs_a_ref.at[0], theirs_a_ref.at[1], theirs_a_ref.at[2], theirs_b_ref,
    )
    terms = []
    for term in range(3):
        begin = third_ref.shape[0] + term * HALF_K
        terms.append(theirs_b_ref[begin : begin + HALF_K, :].astype(F32))
    theirs = (terms[0] + terms[1]) + terms[2]
    for part in range(HALF_K // LANES):
        span = slice(part * LANES, (part + 1) * LANES)
        bias_ref[:, span] = order_ref[span, :].T[:GROUP, :]
        bias_ref[:, HALF_K + part * LANES : HALF_K + (part + 1) * LANES] = theirs[span, :].T[
            :GROUP, :
        ]
    nq = nq_ref[...]
    query = jnp.dot(nq, wq_ref[...], preferred_element_type=F32) * (1.0 / 32**0.5)
    query = query.astype(BF16).astype(F32)
    gate_ref[...] = jax.nn.sigmoid(jnp.dot(nq, wg_ref[...], preferred_element_type=F32))
    wk = twice(wkv_ref[:, :LANES].astype(F32)).astype(BF16)
    wv = twice(wkv_ref[:, LANES:].astype(F32)).astype(BF16)
    lane = lax.broadcasted_iota(jnp.int32, (KB, LANES), 1)
    zero = jnp.zeros((GROUP, LANES), F32)
    for i in range(QROWS // 2):
        sides = []
        masked = []
        for a in (2 * i, 2 * i + 1):
            sides.append(
                jnp.concatenate([ref[a * 96 : (a + 1) * 96, :] for ref in sources], axis=0)
            )
            q = query[a * KB : (a + 1) * KB, :]
            parts = [jnp.where(lane // 32 == h, q, 0.0) for h in range(HEADS)]
            masked.append(jnp.concatenate(parts, axis=0))
        queries = jnp.concatenate(
            [
                jnp.concatenate([masked[0], zero], axis=1),
                jnp.concatenate([zero, masked[1]], axis=1),
            ],
            axis=0,
        ).astype(BF16)
        rows = jnp.concatenate(sides, axis=1)
        keys = jnp.dot(rows, wk, preferred_element_type=F32).astype(BF16)
        values = jnp.dot(rows, wv, preferred_element_type=F32).astype(BF16)
        score = nt_dot(queries, keys)
        for n in range(2):
            a = 2 * i + n
            full = score[n * GROUP : (n + 1) * GROUP, :] + bias_ref[...]
            held_ref[a % 4] = full
            top = jnp.max(full, axis=1, keepdims=True)
            weights = jnp.exp(held_ref[a % 4] - top)
            total = jnp.sum(weights, axis=1, keepdims=True)
            high = weights.astype(BF16)
            low = (weights - high.astype(F32)).astype(BF16)
            both = jnp.dot(
                jnp.concatenate([high, low], axis=0),
                values[:, n * LANES : (n + 1) * LANES],
                preferred_element_type=F32,
            )
            attended = (both[:GROUP, :] + both[GROUP:, :]) / total
            mine = jnp.zeros((KB, LANES), F32)
            for h in range(HEADS):
                mine = jnp.where(lane // 32 == h, attended[h * KB : (h + 1) * KB, :], mine)
            span = slice(a * KB, (a + 1) * KB)
            gated_ref[span, :] = gate_ref[span, :] * mine
    out_ref[...] = jnp.dot(
        gated_ref[...].astype(BF16), wo_ref[...], preferred_element_type=F32
    ).astype(BF16)


def permute_col(value, target):
    return lax.ppermute(value, "col", [(c, target(c)) for c in range(NCOL)])


def permute_all(value, target):
    pairs = []
    for r in range(NROW):
        for c in range(NCOL):
            r2, c2 = target(r, c)
            pairs.append((r * NCOL + c, r2 * NCOL + c2))
    return lax.ppermute(value, ("row", "col"), pairs)


def near_y(mask):
    return lambda c: c ^ (mask * 8)


def ring_x(step):
    return lambda c: c ^ (2 * ((1, 3)[(c + step) % 2]))


def body(pair, ln_gain, w_query, w_keyval, w_gate, w_bias, w_out):
    shape = jax.ShapeDtypeStruct
    rows = pair.reshape(-1, LANES)
    nrows = QROWS * KB
    nq, tile = pl.pallas_call(
        front_kernel,
        in_specs=[whole(pl.ANY)] * 3,
        out_specs=[whole(), whole()],
        out_shape=[shape((nrows, LANES), BF16), shape((2 * KB, LANES), F32)],
        scratch_shapes=[
            VM(rows.shape, BF16),
            VM((1, LANES), F32),
            VM((HEADS, LANES), BF16),
            pltpu.SemaphoreType.DMA((5,)),
        ],
        name="front",
    )(rows, ln_gain.reshape(1, LANES), w_bias.T)
    ys = [nq] + [permute_col(nq, near_y(mask)) for mask in MASKS[1:]]
    tile = permute_all(tile, lambda r, c: (c // 2, 2 * r + c % 2))
    small = pltpu.CompilerParams(vmem_limit_bytes=16 * 1024 * 1024)
    tiles = pl.pallas_call(
        copies_kernel,
        in_specs=[whole()],
        out_specs=whole(pl.ANY),
        out_shape=shape((NROW, 2 * KB, LANES), F32),
        scratch_shapes=[pltpu.SemaphoreType.DMA((NROW,))],
        compiler_params=small,
        cost_estimate=pl.CostEstimate(flops=20 * 10**9, bytes_accessed=0, transcendentals=0),
        name="copies",
    )(tile)
    bias = lax.all_to_all(tiles, "row", 0, 0)
    piece = pl.pallas_call(
        relay_kernel,
        in_specs=[whole()] * 4,
        out_specs=whole(),
        out_shape=shape((4 * nrows, LANES), BF16),
        compiler_params=small,
        cost_estimate=pl.CostEstimate(flops=30 * 10**9, bytes_accessed=0, transcendentals=0),
        name="relay",
    )(*ys)
    first = permute_col(piece, ring_x(0))
    second = permute_col(piece, ring_x(1))
    third = permute_col(first, ring_x(1))
    mine = [piece, first, second, third]
    last, order = pl.pallas_call(
        join_kernel,
        in_specs=[whole()] * 2,
        out_specs=[whole()] * 2,
        out_shape=[
            shape((4 * nrows + 3 * HALF_K, LANES), BF16),
            shape((HALF_K, LANES), F32),
        ],
        compiler_params=small,
        name="join",
    )(third, bias.reshape(-1, LANES))
    theirs = [permute_col(value, lambda c: c ^ 1) for value in (jnp.stack(mine[:3]), last)]
    out = pl.pallas_call(
        attend_kernel,
        in_specs=[whole()] * 12,
        out_specs=whole(),
        out_shape=shape((nrows, LANES), BF16),
        scratch_shapes=[
            VM((GROUP, N_RES), F32),
            VM((4, GROUP, N_RES), F32),
            VM((nrows, LANES), F32),
            VM((nrows, LANES), F32),
        ],
        compiler_params=pltpu.CompilerParams(vmem_limit_bytes=32 * 1024 * 1024),
        name="attend",
    )(*mine, *theirs, order, nq, w_query, w_keyval, w_gate, w_out)
    return out.reshape(QROWS, KB, LANES)


def solution(mesh):
    placed = (P("row", "col", None), P(), P(), P(), P(), P(), P())
    return jax.shard_map(
        body, mesh=mesh, in_specs=placed, out_specs=P("row", "col", None), check_vma=False
    )
```

```python
import jax
import jax.numpy as jnp
from jax import lax
from jax.experimental import pallas as pl
from jax.experimental.pallas import tpu as pltpu
from jax.sharding import PartitionSpec as P

QROWS = 8
KB = 24
HEADS = 4
LANES = 128
NROW = 16
N_RES = 768
NCOL = 32
F32 = jnp.float32
BF16 = jnp.bfloat16
VM = pltpu.VMEM


def whole(space=VM):
    return pl.BlockSpec(memory_space=space)


MASKS = (0, 1, 3, 2)


def norm_rows(block, gain):
    values = block.astype(F32)
    mean = jnp.mean(values, axis=-1, keepdims=True)
    centred = values - mean
    variance = jnp.mean(centred * centred, axis=-1, keepdims=True)
    return (centred * lax.rsqrt(variance + 1e-05) * gain).astype(BF16)


CHUNKS = ((0, 192), (192, 576), (576, 1152))


def front_kernel(
    rows_ref, gain_ref, wb_ref, nq_ref, tile_ref, held_ref, gain_vm, wb_vm, sems
):
    copies = []
    for i, (begin, end) in enumerate(CHUNKS):
        part = pl.ds(begin, end - begin)
        copies.append(pltpu.make_async_copy(rows_ref.at[part], held_ref.at[part], sems.at[i]))
    gain_copy = pltpu.make_async_copy(gain_ref, gain_vm, sems.at[3])
    wb_copy = pltpu.make_async_copy(wb_ref, wb_vm, sems.at[4])
    copies[0].start()
    gain_copy.start()
    wb_copy.start()
    copies[1].start()
    copies[2].start()
    lane = lax.broadcasted_iota(jnp.int32, (KB, LANES), 1)
    place = jnp.where(lane < HEADS * KB, lax.rem(lane, KB), -1)
    gain_copy.wait()
    gain = gain_vm[...]
    wb_copy.wait()
    wb = wb_vm[...].astype(F32)
    spread_t = [jnp.broadcast_to(wb[h : h + 1, :], (KB, LANES)) for h in range(HEADS)]
    spread_t.append(jnp.zeros((LANES - HEADS * KB, LANES), F32))
    spread_t = jnp.concatenate(spread_t, axis=0).astype(BF16)
    total = jnp.zeros((KB, LANES), F32)
    for i, (begin, end) in enumerate(CHUNKS):
        copies[i].wait()
        normed = norm_rows(held_ref[begin:end, :], gain)
        if i == 0:
            nq_ref[...] = normed
        wide = nt_dot(normed, spread_t)
        for j in range(begin // KB, end // KB):
            row = j * KB - begin
            total = jnp.where(place == j % KB, wide[row : row + KB, :], total)
            if j % KB == KB - 1:
                tile_ref[j + 1 - KB : j + 1, :] = total


def copies_kernel(tile_ref, out_ref, sems):
    sends = []
    for r in range(NROW):
        send = pltpu.make_async_copy(tile_ref, out_ref.at[r], sems.at[r])
        send.start()
        sends.append(send)
    for send in sends:
        send.wait()


def relay_kernel(own_ref, first_ref, second_ref, third_ref, out_ref):
    for a in range(QROWS):
        span = slice(a * KB, (a + 1) * KB)
        refs = (own_ref, first_ref, second_ref, third_ref)
        parts = [ref[span, :].astype(F32) for ref in refs]
        out_ref[a * 96 : (a + 1) * 96, :] = jnp.concatenate(parts, axis=0).astype(BF16)


HALF_K = NROW * KB
GROUP = HEADS * KB


def join_kernel(third_ref, bias_ref, payload_ref, order_ref):
    rows = third_ref.shape[0]
    payload_ref[0:rows, :] = third_ref[...]
    col = lax.axis_index("col")
    core = lax.rem(col, 2)
    x = lax.rem(col // 2, 4)
    y_hi = col // 8
    place = 0
    rest = []
    for mask in MASKS:
        for y_mask in MASKS:
            slot = lax.bitwise_xor(y_hi, y_mask) * 4 + lax.bitwise_xor(x, mask)
            mine = pl.multiple_of((slot * 2 + core) * KB, 8)
            theirs = pl.multiple_of((slot * 2 + 1 - core) * KB, 8)
            order_ref[place : place + KB, :] = bias_ref[pl.ds(mine, KB), :]
            rest.append(bias_ref[pl.ds(theirs, KB), :])
            place += KB
    rest = jnp.concatenate(rest, axis=0)
    for term in range(3):
        part = rest.astype(BF16)
        rest = rest - part.astype(F32)
        begin = rows + term * HALF_K
        payload_ref[begin : begin + HALF_K, :] = part


def nt_dot(left, right):
    return lax.dot_general(left, right, (((1,), (1,)), ((), ())), preferred_element_type=F32)


def twice(block):
    zero = jnp.zeros_like(block)
    top = jnp.concatenate([block, zero], axis=1)
    return jnp.concatenate([top, jnp.concatenate([zero, block], axis=1)], axis=0)


def attend_kernel(
    own_ref, first_ref, second_ref, third_ref, theirs_a_ref, theirs_b_ref, order_ref,
    nq_ref, wq_ref, wkv_ref, wg_ref, wo_ref,
    out_ref, bias_ref, held_ref, gate_ref, gated_ref,
):
    sources = (
        own_ref, first_ref, second_ref, third_ref,
        theirs_a_ref.at[0], theirs_a_ref.at[1], theirs_a_ref.at[2], theirs_b_ref,
    )
    terms = []
    for term in range(3):
        begin = third_ref.shape[0] + term * HALF_K
        terms.append(theirs_b_ref[begin : begin + HALF_K, :].astype(F32))
    theirs = (terms[0] + terms[1]) + terms[2]
    for part in range(HALF_K // LANES):
        span = slice(part * LANES, (part + 1) * LANES)
        bias_ref[:, span] = order_ref[span, :].T[:GROUP, :]
        bias_ref[:, HALF_K + part * LANES : HALF_K + (part + 1) * LANES] = theirs[span, :].T[
            :GROUP, :
        ]
    nq = nq_ref[...]
    query = jnp.dot(nq, wq_ref[...], preferred_element_type=F32) * (1.0 / 32**0.5)
    query = query.astype(BF16).astype(F32)
    gate_ref[...] = jax.nn.sigmoid(jnp.dot(nq, wg_ref[...], preferred_element_type=F32))
    wk = twice(wkv_ref[:, :LANES].astype(F32)).astype(BF16)
    wv = twice(wkv_ref[:, LANES:].astype(F32)).astype(BF16)
    lane = lax.broadcasted_iota(jnp.int32, (KB, LANES), 1)
    zero = jnp.zeros((GROUP, LANES), F32)
    for i in range(QROWS // 2):
        sides = []
        masked = []
        for a in (2 * i, 2 * i + 1):
            sides.append(
                jnp.concatenate([ref[a * 96 : (a + 1) * 96, :] for ref in sources], axis=0)
            )
            q = query[a * KB : (a + 1) * KB, :]
            parts = [jnp.where(lane // 32 == h, q, 0.0) for h in range(HEADS)]
            masked.append(jnp.concatenate(parts, axis=0))
        queries = jnp.concatenate(
            [
                jnp.concatenate([masked[0], zero], axis=1),
                jnp.concatenate([zero, masked[1]], axis=1),
            ],
            axis=0,
        ).astype(BF16)
        rows = jnp.concatenate(sides, axis=1)
        keys = jnp.dot(rows, wk, preferred_element_type=F32).astype(BF16)
        values = jnp.dot(rows, wv, preferred_element_type=F32).astype(BF16)
        score = nt_dot(queries, keys)
        for n in range(2):
            a = 2 * i + n
            full = score[n * GROUP : (n + 1) * GROUP, :] + bias_ref[...]
            held_ref[a % 4] = full
            top = jnp.max(full, axis=1, keepdims=True)
            weights = jnp.exp(held_ref[a % 4] - top)
            total = jnp.sum(weights, axis=1, keepdims=True)
            high = weights.astype(BF16)
            low = (weights - high.astype(F32)).astype(BF16)
            both = jnp.dot(
                jnp.concatenate([high, low], axis=0),
                values[:, n * LANES : (n + 1) * LANES],
                preferred_element_type=F32,
            )
            attended = (both[:GROUP, :] + both[GROUP:, :]) / total
            mine = jnp.zeros((KB, LANES), F32)
            for h in range(HEADS):
                mine = jnp.where(lane // 32 == h, attended[h * KB : (h + 1) * KB, :], mine)
            span = slice(a * KB, (a + 1) * KB)
            gated_ref[span, :] = gate_ref[span, :] * mine
    out_ref[...] = jnp.dot(
        gated_ref[...].astype(BF16), wo_ref[...], preferred_element_type=F32
    ).astype(BF16)


def permute_col(value, target):
    return lax.ppermute(value, "col", [(c, target(c)) for c in range(NCOL)])


def permute_all(value, target):
    pairs = []
    for r in range(NROW):
        for c in range(NCOL):
            r2, c2 = target(r, c)
            pairs.append((r * NCOL + c, r2 * NCOL + c2))
    return lax.ppermute(value, ("row", "col"), pairs)


def near_y(mask):
    return lambda c: c ^ (mask * 8)


def near_x(mask):
    return lambda c: c ^ (mask * 2)


def body(pair, ln_gain, w_query, w_keyval, w_gate, w_bias, w_out):
    shape = jax.ShapeDtypeStruct
    rows = pair.reshape(-1, LANES)
    nrows = QROWS * KB
    nq, tile = pl.pallas_call(
        front_kernel,
        in_specs=[whole(pl.ANY)] * 3,
        out_specs=[whole(), whole()],
        out_shape=[shape((nrows, LANES), BF16), shape((2 * KB, LANES), F32)],
        scratch_shapes=[
            VM(rows.shape, BF16),
            VM((1, LANES), F32),
            VM((HEADS, LANES), BF16),
            pltpu.SemaphoreType.DMA((5,)),
        ],
        name="front",
    )(rows, ln_gain.reshape(1, LANES), w_bias.T)
    ys = [nq] + [permute_col(nq, near_y(mask)) for mask in MASKS[1:]]
    tile = permute_all(tile, lambda r, c: (c // 2, 2 * r + c % 2))
    small = pltpu.CompilerParams(vmem_limit_bytes=16 * 1024 * 1024)
    tiles = pl.pallas_call(
        copies_kernel,
        in_specs=[whole()],
        out_specs=whole(pl.ANY),
        out_shape=shape((NROW, 2 * KB, LANES), F32),
        scratch_shapes=[pltpu.SemaphoreType.DMA((NROW,))],
        compiler_params=small,
        cost_estimate=pl.CostEstimate(flops=20 * 10**9, bytes_accessed=0, transcendentals=0),
        name="copies",
    )(tile)
    bias = lax.all_to_all(tiles, "row", 0, 0)
    piece = pl.pallas_call(
        relay_kernel,
        in_specs=[whole()] * 4,
        out_specs=whole(),
        out_shape=shape((4 * nrows, LANES), BF16),
        compiler_params=small,
        cost_estimate=pl.CostEstimate(flops=30 * 10**9, bytes_accessed=0, transcendentals=0),
        name="relay",
    )(*ys)
    first = permute_col(piece, near_x(1))
    second = permute_col(piece, near_x(3))
    third = permute_col(piece, near_x(2))
    mine = [piece, first, second, third]
    last, order = pl.pallas_call(
        join_kernel,
        in_specs=[whole()] * 2,
        out_specs=[whole()] * 2,
        out_shape=[
            shape((4 * nrows + 3 * HALF_K, LANES), BF16),
            shape((HALF_K, LANES), F32),
        ],
        compiler_params=small,
        name="join",
    )(third, bias.reshape(-1, LANES))
    theirs = [permute_col(value, lambda c: c ^ 1) for value in (jnp.stack(mine[:3]), last)]
    out = pl.pallas_call(
        attend_kernel,
        in_specs=[whole()] * 12,
        out_specs=whole(),
        out_shape=shape((nrows, LANES), BF16),
        scratch_shapes=[
            VM((GROUP, N_RES), F32),
            VM((4, GROUP, N_RES), F32),
            VM((nrows, LANES), F32),
            VM((nrows, LANES), F32),
        ],
        compiler_params=pltpu.CompilerParams(vmem_limit_bytes=32 * 1024 * 1024),
        name="attend",
    )(*mine, *theirs, order, nq, w_query, w_keyval, w_gate, w_out)
    return out.reshape(QROWS, KB, LANES)


def solution(mesh):
    placed = (P("row", "col", None), P(), P(), P(), P(), P(), P())
    return jax.shard_map(
        body, mesh=mesh, in_specs=placed, out_specs=P("row", "col", None), check_vma=False
    )
```

```python
import jax
import jax.numpy as jnp
from jax import lax
from jax.experimental import pallas as pl
from jax.experimental.pallas import tpu as pltpu
from jax.sharding import PartitionSpec as P

QROWS = 8
KB = 24
HEADS = 4
LANES = 128
NROW = 16
N_RES = 768
NCOL = 32
F32 = jnp.float32
BF16 = jnp.bfloat16
VM = pltpu.VMEM


def whole(space=VM):
    return pl.BlockSpec(memory_space=space)


MASKS = (0, 1, 3, 2)


def norm_rows(block, gain):
    values = block.astype(F32)
    mean = jnp.mean(values, axis=-1, keepdims=True)
    centred = values - mean
    variance = jnp.mean(centred * centred, axis=-1, keepdims=True)
    return (centred * lax.rsqrt(variance + 1e-05) * gain).astype(BF16)


CHUNKS = ((0, 192), (192, 576), (576, 1152))


def front_kernel(
    rows_ref, gain_ref, wb_ref, nq_ref, tile_ref, held_ref, gain_vm, wb_vm, sems
):
    copies = []
    for i, (begin, end) in enumerate(CHUNKS):
        part = pl.ds(begin, end - begin)
        copies.append(pltpu.make_async_copy(rows_ref.at[part], held_ref.at[part], sems.at[i]))
    gain_copy = pltpu.make_async_copy(gain_ref, gain_vm, sems.at[3])
    wb_copy = pltpu.make_async_copy(wb_ref, wb_vm, sems.at[4])
    copies[0].start()
    gain_copy.start()
    wb_copy.start()
    copies[1].start()
    copies[2].start()
    lane = lax.broadcasted_iota(jnp.int32, (KB, LANES), 1)
    place = jnp.where(lane < HEADS * KB, lax.rem(lane, KB), -1)
    gain_copy.wait()
    gain = gain_vm[...]
    wb_copy.wait()
    wb = wb_vm[...].astype(F32)
    spread_t = [jnp.broadcast_to(wb[h : h + 1, :], (KB, LANES)) for h in range(HEADS)]
    spread_t.append(jnp.zeros((LANES - HEADS * KB, LANES), F32))
    spread_t = jnp.concatenate(spread_t, axis=0).astype(BF16)
    total = jnp.zeros((KB, LANES), F32)
    for i, (begin, end) in enumerate(CHUNKS):
        copies[i].wait()
        normed = norm_rows(held_ref[begin:end, :], gain)
        if i == 0:
            nq_ref[...] = normed
        wide = nt_dot(normed, spread_t)
        for j in range(begin // KB, end // KB):
            row = j * KB - begin
            total = jnp.where(place == j % KB, wide[row : row + KB, :], total)
            if j % KB == KB - 1:
                tile_ref[j + 1 - KB : j + 1, :] = total


def copies_kernel(tile_ref, out_ref, sems):
    sends = []
    for r in range(NROW):
        send = pltpu.make_async_copy(tile_ref, out_ref.at[r], sems.at[r])
        send.start()
        sends.append(send)
    for send in sends:
        send.wait()


def relay_kernel(own_ref, first_ref, second_ref, third_ref, out_ref):
    for a in range(QROWS):
        span = slice(a * KB, (a + 1) * KB)
        refs = (own_ref, first_ref, second_ref, third_ref)
        parts = [ref[span, :].astype(F32) for ref in refs]
        out_ref[a * 96 : (a + 1) * 96, :] = jnp.concatenate(parts, axis=0).astype(BF16)


HALF_K = NROW * KB
GROUP = HEADS * KB


def join_kernel(third_ref, bias_ref, payload_ref, order_ref):
    rows = third_ref.shape[0]
    payload_ref[0:rows, :] = third_ref[...]
    col = lax.axis_index("col")
    core = lax.rem(col, 2)
    x = lax.rem(col // 2, 4)
    y_hi = col // 8
    place = 0
    rest = []
    for mask in MASKS:
        for y_mask in MASKS:
            slot = lax.bitwise_xor(y_hi, y_mask) * 4 + lax.bitwise_xor(x, mask)
            mine = pl.multiple_of((slot * 2 + core) * KB, 8)
            theirs = pl.multiple_of((slot * 2 + 1 - core) * KB, 8)
            order_ref[place : place + KB, :] = bias_ref[pl.ds(mine, KB), :]
            rest.append(bias_ref[pl.ds(theirs, KB), :])
            place += KB
    rest = jnp.concatenate(rest, axis=0)
    for term in range(3):
        part = rest.astype(BF16)
        rest = rest - part.astype(F32)
        begin = rows + term * HALF_K
        payload_ref[begin : begin + HALF_K, :] = part


def nt_dot(left, right):
    return lax.dot_general(left, right, (((1,), (1,)), ((), ())), preferred_element_type=F32)


def twice(block):
    zero = jnp.zeros_like(block)
    top = jnp.concatenate([block, zero], axis=1)
    return jnp.concatenate([top, jnp.concatenate([zero, block], axis=1)], axis=0)


def attend_kernel(
    own_ref, first_ref, second_ref, third_ref, theirs_a_ref, theirs_b_ref, order_ref,
    nq_ref, wq_ref, wkv_ref, wg_ref, wo_ref,
    out_ref, bias_ref, gate_ref, gated_ref,
):
    sources = (
        own_ref, first_ref, second_ref, third_ref,
        theirs_a_ref.at[0], theirs_a_ref.at[1], theirs_a_ref.at[2], theirs_b_ref,
    )
    terms = []
    for term in range(3):
        begin = third_ref.shape[0] + term * HALF_K
        terms.append(theirs_b_ref[begin : begin + HALF_K, :].astype(F32))
    theirs = (terms[0] + terms[1]) + terms[2]
    for part in range(HALF_K // LANES):
        span = slice(part * LANES, (part + 1) * LANES)
        bias_ref[:, span] = order_ref[span, :].T[:GROUP, :]
        bias_ref[:, HALF_K + part * LANES : HALF_K + (part + 1) * LANES] = theirs[span, :].T[
            :GROUP, :
        ]
    nq = nq_ref[...]
    query = jnp.dot(nq, wq_ref[...], preferred_element_type=F32) * (1.0 / 32**0.5)
    query = query.astype(BF16).astype(F32)
    gate_ref[...] = jax.nn.sigmoid(jnp.dot(nq, wg_ref[...], preferred_element_type=F32))
    wk = twice(wkv_ref[:, :LANES].astype(F32)).astype(BF16)
    wv = twice(wkv_ref[:, LANES:].astype(F32)).astype(BF16)
    lane = lax.broadcasted_iota(jnp.int32, (KB, LANES), 1)
    zero = jnp.zeros((GROUP, LANES), F32)
    for i in range(QROWS // 2):
        sides = []
        masked = []
        for a in (2 * i, 2 * i + 1):
            sides.append(
                jnp.concatenate([ref[a * 96 : (a + 1) * 96, :] for ref in sources], axis=0)
            )
            q = query[a * KB : (a + 1) * KB, :]
            parts = [jnp.where(lane // 32 == h, q, 0.0) for h in range(HEADS)]
            masked.append(jnp.concatenate(parts, axis=0))
        queries = jnp.concatenate(
            [
                jnp.concatenate([masked[0], zero], axis=1),
                jnp.concatenate([zero, masked[1]], axis=1),
            ],
            axis=0,
        ).astype(BF16)
        rows = jnp.concatenate(sides, axis=1)
        keys = jnp.dot(rows, wk, preferred_element_type=F32).astype(BF16)
        values = jnp.dot(rows, wv, preferred_element_type=F32).astype(BF16)
        score = nt_dot(queries, keys)
        for n in range(2):
            a = 2 * i + n
            full = score[n * GROUP : (n + 1) * GROUP, :] + bias_ref[...]
            top = jnp.max(full, axis=1, keepdims=True)
            weights = jnp.exp(full - top)
            total = jnp.sum(weights, axis=1, keepdims=True)
            high = weights.astype(BF16)
            low = (weights - high.astype(F32)).astype(BF16)
            both = jnp.dot(
                jnp.concatenate([high, low], axis=0),
                values[:, n * LANES : (n + 1) * LANES],
                preferred_element_type=F32,
            )
            attended = (both[:GROUP, :] + both[GROUP:, :]) * (1.0 / total)
            mine = jnp.zeros((KB, LANES), F32)
            for h in range(HEADS):
                mine = jnp.where(lane // 32 == h, attended[h * KB : (h + 1) * KB, :], mine)
            span = slice(a * KB, (a + 1) * KB)
            gated_ref[span, :] = gate_ref[span, :] * mine
    out_ref[...] = jnp.dot(
        gated_ref[...].astype(BF16), wo_ref[...], preferred_element_type=F32
    ).astype(BF16)


def permute_col(value, target):
    return lax.ppermute(value, "col", [(c, target(c)) for c in range(NCOL)])


def permute_all(value, target):
    pairs = []
    for r in range(NROW):
        for c in range(NCOL):
            r2, c2 = target(r, c)
            pairs.append((r * NCOL + c, r2 * NCOL + c2))
    return lax.ppermute(value, ("row", "col"), pairs)


def near_y(mask):
    return lambda c: c ^ (mask * 8)


def near_x(mask):
    return lambda c: c ^ (mask * 2)


def body(pair, ln_gain, w_query, w_keyval, w_gate, w_bias, w_out):
    shape = jax.ShapeDtypeStruct
    rows = pair.reshape(-1, LANES)
    nrows = QROWS * KB
    nq, tile = pl.pallas_call(
        front_kernel,
        in_specs=[whole(pl.ANY)] * 3,
        out_specs=[whole(), whole()],
        out_shape=[shape((nrows, LANES), BF16), shape((2 * KB, LANES), F32)],
        scratch_shapes=[
            VM(rows.shape, BF16),
            VM((1, LANES), F32),
            VM((HEADS, LANES), BF16),
            pltpu.SemaphoreType.DMA((5,)),
        ],
        name="front",
    )(rows, ln_gain.reshape(1, LANES), w_bias.T)
    ys = [nq] + [permute_col(nq, near_y(mask)) for mask in MASKS[1:]]
    tile = permute_all(tile, lambda r, c: (c // 2, 2 * r + c % 2))
    small = pltpu.CompilerParams(vmem_limit_bytes=16 * 1024 * 1024)
    tiles = pl.pallas_call(
        copies_kernel,
        in_specs=[whole()],
        out_specs=whole(pl.ANY),
        out_shape=shape((NROW, 2 * KB, LANES), F32),
        scratch_shapes=[pltpu.SemaphoreType.DMA((NROW,))],
        compiler_params=small,
        cost_estimate=pl.CostEstimate(flops=20 * 10**9, bytes_accessed=0, transcendentals=0),
        name="copies",
    )(tile)
    bias = lax.all_to_all(tiles, "row", 0, 0)
    piece = pl.pallas_call(
        relay_kernel,
        in_specs=[whole()] * 4,
        out_specs=whole(),
        out_shape=shape((4 * nrows, LANES), BF16),
        compiler_params=small,
        cost_estimate=pl.CostEstimate(flops=30 * 10**9, bytes_accessed=0, transcendentals=0),
        name="relay",
    )(*ys)
    first = permute_col(piece, near_x(1))
    second = permute_col(piece, near_x(3))
    third = permute_col(first, near_x(3))
    mine = [piece, first, second, third]
    last, order = pl.pallas_call(
        join_kernel,
        in_specs=[whole()] * 2,
        out_specs=[whole()] * 2,
        out_shape=[
            shape((4 * nrows + 3 * HALF_K, LANES), BF16),
            shape((HALF_K, LANES), F32),
        ],
        compiler_params=small,
        name="join",
    )(third, bias.reshape(-1, LANES))
    theirs = [permute_col(value, lambda c: c ^ 1) for value in (jnp.stack(mine[:3]), last)]
    out = pl.pallas_call(
        attend_kernel,
        in_specs=[whole()] * 12,
        out_specs=whole(),
        out_shape=shape((nrows, LANES), BF16),
        scratch_shapes=[
            VM((GROUP, N_RES), F32),
            VM((nrows, LANES), F32),
            VM((nrows, LANES), F32),
        ],
        compiler_params=pltpu.CompilerParams(vmem_limit_bytes=32 * 1024 * 1024),
        name="attend",
    )(*mine, *theirs, order, nq, w_query, w_keyval, w_gate, w_out)
    return out.reshape(QROWS, KB, LANES)


def solution(mesh):
    placed = (P("row", "col", None), P(), P(), P(), P(), P(), P())
    return jax.shard_map(
        body, mesh=mesh, in_specs=placed, out_specs=P("row", "col", None), check_vma=False
    )
```
